512 devices in a mesh: group: 16 (over x, z_lo), mp: 32 (over z_hi, y, core).
Axes of the slice: x: 4, y: 4, z: 16 (z_hi: 4, z_lo: 4; z = z_hi * 4 + z_lo), core: 2. Of those that a mesh axis runs over, the one named last changes fastest.
Arguments:
- inputs: bfloat16 [2, 12288, 8192], P(None, 'group', 'mp'), may hold values from -6 to 6
- targets: bfloat16 [2, 12288, 1024], P(None, ('group', 'mp')), may hold values from -6 to 6
- numerator: bfloat16 [16, 8192, 1024], P('group', 'mp'), may hold values from -6 to 6
- momentum: float32 [16, 8192, 1024], P('group', 'mp'), may hold values from -4 to 4
- received: bfloat16 [16, 8192, 1024], P('group', 'mp'), may hold values from -6 to 6
- push_weight: float32 [16], P('group'), may hold values from 0.5 to 2
- received_weight: float32 [16], P('group'), may hold values from 0.5 to 2
- mix_share: int32 [16, 2], P('group'), may hold values from 1 to 7
Outputs:
- final_numerator: bfloat16 [16, 8192, 1024], P('group', 'mp')
- final_weight: float32 [16], P('group')
- final_received: bfloat16 [16, 8192, 1024], P('group', 'mp')
- final_received_weight: float32 [16], P('group')
- value_rows: bfloat16 [2, 12288, 1024], P(None, ('group', 'mp'))
The draws below stay inside these ranges and needn't reach their ends.
All inputs are finite; a program needn't handle non-finite values.
Results may differ from the reference program's by a relative error of at most 0.02.
Values may be sent and summed in bfloat16 or wider, within the bound.
No kernel may reach another device: no remote copies, remote signals or barrier semaphores. Data moves between devices by JAX's collectives and lax.ppermute only.
A program may use at most 64 MiB of HBM per device.

```python
import math
import jax
import jax.numpy as jnp
from jax import lax

D = 8192
KV = 1024
TOK_GRP = 768
STEPS = 2
TOKENS = 12288
N_GROUP = 16
N_MP = 32


def place_ends(values, stream_key, smallest, high):
    spot = [jax.random.randint(jax.random.fold_in(stream_key, axis), (), 0, length) for axis, length in enumerate(values.shape)]
    widest = values.shape.index(max(values.shape))
    neighbour = spot[:widest] + [(spot[widest] + 1) % values.shape[widest]] + spot[widest + 1:]
    return values.at[tuple(spot)].set(smallest).at[tuple(neighbour)].set(high)


def block_levels(stream_key, dims, shards, low, high):
    loudness, own = 1.0, jax.random.fold_in(stream_key, 6)
    for dim, parts in shards:
        heights = jnp.exp(jax.random.uniform(jax.random.fold_in(own, dim), (parts,), jnp.float32, low / len(shards), high / len(shards)))
        loudness = loudness * jnp.repeat(heights, dims[dim] // parts).reshape([-1 if axis == dim else 1 for axis in range(len(dims))])
    return loudness


def centred(key, dims, scale, bound, split=(), held_as=jnp.bfloat16):
    gain = block_levels(key, dims, split, -0.22, 0.18) if split else 1.0
    values = jax.random.normal(key, dims, jnp.float32) * scale * gain
    return jnp.minimum(jnp.maximum(values, -bound), bound).astype(held_as)


def setup_inputs(seed: int = 0) -> dict:
    seeds = jax.random.split(jax.random.key(seed), 9)
    return {
        "inputs": centred(seeds[0], (STEPS, TOKENS, D), 1.0, 6.0, ((1, 16), (2, 32))),
        "targets": centred(seeds[1], (STEPS, TOKENS, KV), 1.0, 6.0, ((1, 512),)),
        "numerator": centred(seeds[2], (N_GROUP, D, KV), 1.0, 6.0, ((0, 16), (1, 32))),
        "momentum": centred(seeds[3], (N_GROUP, D, KV), 0.5, 4.0, ((0, 16), (1, 32)), jnp.float32),
        "received": centred(seeds[4], (N_GROUP, D, KV), 1.0, 6.0, ((0, 16), (1, 32))),
        "push_weight": jnp.clip(jnp.exp(math.log(2.0) - 1.3862944 * jax.random.uniform(seeds[5], (N_GROUP,), jnp.float32) ** block_levels(seeds[5], (N_GROUP,), ((0, 16),), -0.2, 0.2)), 0.5, 2.0),
        "received_weight": jnp.clip(jnp.exp(math.log(2.0) - 1.3862944 * jax.random.uniform(seeds[6], (N_GROUP,), jnp.float32) ** block_levels(seeds[6], (N_GROUP,), ((0, 16),), -0.2, 0.2)), 0.5, 2.0),
        "mix_share": place_ends(jax.random.randint(seeds[7], (N_GROUP, STEPS), 1, 8), jax.random.fold_in(seeds[7], 1), 1, 7).astype(jnp.int32),
    }


momentum_decay = 0.9
step_size = 0.5

def reference(inputs, targets, numerator, momentum, received, push_weight, received_weight, mix_share):
    block_width = D // N_MP
    row_scale = 1.0 / math.sqrt(D)
    grad_scale = 1.0 / math.sqrt(TOK_GRP)
    current = numerator
    velocity = momentum
    arrived = received
    arrived_weight = received_weight
    weights = push_weight
    value_steps = []
    for step_index in range(STEPS):
        hop_length = 2 ** step_index
        new_current, new_velocity, outgoing_all, outgoing_weights, new_weights, group_values = ([], [], [], [], [], [])
        for group_index in range(N_GROUP):
            group_weight = weights[group_index]
            scaled = (current[group_index].astype(jnp.float32) / group_weight).astype(jnp.bfloat16)
            group_tokens = inputs[step_index, group_index * TOK_GRP:(group_index + 1) * TOK_GRP]
            partials = jnp.einsum('tkd,kdo->kto', group_tokens.reshape(TOK_GRP, N_MP, block_width).astype(jnp.float32), scaled.reshape(N_MP, block_width, KV).astype(jnp.float32)) * row_scale
            partials = lax.optimization_barrier(partials.astype(jnp.bfloat16)).astype(jnp.float32)
            values = lax.optimization_barrier(jnp.sum(partials, axis=0)).astype(jnp.bfloat16)
            teacher = targets[step_index, group_index * TOK_GRP:(group_index + 1) * TOK_GRP]
            residual = (values.astype(jnp.float32) - teacher.astype(jnp.float32)).astype(jnp.bfloat16)
            gradient = jnp.dot(group_tokens.T, residual, preferred_element_type=jnp.float32) * grad_scale
            moved = momentum_decay * velocity[group_index] + gradient
            half_step = current[group_index].astype(jnp.float32) - step_size * moved
            kept_share = mix_share[group_index, step_index].astype(jnp.float32) / 8.0
            outgoing_all.append(((1.0 - kept_share) * half_step).astype(jnp.bfloat16))
            outgoing_weights.append(((1.0 - kept_share) * group_weight).astype(jnp.bfloat16).astype(jnp.float32))
            new_current.append((kept_share * half_step + arrived[group_index].astype(jnp.float32)).astype(jnp.bfloat16))
            new_weights.append(kept_share * group_weight + arrived_weight[group_index])
            new_velocity.append(moved)
            group_values.append(values)
        current = jnp.stack(new_current)
        velocity = jnp.stack(new_velocity)
        weights = jnp.stack(new_weights)
        arrived = jnp.roll(jnp.stack(outgoing_all), hop_length, axis=0)
        arrived_weight = jnp.roll(jnp.stack(outgoing_weights), hop_length, axis=0)
        value_steps.append(jnp.concatenate(group_values, axis=0))
    return (current, weights, arrived, arrived_weight, jnp.stack(value_steps))
```

```python
import math

import jax
import jax.numpy as jnp
import numpy as np
from jax import lax
from jax.sharding import PartitionSpec as P

D = 8192
TOK_GRP = 768
N_MP = 32
ROWS = TOK_GRP // N_MP

momentum_decay = 0.9
step_size = 0.5


def turns(core):
    return (1, 3) if core == 0 else (3, 1)


def partner(index, step):
    zh, y, core = index // 8, index // 2 % 4, index % 2
    if step == 0:
        core ^= 1
    elif step <= 2:
        y ^= turns(core)[step - 1]
    else:
        zh ^= turns(core)[step - 3]
    return zh * 8 + y * 2 + core


def block_order():
    table = np.zeros((N_MP, N_MP), np.int32)
    for index in range(N_MP):
        zh, y, core = index // 8, index // 2 % 4, index % 2
        for place in range(N_MP):
            bits = [place >> (4 - k) & 1 for k in range(5)]
            owner = core ^ bits[0]
            t0, t1 = turns(owner)
            dy = (bits[1] * t0) ^ (bits[2] * t1)
            dz = (bits[3] * t0) ^ (bits[4] * t1)
            table[index, place] = (zh ^ dz) * 8 + (y ^ dy) * 2 + owner
    return table


PAIRS = [[(i, partner(i, step)) for i in range(N_MP)] for step in range(5)]


def reduce_scatter(part):
    for step in range(5):
        half = part.shape[0] // 2
        got = lax.ppermute(part[half:], "mp", PAIRS[step])
        part = (part[:half].astype(jnp.float32) + got.astype(jnp.float32)).astype(jnp.bfloat16)
    return part


def all_gather(own):
    for step in (4, 3, 2, 1):
        own = jnp.concatenate([own, lax.ppermute(own, "mp", PAIRS[step])], axis=0)
    return own, lax.ppermute(own, "mp", PAIRS[0])


def local(inputs, targets, numerator, momentum, received, push_weight, received_weight, mix_share):
    row_scale = 1.0 / math.sqrt(D)
    grad_scale = 1.0 / math.sqrt(TOK_GRP)
    count = lax.axis_size("group")
    me = lax.axis_index("group")
    current = numerator[0]
    velocity = momentum[0]
    arrived = received[0]

    kept = mix_share[0].astype(jnp.float32) / 8.0
    weight0 = push_weight[0]
    weight1 = kept[0] * weight0 + received_weight[0]
    sent = jnp.stack([(1.0 - kept[0]) * weight0, (1.0 - kept[1]) * weight1]).astype(jnp.bfloat16)
    all_sent = lax.all_gather(sent, "group", axis=0).astype(jnp.float32)
    arrived0 = lax.dynamic_index_in_dim(all_sent, lax.rem(me + count - 1, count), 0, False)[0]
    arrived1 = lax.dynamic_index_in_dim(all_sent, lax.rem(me + count - 2, count), 0, False)[1]
    weight2 = kept[1] * weight1 + arrived0
    weights = (weight0, weight1)

    order = jnp.asarray(block_order())[lax.axis_index("mp")]
    place = lax.broadcasted_iota(jnp.int32, (N_MP, ROWS, TOK_GRP), 2)
    want = order[:, None, None] * ROWS + lax.broadcasted_iota(jnp.int32, (N_MP, ROWS, TOK_GRP), 1)
    pick = (place == want).astype(jnp.bfloat16).reshape(TOK_GRP, TOK_GRP)

    value_steps = []
    for step in range(2):
        tokens = jnp.dot(pick, inputs[step], preferred_element_type=jnp.float32).astype(jnp.bfloat16)
        scaled = (current.astype(jnp.float32) / weights[step]).astype(jnp.bfloat16)
        product = jnp.dot(tokens, scaled, preferred_element_type=jnp.float32) * row_scale
        values = reduce_scatter(product.astype(jnp.bfloat16))
        residual = (
            values.astype(jnp.float32) - targets[step].astype(jnp.float32)
        ).astype(jnp.bfloat16)
        near, far = all_gather(residual)
        half = near.shape[0]
        dims = (((0,), (0,)), ((), ()))
        gradient = (
            lax.dot_general(tokens[:half], near, dims, preferred_element_type=jnp.float32)
            + lax.dot_general(tokens[half:], far, dims, preferred_element_type=jnp.float32)
        ) * grad_scale
        velocity = momentum_decay * velocity + gradient
        half_step = current.astype(jnp.float32) - step_size * velocity
        outgoing = ((1.0 - kept[step]) * half_step).astype(jnp.bfloat16)
        current = (kept[step] * half_step + arrived.astype(jnp.float32)).astype(jnp.bfloat16)
        hop = 2**step
        arrived = lax.ppermute(outgoing, "group", [(i, (i + hop) % count) for i in range(count)])
        value_steps.append(values)
    return (
        current[None],
        weight2[None],
        arrived[None],
        arrived1[None],
        jnp.stack(value_steps),
    )


def solution(mesh):
    placed = (
        P(None, "group", "mp"),
        P(None, ("group", "mp"), None),
        P("group", "mp", None),
        P("group", "mp", None),
        P("group", "mp", None),
        P("group"),
        P("group"),
        P("group", None),
    )
    return jax.shard_map(
        local,
        mesh=mesh,
        in_specs=placed,
        out_specs=(
            P("group", "mp", None),
            P("group"),
            P("group", "mp", None),
            P("group"),
            P(None, ("group", "mp"), None),
        ),
        check_vma=False,
    )
```

```python
import math

import jax
import jax.numpy as jnp
from jax import lax
from jax.sharding import Mesh
from jax.sharding import PartitionSpec as P

GROUP = ("x", "z_lo")
MP = ("z_hi", "y", "core")
SIZES = (4, 4, 4, 4, 2)

momentum_decay = 0.9
step_size = 0.5


def f32(value):
    return value.astype(jnp.float32)


def bf16(value):
    return value.astype(jnp.bfloat16)


def pick(first, when_true, when_false):
    return jnp.where(first, when_true, when_false)


def z_pairs(step):
    pairs = []
    for zh in range(SIZES[2]):
        for core in range(2):
            turn = (1, 3)[step ^ core]
            pairs.append((zh * 2 + core, (zh ^ turn) * 2 + core))
    return pairs


def reduce_y(part):
    count = SIZES[3]
    rows = part.shape[0] // count
    got = lax.all_to_all(part, "y", 0, 0, tiled=True).reshape(count, rows, part.shape[1])
    return bf16(jnp.sum(f32(got), axis=0))


def reduce_z(part):
    for step in range(2):
        part = bf16(f32(part) + f32(lax.ppermute(part, ("z_hi", "core"), z_pairs(step))))
    return part


def swap_core(value):
    return lax.ppermute(value, "core", [(0, 1), (1, 0)])


def to_group(value, hop):
    count = SIZES[0] * SIZES[1]
    return lax.ppermute(value, GROUP, [(i, (i + hop) % count) for i in range(count)])


def dot(a, b, dims):
    return lax.dot_general(a, b, (dims, ((), ())), preferred_element_type=jnp.float32)


def local(inputs, targets, numerator, momentum, received, push_weight, received_weight, mix_share):
    tokens_count, width = inputs.shape[1:]
    value_count = numerator.shape[2]
    row_scale = 1.0 / math.sqrt(width * SIZES[2] * SIZES[3] * SIZES[4])
    grad_scale = 1.0 / math.sqrt(tokens_count)
    core = lax.axis_index("core")
    first = core == 0
    cols = value_count // 2
    own_rows = targets.shape[1]

    def own_half(value):
        return pick(first, value[..., :cols], value[..., cols:])

    def other_half(value):
        return pick(first, value[..., cols:], value[..., :cols])

    kept = f32(mix_share[0]) / 8.0
    weight0 = push_weight[0]
    weight1 = kept[0] * weight0 + received_weight[0]
    arrived0 = f32(to_group(bf16((1.0 - kept[0]) * weight0)[None], 1))
    arrived1 = f32(to_group(bf16((1.0 - kept[1]) * weight1)[None], 2))
    weight2 = kept[1] * weight1 + arrived0

    slab = inputs.reshape(2, SIZES[2], SIZES[3], 2 * own_rows, width)
    tokens = slab.transpose(0, 2, 1, 3, 4).reshape(2, tokens_count, width)

    split = cols // 2
    away = other_half(numerator[0])
    got = swap_core(jnp.concatenate([tokens[0], away[:, :split], away[:, split:]], axis=0))
    tokens1 = jnp.concatenate([tokens[0], got[:tokens_count]], axis=1)
    far = got[tokens_count:]
    start = jnp.concatenate(
        [own_half(numerator[0]), jnp.concatenate([far[:width], far[width:]], axis=1)], axis=0
    )
    scaled = bf16(f32(start) / weight0)
    part1 = bf16(dot(tokens1, scaled, ((1,), (0,))) * row_scale)
    values1 = reduce_z(reduce_y(part1))

    away = other_half(received[0])
    got = swap_core(jnp.concatenate([tokens[1], away[:, :split], away[:, split:]], axis=0))
    tokens2 = jnp.concatenate([tokens[1], got[:tokens_count]], axis=1)
    far = got[tokens_count:]
    arrived = jnp.concatenate(
        [own_half(received[0]), jnp.concatenate([far[:width], far[width:]], axis=1)], axis=0
    )
    velocity = jnp.concatenate(
        [own_half(momentum[0]), swap_core(other_half(momentum[0]))], axis=0
    )

    ahead = f32(start) - (step_size * momentum_decay) * velocity
    base = kept[0] * ahead + f32(arrived)
    part2 = bf16(dot(tokens2, bf16(base / weight1), ((1,), (0,))) * row_scale)
    gram_cols = tokens_count // 2
    mine = lax.dynamic_slice_in_dim(tokens1, core * gram_cols, gram_cols, 0)
    gram_part = bf16(dot(tokens2, mine, ((1,), (1,))))
    second = reduce_z(reduce_y(jnp.concatenate([part2, gram_part], axis=1)))
    values2, gram = second[:, :cols], second[:, cols:]
    gram_far = swap_core(gram)

    taught = lax.all_gather(targets, ("z_hi", "core"), axis=1)
    taught = own_half(taught.reshape(2, -1, value_count))

    residual1 = bf16(f32(values1) - f32(taught[0]))
    all1 = lax.all_gather(residual1, "y", axis=0, tiled=True)
    rows_mine = lax.dynamic_slice_in_dim(all1, core * gram_cols, gram_cols, 0)
    rows_far = lax.dynamic_slice_in_dim(all1, (1 - core) * gram_cols, gram_cols, 0)
    turned = dot(gram, rows_mine, ((1,), (0,))) + dot(gram_far, rows_far, ((1,), (0,)))
    values2 = bf16(
        f32(values2) - (step_size * grad_scale * row_scale * kept[0] / weight1) * turned
    )
    residual2 = bf16(f32(values2) - f32(taught[1]))
    all2 = lax.all_gather(residual2, "y", axis=0, tiled=True)

    gradient1 = dot(tokens1, all1, ((0,), (0,))) * grad_scale
    current = bf16(base - (step_size * kept[0]) * gradient1)
    outgoing = bf16((1.0 - kept[0]) * (ahead - step_size * gradient1))
    arrived = to_group(outgoing, 1)
    velocity = momentum_decay * velocity + gradient1

    gradient2 = dot(tokens2, all2, ((0,), (0,))) * grad_scale
    half_step = f32(current) - step_size * (momentum_decay * velocity + gradient2)
    outgoing = bf16((1.0 - kept[1]) * half_step)
    current = bf16(kept[1] * half_step + f32(arrived))

    count = SIZES[0] * SIZES[1]
    hop = [((i * 2 + c), ((i + 2) % count) * 2 + (1 - c)) for i in range(count) for c in range(2)]
    sent_far = lax.ppermute(outgoing[width:], GROUP + ("core",), hop)
    sent_own = to_group(outgoing[:width], 2)

    both = jnp.stack([values1, values2])
    at = lax.axis_index("z_hi") * (2 * own_rows)
    mine = lax.dynamic_slice_in_dim(both, at + core * own_rows, own_rows, 1)
    theirs = lax.dynamic_slice_in_dim(both, at + (1 - core) * own_rows, own_rows, 1)
    got = swap_core(jnp.concatenate([current[width:], theirs.reshape(2 * own_rows, cols)], axis=0))

    def whole(near, far):
        return jnp.concatenate([pick(first, near, far), pick(first, far, near)], axis=-1)

    return (
        whole(current[:width], got[:width])[None],
        weight2,
        whole(sent_own, sent_far)[None],
        arrived1,
        whole(mine, got[width:].reshape(2, own_rows, cols)),
    )


def solution(mesh):
    fine = Mesh(mesh.devices.reshape(SIZES), GROUP + MP)
    placed = (
        P(None, GROUP, MP),
        P(None, GROUP + MP, None),
        P(GROUP, MP, None),
        P(GROUP, MP, None),
        P(GROUP, MP, None),
        P(GROUP),
        P(GROUP),
        P(GROUP, None),
    )
    return jax.shard_map(
        local,
        mesh=fine,
        in_specs=placed,
        out_specs=(
            P(GROUP, MP, None),
            P(GROUP),
            P(GROUP, MP, None),
            P(GROUP),
            P(None, GROUP + MP, None),
        ),
        check_vma=False,
    )
```

```python
import functools
import math

import jax
import jax.numpy as jnp
from jax import lax
from jax.experimental import pallas as pl
from jax.experimental.pallas import tpu as pltpu
from jax.sharding import Mesh
from jax.sharding import PartitionSpec as P

GROUP = ("x", "z_lo")
MP = ("z_hi", "y", "core")
SIZES = (4, 4, 4, 4, 2)
N_Z, N_Y = SIZES[2], SIZES[3]

momentum_decay = 0.9
step_size = 0.5

ROWS = 24
BLOCK = 2 * ROWS
SLAB = N_Z * BLOCK
TOKENS = N_Y * SLAB
WIDTH = 256
VALUES = 1024
COLS = VALUES // 2
HALF = TOKENS // 2
PADDED = 32
ROW_SCALE = 1.0 / math.sqrt(WIDTH * N_Z * N_Y * 2)
GRAD_SCALE = 1.0 / math.sqrt(TOKENS)

X2_AT = TOKENS
W_AT = 2 * TOKENS
REC_AT = W_AT + 2 * WIDTH
T_AT = REC_AT + 2 * WIDTH
MESSAGE = T_AT + 4 * PADDED


def f32(value):
    return value.astype(jnp.float32)


def bf16(value):
    return value.astype(jnp.bfloat16)


def dot(a, b, dims=((1,), (0,))):
    return lax.dot_general(a, b, (dims, ((), ())), preferred_element_type=jnp.float32)


def cols_of(core):
    return pl.ds(pl.multiple_of(core * COLS, COLS), COLS)


def block_of(index):
    return pl.ds(pl.multiple_of(index * BLOCK, 16), BLOCK)


def by_y():
    return [((zh * N_Y + y) * BLOCK, (y * N_Z + zh) * BLOCK) for zh in range(N_Z) for y in range(N_Y)]


def first_values(ids, facts, x, w, far, own):
    core = ids[0]
    for out, side in ((far, 1 - core), (own, core)):
        scaled = bf16(f32(w[0, :, cols_of(side)]) / facts[0])
        part = bf16(dot(x[0], scaled) * ROW_SCALE)
        for at, to in by_y():
            out[to : to + BLOCK] = part[at : at + BLOCK]


def make_message(ids, x, w, rec, targets, velocity, message, velocity_far):
    far = 1 - ids[0]
    for step in range(2):
        for at, to in by_y():
            message[step * TOKENS + to : step * TOKENS + to + BLOCK] = x[step, at : at + BLOCK]
    for ref, row in ((w, W_AT), (rec, REC_AT)):
        half = ref[0, :, cols_of(far)]
        message[row : row + WIDTH] = half[:, :WIDTH]
        message[row + WIDTH : row + 2 * WIDTH] = half[:, WIDTH:]
    for step in range(2):
        half = targets[step, :, cols_of(far)]
        row = T_AT + 2 * step * PADDED
        message[row : row + PADDED] = half[:, :WIDTH]
        message[row + PADDED : row + 2 * PADDED] = half[:, WIDTH:]
    velocity_far[...] = velocity[0, :, cols_of(far)]


def second_values(ids, facts, mine, got, w, rec, velocity, velocity_got, out, ahead, base):
    core = ids[0]
    keep, weight = facts[2], facts[1]
    side = cols_of(core)
    decayed = step_size * momentum_decay
    ahead[:WIDTH] = f32(w[0, :, side]) - decayed * velocity[0, :, side]
    base[:WIDTH] = keep * ahead[:WIDTH] + f32(rec[0, :, side])
    for k in range(2):
        part = slice(k * WIDTH, (k + 1) * WIDTH)
        ahead[WIDTH:, part] = (
            f32(got[W_AT + k * WIDTH : W_AT + (k + 1) * WIDTH]) - decayed * velocity_got[:, part]
        )
        base[WIDTH:, part] = keep * ahead[WIDTH:, part] + f32(
            got[REC_AT + k * WIDTH : REC_AT + (k + 1) * WIDTH]
        )
    scaled = bf16(base[...] / weight)
    near, far = mine[X2_AT : X2_AT + TOKENS], got[X2_AT : X2_AT + TOKENS]
    out[:, :COLS] = bf16((dot(near, scaled[:WIDTH]) + dot(far, scaled[WIDTH:])) * ROW_SCALE)
    rows = pl.ds(pl.multiple_of(core * HALF, 16), HALF)
    across = ((1,), (1,))
    out[:, COLS:] = bf16(dot(near, mine[rows], across) + dot(far, got[rows], across))


def sum_and_split(ids, parts, keep, send):
    for out, first in ((keep, 1), (send, 3)):
        for k in range(2):
            rows = block_of(ids[first + k])
            total = f32(parts[0, rows])
            for y in range(1, N_Y):
                total = total + f32(parts[y, rows])
            out[k * BLOCK : (k + 1) * BLOCK] = bf16(total)


def spread(ids, mine, got, out):
    for ref, first in ((mine, 1), (got, 3)):
        for k in range(2):
            rows = block_of(ids[first + k])
            for y in range(N_Y):
                out[y, rows] = ref[k * BLOCK : (k + 1) * BLOCK]


def merge_gram(ids, mine, got, gram):
    for ref, first in ((mine, 1), (got, 3)):
        for k in range(2):
            gram[block_of(ids[first + k])] = ref[k * BLOCK : (k + 1) * BLOCK, COLS:]


def second_residual(ids, facts, gram, gram_got, all1, mine, got, values, out, own_values, turned):
    core = ids[0]
    near = all1[pl.ds(pl.multiple_of(core * HALF, 16), HALF)]
    far = all1[pl.ds(pl.multiple_of((1 - core) * HALF, 16), HALF)]
    turned[...] = (dot(gram[...], near) + dot(gram_got[...], far)) * facts[4]
    for ref, first in ((mine, 1), (got, 3)):
        for k in range(2):
            rows = block_of(ids[first + k])
            block = bf16(f32(ref[k * BLOCK : (k + 1) * BLOCK, :COLS]) - turned[rows])
            for y in range(N_Y):
                out[y, rows] = block
    own_values[...] = bf16(f32(values[block_of(ids[6])]) - turned[block_of(ids[5])])


def first_gradient(ids, facts, mine, got, all1, ahead, base, velocity, velocity_got, out, ready):
    side = cols_of(ids[0])
    keep = facts[2]
    down = ((0,), (0,))
    for k, x, old in ((0, mine, velocity[0, :, side]), (1, got, velocity_got[...])):
        rows = slice(k * WIDTH, (k + 1) * WIDTH)
        gradient = dot(x[:TOKENS], all1[...], down) * GRAD_SCALE
        out[rows] = bf16((1.0 - keep) * (ahead[rows] - step_size * gradient))
        current = bf16(base[rows] - (step_size * keep) * gradient)
        moved = momentum_decay * old + gradient
        ready[rows] = f32(current) - (step_size * momentum_decay) * moved


def second_gradient(facts, mine, got, all2, ready, near, far, half):
    keep = facts[3]
    down = ((0,), (0,))
    for k, x, out in ((1, got, far), (0, mine, near)):
        rows = slice(k * WIDTH, (k + 1) * WIDTH)
        gradient = dot(x[X2_AT : X2_AT + TOKENS], all2[...], down) * GRAD_SCALE
        moved = ready[rows] - step_size * gradient
        out[...] = bf16((1.0 - keep) * moved)
        half[rows] = keep * moved


def add_arrived(half, arrived, near, far):
    near[...] = bf16(half[:WIDTH] + f32(arrived[:WIDTH]))
    far[...] = bf16(half[WIDTH:] + f32(arrived[WIDTH:]))


def join(ids, near, far, out):
    core = ids[0]
    out[0, :, cols_of(core)] = near[...]
    out[0, :, cols_of(1 - core)] = far[...]


SMEM = pl.BlockSpec(memory_space=pltpu.SMEM)
VMEM = pl.BlockSpec(memory_space=pltpu.VMEM)


def call(body, scalars, arrays, outs, scratch=(), flops=0):
    result = [jax.ShapeDtypeStruct(shape, kind) for shape, kind in outs]
    moved = sum(a.size * a.dtype.itemsize for a in list(arrays) + result)
    got = pl.pallas_call(
        body,
        out_shape=result,
        in_specs=[SMEM] * len(scalars) + [VMEM] * len(arrays),
        out_specs=[VMEM] * len(outs),
        scratch_shapes=[pltpu.VMEM(shape, kind) for shape, kind in scratch],
        compiler_params=pltpu.CompilerParams(vmem_limit_bytes=28 * 2**20),
        cost_estimate=pl.CostEstimate(flops=flops, bytes_accessed=moved, transcendentals=0),
        name=body.__name__,
    )(*scalars, *arrays)
    return got


B16, F32 = jnp.bfloat16, jnp.float32


def z_pairs(step):
    pairs = []
    for zh in range(N_Z):
        for core in range(2):
            turn = (1, 3)[step ^ core]
            pairs.append((zh * 2 + core, (zh ^ turn) * 2 + core))
    return pairs


def over_z(value, step):
    return lax.ppermute(value, ("z_hi", "core"), z_pairs(step))


def over_y(value):
    return lax.all_to_all(value, "y", 0, 0, tiled=True)


def swap_core(value):
    return lax.ppermute(value, "core", [(0, 1), (1, 0)])


def to_group(value, hop):
    count = SIZES[0] * SIZES[1]
    return lax.ppermute(value, GROUP, [(i, (i + hop) % count) for i in range(count)])


def reduce_slab(ids, part):
    columns = part.shape[1]
    got = over_y(part.reshape(N_Y, SLAB, columns))
    keep, send = call(
        sum_and_split, [ids], [got], [((2 * BLOCK, columns), B16), ((2 * BLOCK, columns), B16)]
    )
    mine = bf16(f32(keep) + f32(over_z(send, 0)))
    return f32(mine) + f32(over_z(mine, 1))


def local(inputs, targets, numerator, momentum, received, push_weight, received_weight, mix_share):
    core = lax.axis_index("core")
    zh = lax.axis_index("z_hi")
    first = core == 0
    pick = functools.partial(jnp.where, first)

    kept = f32(mix_share[0]) / 8.0
    weight0 = push_weight[0]
    weight1 = kept[0] * weight0 + received_weight[0]
    arrived0 = f32(to_group(bf16((1.0 - kept[0]) * weight0)[None], 1))
    arrived1 = f32(to_group(bf16((1.0 - kept[1]) * weight1)[None], 2))
    weight2 = kept[1] * weight1 + arrived0

    step0 = jnp.where(first, 1, 3)
    step1 = jnp.where(first, 3, 1)
    meet, away = zh ^ step1, zh ^ step0
    across = away ^ step1
    low, high = jnp.minimum(zh, meet), jnp.maximum(zh, meet)
    ids = jnp.stack(
        [core, low, high, jnp.minimum(away, across), jnp.maximum(away, across), zh, (zh == high) * 1, core]
    ).astype(jnp.int32)
    back = step_size * GRAD_SCALE * ROW_SCALE * kept[0] / weight1
    facts = jnp.stack([weight0, weight1, kept[0], kept[1], back, back, back, back])

    part = [((TOKENS, COLS), B16)] * 2
    part_far, part_own = call(first_values, [ids, facts], [inputs, numerator], part)
    part_got = swap_core(part_far)
    part1 = bf16(f32(part_own) + f32(part_got))

    padded = jnp.pad(targets, ((0, 0), (0, PADDED - ROWS), (0, 0)))
    padded, part_far = lax.optimization_barrier((padded, part_far))
    mine, velocity_far = call(
        make_message,
        [ids],
        [inputs, numerator, received, padded, momentum],
        [((MESSAGE, WIDTH), B16), ((WIDTH, COLS), F32)],
    )
    got = swap_core(mine)
    velocity_got = swap_core(velocity_far)

    near_rows = pick(targets[..., :COLS], targets[..., COLS:])
    far_rows = got[T_AT:].reshape(2, 2, PADDED, WIDTH)[:, :, :ROWS].transpose(0, 2, 1, 3)
    far_rows = far_rows.reshape(2, ROWS, COLS)
    chip = jnp.concatenate([pick(near_rows, far_rows), pick(far_rows, near_rows)], axis=1)
    chip_met = over_z(chip, 1)
    is_low = zh == low
    taught = jnp.concatenate(
        [jnp.where(is_low, chip, chip_met), jnp.where(is_low, chip_met, chip)], axis=1
    )

    part2, ahead, base = call(
        second_values,
        [ids, facts],
        [mine, got, numerator, received, momentum, velocity_got],
        [((TOKENS, COLS + HALF), B16), ((2 * WIDTH, COLS), F32), ((2 * WIDTH, COLS), F32)],
    )

    values1 = bf16(reduce_slab(ids, part1))
    residual1 = bf16(f32(values1) - f32(taught[0]))
    slab = [((N_Y, SLAB, COLS), B16)]
    (sent,) = call(spread, [ids], [residual1, over_z(residual1, 0)], slab)
    all1 = over_y(sent).reshape(TOKENS, COLS)

    second = reduce_slab(ids, part2)
    values2 = second[:, :COLS]
    second = jnp.concatenate([values2 - f32(taught[1]), second[:, COLS:]], axis=1)
    second = bf16(second)
    second_got = over_z(second, 0)
    (gram,) = call(merge_gram, [ids], [second, second_got], [((SLAB, HALF), B16)])
    gram_got = swap_core(gram)

    outgoing, ready = call(
        first_gradient,
        [ids, facts],
        [mine, got, all1, ahead, base, momentum, velocity_got],
        [((2 * WIDTH, COLS), B16), ((2 * WIDTH, COLS), F32)],
    )
    arrived = to_group(outgoing, 1)

    sent, own2 = call(
        second_residual,
        [ids, facts],
        [gram, gram_got, all1, second, second_got, values2],
        slab + [((BLOCK, COLS), B16)],
        [((SLAB, COLS), F32)],
    )
    all2 = over_y(sent).reshape(TOKENS, COLS)

    near, far, half = call(
        second_gradient,
        [facts],
        [mine, got, all2, ready],
        [((WIDTH, COLS), B16), ((WIDTH, COLS), B16), ((2 * WIDTH, COLS), F32)],
    )

    count = SIZES[0] * SIZES[1]
    hop = [(i * 2 + c, (i + 2) % count * 2 + 1 - c) for i in range(count) for c in range(2)]
    sent_far = lax.ppermute(far, GROUP + ("core",), hop)
    sent_own = to_group(near, 2)

    current, current_far = call(add_arrived, [], [half, arrived], [((WIDTH, COLS), B16)] * 2)
    own1 = lax.dynamic_slice_in_dim(values1, (zh == high) * BLOCK, BLOCK, 0)
    both = jnp.stack([own1, own2]).reshape(2, 2, ROWS, COLS)
    values_near = pick(both[:, 0], both[:, 1])
    values_far = pick(both[:, 1], both[:, 0])
    values_got = swap_core(values_far)
    current_got = swap_core(current_far)
    whole = [((1, WIDTH, VALUES), B16)]
    (final_numerator,) = call(join, [ids], [current, current_got], whole)
    (final_received,) = call(join, [ids], [sent_own, sent_far], whole)
    value_rows = jnp.concatenate(
        [pick(values_near, values_got), pick(values_got, values_near)], axis=-1
    )
    return final_numerator, weight2, final_received, arrived1, value_rows


def solution(mesh):
    fine = Mesh(mesh.devices.reshape(SIZES), GROUP + MP)
    placed = (
        P(None, GROUP, MP),
        P(None, GROUP + MP, None),
        P(GROUP, MP, None),
        P(GROUP, MP, None),
        P(GROUP, MP, None),
        P(GROUP),
        P(GROUP),
        P(GROUP, None),
    )
    return jax.shard_map(
        local,
        mesh=fine,
        in_specs=placed,
        out_specs=(
            P(GROUP, MP, None),
            P(GROUP),
            P(GROUP, MP, None),
            P(GROUP),
            P(None, GROUP + MP, None),
        ),
        check_vma=False,
    )
```

```python
import functools
import math

import jax
import jax.numpy as jnp
from jax import lax
from jax.experimental import pallas as pl
from jax.experimental.pallas import tpu as pltpu
from jax.sharding import Mesh
from jax.sharding import PartitionSpec as P

GROUP = ("x", "z_lo")
MP = ("z_hi", "y", "core")
SIZES = (4, 4, 4, 4, 2)
N_Z, N_Y = SIZES[2], SIZES[3]

momentum_decay = 0.9
step_size = 0.5

ROWS = 24
BLOCK = 2 * ROWS
SLAB = N_Z * BLOCK
TOKENS = N_Y * SLAB
WIDTH = 256
VALUES = 1024
COLS = VALUES // 2
HALF = TOKENS // 2
PADDED = 32
EXTRA = 16
ROW_SCALE = 1.0 / math.sqrt(WIDTH * N_Z * N_Y * 2)
GRAD_SCALE = 1.0 / math.sqrt(TOKENS)

X2_AT = TOKENS
W_AT = 2 * TOKENS
REC_AT = W_AT + 2 * WIDTH
T_AT = REC_AT + 2 * WIDTH
MESSAGE = T_AT + 4 * PADDED

B16, F32 = jnp.bfloat16, jnp.float32


def f32(value):
    return value.astype(jnp.float32)


def bf16(value):
    return value.astype(jnp.bfloat16)


def dot(a, b, dims=((1,), (0,))):
    return lax.dot_general(a, b, (dims, ((), ())), preferred_element_type=jnp.float32)


def cols_of(core):
    return pl.ds(pl.multiple_of(core * COLS, COLS), COLS)


def half_of(core):
    return pl.ds(pl.multiple_of(core * HALF, 16), HALF)


def own_block():
    return pl.ds(pl.multiple_of(lax.axis_index("z_hi") * BLOCK, 16), BLOCK)


def kept(mix, step):
    return mix[0, step].astype(jnp.float32) * 0.125


def by_y():
    return [((zh * N_Y + y) * BLOCK, (y * N_Z + zh) * BLOCK) for zh in range(N_Z) for y in range(N_Y)]


def first_values(push, x, w, far, own):
    core = lax.axis_index("core")
    for out, side in ((far, 1 - core), (own, core)):
        scaled = bf16(f32(w[:, cols_of(side)]) / push[0])
        part = bf16(dot(x[...], scaled) * ROW_SCALE)
        for at, to in by_y():
            out[to : to + BLOCK] = part[at : at + BLOCK]


def make_message(x, w, rec, targets, velocity, message, velocity_far):
    far = 1 - lax.axis_index("core")
    for step in range(2):
        for at, to in by_y():
            message[step * TOKENS + to : step * TOKENS + to + BLOCK] = x[step, at : at + BLOCK]
    for ref, row in ((w, W_AT), (rec, REC_AT)):
        half = ref[:, cols_of(far)]
        message[row : row + WIDTH] = half[:, :WIDTH]
        message[row + WIDTH : row + 2 * WIDTH] = half[:, WIDTH:]
    spare = jnp.zeros((PADDED - ROWS, COLS), jnp.float32)
    for step in range(2):
        half = bf16(jnp.concatenate([f32(targets[step, :, cols_of(far)]), spare], axis=0))
        row = T_AT + 2 * step * PADDED
        message[row : row + PADDED] = half[:, :WIDTH]
        message[row + PADDED : row + 2 * PADDED] = half[:, WIDTH:]
    velocity_far[...] = velocity[:, cols_of(far)]


def second_values(
    push, push_got, mix, w, rec, velocity, targets, mine, got, velocity_got, out, ahead, base, taught
):
    core = lax.axis_index("core")
    keep = kept(mix, 0)
    weight = keep * push[0] + push_got[0]
    side = cols_of(core)
    decayed = step_size * momentum_decay
    ahead[:WIDTH] = f32(w[:, side]) - decayed * velocity[:, side]
    base[:WIDTH] = keep * ahead[:WIDTH] + f32(rec[:, side])
    for k in range(2):
        part = slice(k * WIDTH, (k + 1) * WIDTH)
        ahead[WIDTH:, part] = (
            f32(got[W_AT + k * WIDTH : W_AT + (k + 1) * WIDTH]) - decayed * velocity_got[:, part]
        )
        base[WIDTH:, part] = keep * ahead[WIDTH:, part] + f32(
            got[REC_AT + k * WIDTH : REC_AT + (k + 1) * WIDTH]
        )
    scaled = bf16(base[...] / weight)
    near, far = mine[X2_AT : X2_AT + TOKENS], got[X2_AT : X2_AT + TOKENS]
    out[:, :COLS] = bf16((dot(near, scaled[:WIDTH]) + dot(far, scaled[WIDTH:])) * ROW_SCALE)
    rows = half_of(core)
    across = ((1,), (1,))
    out[:, COLS:] = bf16(dot(near, mine[rows], across) + dot(far, got[rows], across))
    for step in range(2):
        own = f32(targets[step, :, side])
        row = T_AT + 2 * step * PADDED
        other = jnp.concatenate(
            [f32(got[row : row + PADDED]), f32(got[row + PADDED : row + 2 * PADDED])], axis=1
        )[:ROWS]
        taught[step, :ROWS] = jnp.where(core == 0, own, other)
        taught[step, ROWS:] = jnp.where(core == 0, other, own)


def sum_over_y(step, parts, taught, slab, own):
    total = f32(parts[0])
    for y in range(1, N_Y):
        total = total + f32(parts[y])
    slab[...] = bf16(total)
    rows = own_block()
    total = f32(parts[0, rows, :COLS])
    for y in range(1, N_Y):
        total = total + f32(parts[y, rows, :COLS])
    own[...] = total
    slab[rows, :COLS] = bf16(total - taught[step])


def add_slab(mine, got, own, out, own_out):
    out[...] = bf16(f32(mine[...]) + f32(got[...]))
    own_out[...] = own[...] + f32(got[own_block(), :COLS])


def add_and_spread(mine, got, own, out, own_out):
    total = bf16(f32(mine[...]) + f32(got[...]))
    for y in range(N_Y):
        out[y] = total
    own_out[...] = own[...] + f32(got[own_block()])


def add_and_part(mine, got, own, out, gram, own_out):
    out[...] = bf16(f32(mine[:, :COLS]) + f32(got[:, :COLS]))
    gram[...] = bf16(f32(mine[:, COLS:]) + f32(got[:, COLS:]))
    own_out[...] = own[...] + f32(got[own_block(), :COLS])


def second_residual(push, push_got, mix, all1, gram, gram_got, base, own, out, own_out, turned):
    core = lax.axis_index("core")
    keep = kept(mix, 0)
    back = step_size * GRAD_SCALE * ROW_SCALE * keep / (keep * push[0] + push_got[0])
    near, far = all1[half_of(core)], all1[half_of(1 - core)]
    turned[...] = (dot(gram[...], near) + dot(gram_got[...], far)) * back
    residual = bf16(f32(base[...]) - turned[...])
    for y in range(N_Y):
        out[y] = residual
    own_out[...] = own[...] - turned[own_block()]


def first_gradient(push, mix, all1, mine, got, ahead, base, velocity, velocity_got, out, ready):
    side = cols_of(lax.axis_index("core"))
    keep = kept(mix, 0)
    down = ((0,), (0,))
    for k, x, old in ((0, mine, velocity[:, side]), (1, got, velocity_got[...])):
        rows = slice(k * WIDTH, (k + 1) * WIDTH)
        gradient = dot(x[:TOKENS], all1[...], down) * GRAD_SCALE
        out[rows] = bf16((1.0 - keep) * (ahead[rows] - step_size * gradient))
        current = bf16(base[rows] - (step_size * keep) * gradient)
        moved = momentum_decay * old + gradient
        ready[rows] = f32(current) - (step_size * momentum_decay) * moved
    out[2 * WIDTH :] = bf16(jnp.full((EXTRA, COLS), (1.0 - keep) * push[0], jnp.float32))


def second_gradient(push, push_got, mix, all2, mine, got, ready, far, near, half):
    keep = kept(mix, 1)
    down = ((0,), (0,))
    for k, x, out in ((1, got, far), (0, mine, near)):
        rows = slice(k * WIDTH, (k + 1) * WIDTH)
        gradient = dot(x[...], all2[...], down) * GRAD_SCALE
        moved = ready[rows] - step_size * gradient
        out[:WIDTH] = bf16((1.0 - keep) * moved)
        half[rows] = keep * moved
    first = kept(mix, 0)
    weight = first * push[0] + push_got[0]
    near[WIDTH:] = bf16(jnp.full((EXTRA, COLS), (1.0 - keep) * weight, jnp.float32))


def add_arrived(half, arrived, own1, own2, near, far, values):
    core = lax.axis_index("core")
    near[...] = bf16(half[:WIDTH] + f32(arrived[:WIDTH]))
    far[:WIDTH] = bf16(half[WIDTH:] + f32(arrived[WIDTH : 2 * WIDTH]))
    spare = jnp.zeros((PADDED - ROWS, COLS), jnp.float32)
    for step, own in ((0, own1), (1, own2)):
        low, high = own[:ROWS], own[ROWS:]
        values[step] = bf16(jnp.where(core == 0, low, high))
        row = WIDTH + step * PADDED
        far[row : row + PADDED] = bf16(
            jnp.concatenate([jnp.where(core == 0, high, low), spare], axis=0)
        )


def join_numerator(near, far, values, out, rows_out):
    core = lax.axis_index("core")
    out[0, :, cols_of(core)] = near[...]
    out[0, :, cols_of(1 - core)] = far[:WIDTH]
    for step in range(2):
        row = WIDTH + step * PADDED
        rows_out[step, :, cols_of(core)] = values[step]
        rows_out[step, :, cols_of(1 - core)] = bf16(f32(far[row : row + PADDED])[:ROWS])


def join_received(near, far, out):
    core = lax.axis_index("core")
    out[0, :, cols_of(core)] = near[:WIDTH]
    out[0, :, cols_of(1 - core)] = far[...]


SMEM = pl.BlockSpec(memory_space=pltpu.SMEM)
VMEM = pl.BlockSpec(memory_space=pltpu.VMEM)
ANY = pl.BlockSpec(memory_space=pl.ANY)


def call(body, scalars, fetched, arrays, outs, scratch=(), flops=0):
    fetched = [f if isinstance(f, tuple) else (f, None) for f in fetched]
    result = [jax.ShapeDtypeStruct(shape, kind) for shape, kind in outs]
    n, first, last = len(fetched), len(scalars), len(scalars) + len(fetched)

    def view(ref, where):
        return ref if where is None else ref.at[where]

    def shape(value, where):
        if where is None:
            return value.shape
        if isinstance(where, int):
            return value.shape[1:]
        return (where.size,) + value.shape[1:]

    def kernel(*refs):
        count = last + len(arrays) + len(outs)
        buffers = refs[count : count + n]
        rest = refs[count + n :]
        if n:
            sems, rest = rest[0], rest[1:]
            copies = [
                pltpu.make_async_copy(view(refs[first + i], fetched[i][1]), buffers[i], sems.at[i])
                for i in range(n)
            ]
            for copy in copies:
                copy.start()
            for copy in copies:
                copy.wait()
        body(*refs[:first], *buffers, *refs[last:count], *rest)

    held = [pltpu.VMEM(shape(value, where), value.dtype) for value, where in fetched]
    if n:
        held.append(pltpu.SemaphoreType.DMA((n,)))
    moved = sum(a.size * a.dtype.itemsize for a in [f[0] for f in fetched] + list(arrays) + result)
    return pl.pallas_call(
        kernel,
        out_shape=result,
        in_specs=[SMEM] * len(scalars) + [ANY] * n + [VMEM] * len(arrays),
        out_specs=[VMEM] * len(outs),
        scratch_shapes=held + [pltpu.VMEM(size, kind) for size, kind in scratch],
        compiler_params=pltpu.CompilerParams(vmem_limit_bytes=20 * 2**20),
        cost_estimate=pl.CostEstimate(flops=flops, bytes_accessed=moved, transcendentals=0),
        name=body.func.__name__ if isinstance(body, functools.partial) else body.__name__,
    )(*scalars, *[f[0] for f in fetched], *arrays)


def z_pairs(step):
    pairs = []
    for zh in range(N_Z):
        for core in range(2):
            turn = (1, 3)[step ^ core]
            pairs.append((zh * 2 + core, (zh ^ turn) * 2 + core))
    return pairs


def over_z(value, step):
    return lax.ppermute(value, ("z_hi", "core"), z_pairs(step))


def over_y(value):
    return lax.all_to_all(value, "y", 0, 0, tiled=True)


def swap_core(value):
    return lax.ppermute(value, "core", [(0, 1), (1, 0)])


def to_group(value, hop):
    count = SIZES[0] * SIZES[1]
    return lax.ppermute(value, GROUP, [(i, (i + hop) % count) for i in range(count)])


def reduce_slab(step, part, taught):
    columns = part.shape[1]
    parts = over_y(part.reshape(N_Y, SLAB, columns))
    own = ((BLOCK, COLS), F32)
    whole = ((SLAB, columns), B16)
    slab, values = call(functools.partial(sum_over_y, step), [], [parts], [taught], [whole, own])
    return call(add_slab, [], [], [slab, over_z(slab, 0), values], [whole, own])


def local(inputs, targets, numerator, momentum, received, push_weight, received_weight, mix_share):
    push, push_got, mix = push_weight, received_weight, mix_share

    part = [((TOKENS, COLS), B16)] * 2
    part_far, part_own = call(first_values, [push], [(inputs, 0), (numerator, 0)], [], part)
    part1 = bf16(f32(part_own) + f32(swap_core(part_far)))

    targets, part_far = lax.optimization_barrier((targets, part_far))
    mine, velocity_far = call(
        make_message,
        [],
        [inputs, (numerator, 0), (received, 0), targets, (momentum, 0)],
        [],
        [((MESSAGE, WIDTH), B16), ((WIDTH, COLS), F32)],
    )
    got = swap_core(mine)
    velocity_got = swap_core(velocity_far)

    tile = ((2 * WIDTH, COLS), F32)
    part2, ahead, base, taught = call(
        second_values,
        [push, push_got, mix],
        [(numerator, 0), (received, 0), (momentum, 0), targets],
        [mine, got, velocity_got],
        [((TOKENS, COLS + HALF), B16), tile, tile, ((2, BLOCK, COLS), F32)],
    )

    spread = ((N_Y, SLAB, COLS), B16)
    own = ((BLOCK, COLS), F32)
    slab1, own1 = reduce_slab(0, part1, taught)
    sent, own1 = call(add_and_spread, [], [], [slab1, over_z(slab1, 1), own1], [spread, own])
    all1 = over_y(sent).reshape(TOKENS, COLS)

    slab2, own2 = reduce_slab(1, part2, taught)
    ahead2, gram, own2 = call(
        add_and_part,
        [],
        [],
        [slab2, over_z(slab2, 1), own2],
        [((SLAB, COLS), B16), ((SLAB, HALF), B16), own],
    )
    gram_got = swap_core(gram)
    sent, own2 = call(
        second_residual,
        [push, push_got, mix],
        [all1],
        [gram, gram_got, ahead2, own2],
        [spread, own],
        [((SLAB, COLS), F32)],
    )
    all2 = over_y(sent).reshape(TOKENS, COLS)

    outgoing, ready = call(
        first_gradient,
        [push, mix],
        [
            all1,
            (mine, pl.ds(0, TOKENS)),
            (got, pl.ds(0, TOKENS)),
            ahead,
            base,
            (momentum, 0),
            velocity_got,
        ],
        [],
        [((2 * WIDTH + EXTRA, COLS), B16), tile],
    )
    arrived = to_group(outgoing, 1)

    far, near, half = call(
        second_gradient,
        [push, push_got, mix],
        [all2, (mine, pl.ds(X2_AT, TOKENS)), (got, pl.ds(X2_AT, TOKENS)), ready],
        [],
        [((WIDTH, COLS), B16), ((WIDTH + EXTRA, COLS), B16), tile],
    )

    count = SIZES[0] * SIZES[1]
    hop = [(i * 2 + c, (i + 2) % count * 2 + 1 - c) for i in range(count) for c in range(2)]
    sent_far = lax.ppermute(far, GROUP + ("core",), hop)
    sent_own = to_group(near, 2)

    current, current_far, values = call(
        add_arrived,
        [],
        [half, arrived, own1, own2],
        [],
        [((WIDTH, COLS), B16), ((WIDTH + 2 * PADDED, COLS), B16), ((2, ROWS, COLS), B16)],
    )
    whole = ((1, WIDTH, VALUES), B16)
    final_numerator, value_rows = call(
        join_numerator,
        [],
        [],
        [current, swap_core(current_far), values],
        [whole, ((2, ROWS, VALUES), B16)],
    )
    arrived_weight = f32(arrived[2 * WIDTH, :1])
    keep = f32(mix[0]) / 8.0
    final_weight = keep[1] * (keep[0] * push + push_got) + arrived_weight
    sent_far, final_numerator, final_weight = lax.optimization_barrier(
        (sent_far, final_numerator, final_weight)
    )
    (final_received,) = call(join_received, [], [], [sent_own, sent_far], [whole])
    return final_numerator, final_weight, final_received, f32(sent_own[WIDTH, :1]), value_rows


def solution(mesh):
    fine = Mesh(mesh.devices.reshape(SIZES), GROUP + MP)
    placed = (
        P(None, GROUP, MP),
        P(None, GROUP + MP, None),
        P(GROUP, MP, None),
        P(GROUP, MP, None),
        P(GROUP, MP, None),
        P(GROUP),
        P(GROUP),
        P(GROUP, None),
    )
    return jax.shard_map(
        local,
        mesh=fine,
        in_specs=placed,
        out_specs=(
            P(GROUP, MP, None),
            P(GROUP),
            P(GROUP, MP, None),
            P(GROUP),
            P(None, GROUP + MP, None),
        ),
        check_vma=False,
    )
```

```python
import functools
import math

import jax
import jax.numpy as jnp
from jax import lax
from jax.experimental import pallas as pl
from jax.experimental.pallas import tpu as pltpu
from jax.sharding import Mesh
from jax.sharding import PartitionSpec as P

GROUP = ("x", "z_lo")
MP = ("z_hi", "y", "core")
SIZES = (4, 4, 4, 4, 2)
N_Z, N_Y = SIZES[2], SIZES[3]

momentum_decay = 0.9
step_size = 0.5

ROWS = 24
BLOCK = 2 * ROWS
SLAB = N_Z * BLOCK
TOKENS = N_Y * SLAB
WIDTH = 256
VALUES = 1024
COLS = VALUES // 2
HALF = TOKENS // 2
PADDED = 32
EXTRA = 16
ROW_SCALE = 1.0 / math.sqrt(WIDTH * N_Z * N_Y * 2)
GRAD_SCALE = 1.0 / math.sqrt(TOKENS)

X2_AT = TOKENS
W_AT = 2 * TOKENS
REC_AT = W_AT + 2 * WIDTH
T_AT = REC_AT + 2 * WIDTH
MESSAGE = T_AT + 4 * PADDED

B16, F32 = jnp.bfloat16, jnp.float32


def f32(value):
    return value.astype(jnp.float32)


def bf16(value):
    return value.astype(jnp.bfloat16)


def dot(a, b, dims=((1,), (0,))):
    return lax.dot_general(a, b, (dims, ((), ())), preferred_element_type=jnp.float32)


def cols_of(core):
    return pl.ds(pl.multiple_of(core * COLS, COLS), COLS)


def half_of(core):
    return pl.ds(pl.multiple_of(core * HALF, 16), HALF)


def own_block():
    return pl.ds(pl.multiple_of(lax.axis_index("z_hi") * BLOCK, 16), BLOCK)


def kept(mix, step):
    return mix[0, step].astype(jnp.float32) * 0.125


def by_y():
    return [((zh * N_Y + y) * BLOCK, (y * N_Z + zh) * BLOCK) for zh in range(N_Z) for y in range(N_Y)]


def first_values(push, x, w, far, own):
    core = lax.axis_index("core")
    for out, side in ((far, 1 - core), (own, core)):
        scaled = bf16(f32(w[:, cols_of(side)]) / push[0])
        part = bf16(dot(x[...], scaled) * ROW_SCALE)
        for at, to in by_y():
            out[to : to + BLOCK] = part[at : at + BLOCK]


def make_message(x, w, rec, targets, velocity, message, velocity_far):
    far = 1 - lax.axis_index("core")
    for step in range(2):
        for at, to in by_y():
            message[step * TOKENS + to : step * TOKENS + to + BLOCK] = x[step, at : at + BLOCK]
    for ref, row in ((w, W_AT), (rec, REC_AT)):
        half = ref[:, cols_of(far)]
        message[row : row + WIDTH] = half[:, :WIDTH]
        message[row + WIDTH : row + 2 * WIDTH] = half[:, WIDTH:]
    spare = jnp.zeros((PADDED - ROWS, COLS), jnp.float32)
    for step in range(2):
        half = bf16(jnp.concatenate([f32(targets[step, :, cols_of(far)]), spare], axis=0))
        row = T_AT + 2 * step * PADDED
        message[row : row + PADDED] = half[:, :WIDTH]
        message[row + PADDED : row + 2 * PADDED] = half[:, WIDTH:]
    velocity_far[...] = velocity[:, cols_of(far)]


def second_values(
    push, push_got, mix, w, rec, velocity, targets, mine, got, velocity_got, out, ahead, base, taught
):
    core = lax.axis_index("core")
    keep = kept(mix, 0)
    weight = keep * push[0] + push_got[0]
    side = cols_of(core)
    decayed = step_size * momentum_decay
    ahead[:WIDTH] = f32(w[:, side]) - decayed * velocity[:, side]
    base[:WIDTH] = keep * ahead[:WIDTH] + f32(rec[:, side])
    for k in range(2):
        part = slice(k * WIDTH, (k + 1) * WIDTH)
        ahead[WIDTH:, part] = (
            f32(got[W_AT + k * WIDTH : W_AT + (k + 1) * WIDTH]) - decayed * velocity_got[:, part]
        )
        base[WIDTH:, part] = keep * ahead[WIDTH:, part] + f32(
            got[REC_AT + k * WIDTH : REC_AT + (k + 1) * WIDTH]
        )
    scaled = bf16(base[...] / weight)
    near, far = mine[X2_AT : X2_AT + TOKENS], got[X2_AT : X2_AT + TOKENS]
    out[:, :COLS] = bf16((dot(near, scaled[:WIDTH]) + dot(far, scaled[WIDTH:])) * ROW_SCALE)
    rows = half_of(core)
    across = ((1,), (1,))
    out[:, COLS:] = bf16(dot(near, mine[rows], across) + dot(far, got[rows], across))
    for step in range(2):
        own = f32(targets[step, :, side])
        row = T_AT + 2 * step * PADDED
        other = jnp.concatenate(
            [f32(got[row : row + PADDED]), f32(got[row + PADDED : row + 2 * PADDED])], axis=1
        )[:ROWS]
        taught[step, :ROWS] = jnp.where(core == 0, own, other)
        taught[step, ROWS:] = jnp.where(core == 0, other, own)


def sum_over_y(step, parts, taught, slab, own):
    total = f32(parts[0])
    for y in range(1, N_Y):
        total = total + f32(parts[y])
    slab[...] = bf16(total)
    rows = own_block()
    total = f32(parts[0, rows, :COLS])
    for y in range(1, N_Y):
        total = total + f32(parts[y, rows, :COLS])
    own[...] = total
    slab[rows, :COLS] = bf16(total - taught[step])


def add_slab(mine, got, own, out, own_out):
    out[...] = bf16(f32(mine[...]) + f32(got[...]))
    own_out[...] = own[...] + f32(got[own_block(), :COLS])


def add_and_spread(mine, got, own, out, own_out):
    total = bf16(f32(mine[...]) + f32(got[...]))
    for y in range(N_Y):
        out[y] = total
    own_out[...] = own[...] + f32(got[own_block()])


def add_and_part(mine, got, own, out, gram, own_out):
    out[...] = bf16(f32(mine[:, :COLS]) + f32(got[:, :COLS]))
    gram[...] = bf16(f32(mine[:, COLS:]) + f32(got[:, COLS:]))
    own_out[...] = own[...] + f32(got[own_block(), :COLS])


def second_residual(push, push_got, mix, all1, gram, gram_got, base, own, out, own_out, turned):
    core = lax.axis_index("core")
    keep = kept(mix, 0)
    back = step_size * GRAD_SCALE * ROW_SCALE * keep / (keep * push[0] + push_got[0])
    near, far = all1[half_of(core)], all1[half_of(1 - core)]
    turned[...] = (dot(gram[...], near) + dot(gram_got[...], far)) * back
    residual = bf16(f32(base[...]) - turned[...])
    for y in range(N_Y):
        out[y] = residual
    own_out[...] = own[...] - turned[own_block()]


def first_gradient(push, mix, all1, mine, got, ahead, base, velocity, velocity_got, near, far, ready):
    side = cols_of(lax.axis_index("core"))
    keep = kept(mix, 0)
    down = ((0,), (0,))
    for k, x, old, out in ((0, mine, velocity[:, side], near), (1, got, velocity_got[...], far)):
        rows = slice(k * WIDTH, (k + 1) * WIDTH)
        gradient = dot(x[:TOKENS], all1[...], down) * GRAD_SCALE
        out[:WIDTH] = bf16((1.0 - keep) * (ahead[rows] - step_size * gradient))
        current = bf16(base[rows] - (step_size * keep) * gradient)
        moved = momentum_decay * old + gradient
        ready[rows] = f32(current) - (step_size * momentum_decay) * moved
    near[WIDTH:] = bf16(jnp.full((EXTRA, COLS), (1.0 - keep) * push[0], jnp.float32))


def second_gradient(push, push_got, mix, mine, got, ready, all2, own1, own2, far, near, half, message):
    core = lax.axis_index("core")
    keep = kept(mix, 1)
    down = ((0,), (0,))
    for k, x, out, held in ((1, got, far, message), (0, mine, near, half)):
        gradient = dot(x[...], all2[...], down) * GRAD_SCALE
        moved = ready[k * WIDTH : (k + 1) * WIDTH] - step_size * gradient
        out[:WIDTH] = bf16((1.0 - keep) * moved)
        held[:WIDTH] = keep * moved
    weight = kept(mix, 0) * push[0] + push_got[0]
    near[WIDTH:] = bf16(jnp.full((EXTRA, COLS), (1.0 - keep) * weight, jnp.float32))
    for step, own in ((0, own1), (1, own2)):
        row = WIDTH + step * ROWS
        message[row : row + ROWS] = jnp.where(core == 0, own[ROWS:], own[:ROWS])


def join_numerator(
    push, push_got, mix, half, message, own1, own2, arrived, arrived_far, out, rows_out, weight
):
    core = lax.axis_index("core")
    out[0, :, cols_of(core)] = bf16(half[...] + f32(arrived[:WIDTH]))
    out[0, :, cols_of(1 - core)] = bf16(message[:WIDTH] + f32(arrived_far[...]))
    for step, own in ((0, own1), (1, own2)):
        row = WIDTH + step * ROWS
        rows_out[step, :, cols_of(core)] = bf16(jnp.where(core == 0, own[:ROWS], own[ROWS:]))
        rows_out[step, :, cols_of(1 - core)] = bf16(message[row : row + ROWS])
    last = kept(mix, 0) * push[0] + push_got[0]
    weight[0] = kept(mix, 1) * last + jnp.max(f32(arrived[WIDTH:]))


def join_received(near, far, out, weight):
    core = lax.axis_index("core")
    out[0, :, cols_of(core)] = near[:WIDTH]
    out[0, :, cols_of(1 - core)] = far[...]
    weight[0] = jnp.max(f32(near[WIDTH:]))


SMEM = pl.BlockSpec(memory_space=pltpu.SMEM)
VMEM = pl.BlockSpec(memory_space=pltpu.VMEM)
HBM = pl.BlockSpec(memory_space=pltpu.HBM)


def call(body, scalars, fetched, arrays, outs, scratch=(), flops=0):
    fetched = [f if isinstance(f, tuple) else (f, None) for f in fetched]
    result = [jax.ShapeDtypeStruct(shape, kind) for shape, kind in outs]
    n, first, last = len(fetched), len(scalars), len(scalars) + len(fetched)

    def view(ref, where):
        return ref if where is None else ref.at[where]

    def shape(value, where):
        if where is None:
            return value.shape
        if isinstance(where, int):
            return value.shape[1:]
        return (where.size,) + value.shape[1:]

    def kernel(*refs):
        count = last + len(arrays) + len(outs)
        buffers = refs[count : count + n]
        rest = refs[count + n :]
        if n:
            sems, rest = rest[0], rest[1:]
            copies = [
                pltpu.make_async_copy(view(refs[first + i], fetched[i][1]), buffers[i], sems.at[i])
                for i in range(n)
            ]
            for copy in copies:
                copy.start()
            for copy in copies:
                copy.wait()
        body(*refs[:first], *buffers, *refs[last:count], *rest)

    held = [pltpu.VMEM(shape(value, where), value.dtype) for value, where in fetched]
    if n:
        held.append(pltpu.SemaphoreType.DMA((n,)))
    moved = sum(a.size * a.dtype.itemsize for a in [f[0] for f in fetched] + list(arrays) + result)
    return pl.pallas_call(
        kernel,
        out_shape=result,
        in_specs=[SMEM] * len(scalars) + [HBM] * n + [VMEM] * len(arrays),
        out_specs=[SMEM if shape == (1,) else VMEM for shape, _ in outs],
        scratch_shapes=held + [pltpu.VMEM(size, kind) for size, kind in scratch],
        compiler_params=pltpu.CompilerParams(vmem_limit_bytes=20 * 2**20),
        cost_estimate=pl.CostEstimate(flops=flops, bytes_accessed=moved, transcendentals=0),
        name=body.func.__name__ if isinstance(body, functools.partial) else body.__name__,
    )(*scalars, *[f[0] for f in fetched], *arrays)


def z_pairs(step):
    pairs = []
    for zh in range(N_Z):
        for core in range(2):
            turn = (1, 3)[step ^ core]
            pairs.append((zh * 2 + core, (zh ^ turn) * 2 + core))
    return pairs


def over_z(value, step):
    return lax.ppermute(value, ("z_hi", "core"), z_pairs(step))


def over_y(value):
    return lax.all_to_all(value, "y", 0, 0, tiled=True)


def swap_core(value):
    return lax.ppermute(value, "core", [(0, 1), (1, 0)])


def to_group(value, hop):
    count = SIZES[0] * SIZES[1]
    return lax.ppermute(value, GROUP, [(i, (i + hop) % count) for i in range(count)])


def to_group_other(value, hop):
    count = SIZES[0] * SIZES[1]
    pairs = [(i * 2 + c, (i + hop) % count * 2 + 1 - c) for i in range(count) for c in range(2)]
    return lax.ppermute(value, GROUP + ("core",), pairs)


def sum_slab(step, parts, taught):
    own = ((BLOCK, COLS), F32)
    whole = ((SLAB, parts.shape[2]), B16)
    slab, values = call(functools.partial(sum_over_y, step), [], [parts], [taught], [whole, own])
    return call(add_slab, [], [], [slab, over_z(slab, 0), values], [whole, own])


def local(inputs, targets, numerator, momentum, received, push_weight, received_weight, mix_share):
    push, push_got, mix = push_weight, received_weight, mix_share

    part = [((TOKENS, COLS), B16)] * 2
    part_far, part_own = call(first_values, [push], [(inputs, 0), (numerator, 0)], [], part)
    part1 = bf16(f32(part_own) + f32(swap_core(part_far)))

    targets, part_far = lax.optimization_barrier((targets, part_far))
    mine, velocity_far = call(
        make_message,
        [],
        [inputs, (numerator, 0), (received, 0), targets, (momentum, 0)],
        [],
        [((MESSAGE, WIDTH), B16), ((WIDTH, COLS), F32)],
    )
    got = swap_core(mine)
    velocity_got = swap_core(velocity_far)

    tile = ((2 * WIDTH, COLS), F32)
    part2, ahead, base, taught = call(
        second_values,
        [push, push_got, mix],
        [(numerator, 0), (received, 0), (momentum, 0), targets],
        [mine, got, velocity_got],
        [((TOKENS, COLS + HALF), B16), tile, tile, ((2, BLOCK, COLS), F32)],
    )

    spread = ((N_Y, SLAB, COLS), B16)
    own = ((BLOCK, COLS), F32)
    parts2 = over_y(part2.reshape(N_Y, SLAB, COLS + HALF))
    slab1, own1 = sum_slab(0, over_y(part1.reshape(N_Y, SLAB, COLS)), taught)
    parts2, _ = lax.optimization_barrier((parts2, slab1))
    sent, own1 = call(add_and_spread, [], [], [slab1, over_z(slab1, 1), own1], [spread, own])
    all1 = over_y(sent).reshape(TOKENS, COLS)

    slab2, own2 = sum_slab(1, parts2, taught)
    near, far, ready = call(
        first_gradient,
        [push, mix],
        [
            all1,
            (mine, pl.ds(0, TOKENS)),
            (got, pl.ds(0, TOKENS)),
            ahead,
            base,
            (momentum, 0),
            velocity_got,
        ],
        [],
        [((WIDTH + EXTRA, COLS), B16), ((WIDTH, COLS), B16), tile],
    )
    slab2_got, _ = lax.optimization_barrier((over_z(slab2, 1), far))
    arrived, arrived_far = to_group(near, 1), to_group_other(far, 1)
    ahead2, gram, own2 = call(
        add_and_part,
        [],
        [],
        [slab2, slab2_got, own2],
        [((SLAB, COLS), B16), ((SLAB, HALF), B16), own],
    )
    gram_got = swap_core(gram)
    sent, own2 = call(
        second_residual,
        [push, push_got, mix],
        [],
        [all1, gram, gram_got, ahead2, own2],
        [spread, own],
        [((SLAB, COLS), F32)],
    )
    all2 = over_y(sent).reshape(TOKENS, COLS)
    all2, arrived, arrived_far = lax.optimization_barrier((all2, arrived, arrived_far))

    far, near, half, message = call(
        second_gradient,
        [push, push_got, mix],
        [(mine, pl.ds(X2_AT, TOKENS)), (got, pl.ds(X2_AT, TOKENS)), ready],
        [all2, own1, own2],
        [
            ((WIDTH, COLS), B16),
            ((WIDTH + EXTRA, COLS), B16),
            ((WIDTH, COLS), F32),
            ((WIDTH + 2 * ROWS, COLS), F32),
        ],
    )

    sent_far, sent_own = to_group_other(far, 2), to_group(near, 2)
    whole = ((1, WIDTH, VALUES), B16)
    number = ((1,), F32)
    final_numerator, value_rows, final_weight = call(
        join_numerator,
        [push, push_got, mix],
        [],
        [half, swap_core(message), own1, own2, arrived, arrived_far],
        [whole, ((2, ROWS, VALUES), B16), number],
    )
    sent_far, final_numerator = lax.optimization_barrier((sent_far, final_numerator))
    final_received, got_weight = call(join_received, [], [], [sent_own, sent_far], [whole, number])
    return final_numerator, final_weight, final_received, got_weight, value_rows


def solution(mesh):
    fine = Mesh(mesh.devices.reshape(SIZES), GROUP + MP)
    placed = (
        P(None, GROUP, MP),
        P(None, GROUP + MP, None),
        P(GROUP, MP, None),
        P(GROUP, MP, None),
        P(GROUP, MP, None),
        P(GROUP),
        P(GROUP),
        P(GROUP, None),
    )
    return jax.shard_map(
        local,
        mesh=fine,
        in_specs=placed,
        out_specs=(
            P(GROUP, MP, None),
            P(GROUP),
            P(GROUP, MP, None),
            P(GROUP),
            P(None, GROUP + MP, None),
        ),
        check_vma=False,
    )
```

```python
import functools
import math

import jax
import jax.numpy as jnp
from jax import lax
from jax.experimental import pallas as pl
from jax.experimental.pallas import tpu as pltpu
from jax.sharding import Mesh
from jax.sharding import PartitionSpec as P

GROUP = ("x", "z_lo")
MP = ("z_hi", "y", "core")
SIZES = (4, 4, 4, 4, 2)
N_Z, N_Y = SIZES[2], SIZES[3]

momentum_decay = 0.9
step_size = 0.5

ROWS = 24
BLOCK = 2 * ROWS
SLAB = N_Z * BLOCK
TOKENS = N_Y * SLAB
WIDTH = 256
VALUES = 1024
COLS = VALUES // 2
HALF = TOKENS // 2
PADDED = 32
EXTRA = 16
ROW_SCALE = 1.0 / math.sqrt(WIDTH * N_Z * N_Y * 2)
GRAD_SCALE = 1.0 / math.sqrt(TOKENS)

X2_AT = TOKENS
W_AT = 2 * TOKENS
REC_AT = W_AT + 2 * WIDTH
T_AT = REC_AT + 2 * WIDTH
MESSAGE = T_AT + 4 * PADDED

B16, F32 = jnp.bfloat16, jnp.float32


def f32(value):
    return value.astype(jnp.float32)


def bf16(value):
    return value.astype(jnp.bfloat16)


def dot(a, b, dims=((1,), (0,))):
    return lax.dot_general(a, b, (dims, ((), ())), preferred_element_type=jnp.float32)


def cols_of(core):
    return pl.ds(pl.multiple_of(core * COLS, COLS), COLS)


def half_of(core):
    return pl.ds(pl.multiple_of(core * HALF, 16), HALF)


def own_block():
    return pl.ds(pl.multiple_of(lax.axis_index("z_hi") * BLOCK, 16), BLOCK)


def kept(mix, step):
    return mix[0, step].astype(jnp.float32) * 0.125


def by_y():
    return [((zh * N_Y + y) * BLOCK, (y * N_Z + zh) * BLOCK) for zh in range(N_Z) for y in range(N_Y)]


def first_values(push, x, w, far, own):
    core = lax.axis_index("core")
    for out, side in ((far, 1 - core), (own, core)):
        scaled = bf16(f32(w[:, cols_of(side)]) / push[0])
        part = bf16(dot(x[...], scaled) * ROW_SCALE)
        for at, to in by_y():
            out[to : to + BLOCK] = part[at : at + BLOCK]


def make_message(x, w, rec, targets, velocity, message, velocity_far):
    far = 1 - lax.axis_index("core")
    for step in range(2):
        for at, to in by_y():
            message[step * TOKENS + to : step * TOKENS + to + BLOCK] = x[step, at : at + BLOCK]
    for ref, row in ((w, W_AT), (rec, REC_AT)):
        half = ref[:, cols_of(far)]
        message[row : row + WIDTH] = half[:, :WIDTH]
        message[row + WIDTH : row + 2 * WIDTH] = half[:, WIDTH:]
    spare = jnp.zeros((PADDED - ROWS, COLS), jnp.float32)
    for step in range(2):
        half = bf16(jnp.concatenate([f32(targets[step, :, cols_of(far)]), spare], axis=0))
        row = T_AT + 2 * step * PADDED
        message[row : row + PADDED] = half[:, :WIDTH]
        message[row + PADDED : row + 2 * PADDED] = half[:, WIDTH:]
    velocity_far[...] = velocity[:, cols_of(far)]


def tile(mix, w, rec, velocity, got, velocity_got, k):
    keep = kept(mix, 0)
    if k == 0:
        side = cols_of(lax.axis_index("core"))
        start, arrived, old = w[:, side], rec[:, side], velocity[:, side]
    else:
        start, arrived = (
            jnp.concatenate([got[at : at + WIDTH], got[at + WIDTH : at + 2 * WIDTH]], axis=1)
            for at in (W_AT, REC_AT)
        )
        old = velocity_got[...]
    ahead = f32(start) - (step_size * momentum_decay) * old
    return ahead, keep * ahead + f32(arrived), old


def second_values(push, push_got, mix, w, rec, velocity, targets, velocity_got, mine, got, out, taught):
    core = lax.axis_index("core")
    weight = kept(mix, 0) * push[0] + push_got[0]
    near, far = mine[X2_AT : X2_AT + TOKENS], got[X2_AT : X2_AT + TOKENS]
    scaled = [bf16(tile(mix, w, rec, velocity, got, velocity_got, k)[1] / weight) for k in range(2)]
    out[:, :COLS] = bf16((dot(near, scaled[0]) + dot(far, scaled[1])) * ROW_SCALE)
    rows = half_of(core)
    across = ((1,), (1,))
    out[:, COLS:] = bf16(dot(near, mine[rows], across) + dot(far, got[rows], across))
    for step in range(2):
        own = f32(targets[step, :, cols_of(core)])
        row = T_AT + 2 * step * PADDED
        other = jnp.concatenate(
            [f32(got[row : row + PADDED]), f32(got[row + PADDED : row + 2 * PADDED])], axis=1
        )[:ROWS]
        taught[step, :ROWS] = jnp.where(core == 0, own, other)
        taught[step, ROWS:] = jnp.where(core == 0, other, own)


def sum_over_y(step, parts, taught, slab, own):
    total = f32(parts[0])
    for y in range(1, N_Y):
        total = total + f32(parts[y])
    slab[...] = bf16(total)
    rows = own_block()
    total = f32(parts[0, rows, :COLS])
    for y in range(1, N_Y):
        total = total + f32(parts[y, rows, :COLS])
    own[...] = total
    slab[rows, :COLS] = bf16(total - taught[step])


def add_slab(own, mine, got, out, own_out):
    out[...] = bf16(f32(mine[...]) + f32(got[...]))

    def later():
        own_out[...] = own[...] + f32(got[own_block(), :COLS])

    return later


def add_and_spread(own, mine, got, out, own_out):
    total = bf16(f32(mine[...]) + f32(got[...]))
    for y in range(N_Y):
        out[y] = total

    def later():
        own_out[...] = own[...] + f32(got[own_block()])

    return later


def add_and_part(own, mine, got, out, gram, own_out):
    out[...] = bf16(f32(mine[:, :COLS]) + f32(got[:, :COLS]))
    gram[...] = bf16(f32(mine[:, COLS:]) + f32(got[:, COLS:]))

    def later():
        own_out[...] = own[...] + f32(got[own_block(), :COLS])

    return later


def second_residual(push, push_got, mix, own, all1, gram, gram_got, base, out, own_out, turned):
    core = lax.axis_index("core")
    keep = kept(mix, 0)
    back = step_size * GRAD_SCALE * ROW_SCALE * keep / (keep * push[0] + push_got[0])
    near, far = all1[half_of(core)], all1[half_of(1 - core)]
    turned[...] = (dot(gram[...], near) + dot(gram_got[...], far)) * back
    residual = bf16(f32(base[...]) - turned[...])
    for y in range(N_Y):
        out[y] = residual

    def later():
        own_out[...] = own[...] - turned[own_block()]

    return later


def first_gradient(push, mix, w, rec, velocity, velocity_got, all1, mine, got, near, far, ready):
    keep = kept(mix, 0)
    down = ((0,), (0,))
    for k, x, out in ((0, mine, near), (1, got, far)):
        ahead, base, old = tile(mix, w, rec, velocity, got, velocity_got, k)
        gradient = dot(x[:TOKENS], all1[...], down) * GRAD_SCALE
        out[:WIDTH] = bf16((1.0 - keep) * (ahead - step_size * gradient))
        current = bf16(base - (step_size * keep) * gradient)
        moved = momentum_decay * old + gradient
        ready[k * WIDTH : (k + 1) * WIDTH] = f32(current) - (step_size * momentum_decay) * moved
    near[WIDTH:] = bf16(jnp.full((EXTRA, COLS), (1.0 - keep) * push[0], jnp.float32))


def second_gradient(push, push_got, mix, ready, own1, own2, mine, got, all2, far, near, half, message):
    core = lax.axis_index("core")
    keep = kept(mix, 1)
    down = ((0,), (0,))
    for k, x, out, held in ((1, got, far, message), (0, mine, near, half)):
        gradient = dot(x[X2_AT : X2_AT + TOKENS], all2[...], down) * GRAD_SCALE
        moved = ready[k * WIDTH : (k + 1) * WIDTH] - step_size * gradient
        out[:WIDTH] = bf16((1.0 - keep) * moved)
        held[:WIDTH] = keep * moved
    weight = kept(mix, 0) * push[0] + push_got[0]
    near[WIDTH:] = bf16(jnp.full((EXTRA, COLS), (1.0 - keep) * weight, jnp.float32))
    for step, own in ((0, own1), (1, own2)):
        row = WIDTH + step * ROWS
        message[row : row + ROWS] = jnp.where(core == 0, own[ROWS:], own[:ROWS])


def join_numerator(
    push, push_got, mix, own1, own2, arrived, arrived_far, half, message, out, rows_out, weight
):
    core = lax.axis_index("core")
    out[0, :, cols_of(core)] = bf16(half[...] + f32(arrived[:WIDTH]))
    out[0, :, cols_of(1 - core)] = bf16(message[:WIDTH] + f32(arrived_far[...]))
    for step, own in ((0, own1), (1, own2)):
        row = WIDTH + step * ROWS
        rows_out[step, :, cols_of(core)] = bf16(jnp.where(core == 0, own[:ROWS], own[ROWS:]))
        rows_out[step, :, cols_of(1 - core)] = bf16(message[row : row + ROWS])
    last = kept(mix, 0) * push[0] + push_got[0]
    weight[0] = kept(mix, 1) * last + jnp.max(f32(arrived[WIDTH:]))


def join_received(near, far, out, weight):
    core = lax.axis_index("core")
    out[0, :, cols_of(core)] = near[:WIDTH]
    out[0, :, cols_of(1 - core)] = far[...]
    weight[0] = jnp.max(f32(near[WIDTH:]))


SMEM = pl.BlockSpec(memory_space=pltpu.SMEM)
HBM = pl.BlockSpec(memory_space=pltpu.HBM)
VMEM = pl.BlockSpec(memory_space=pltpu.VMEM)


def call(body, scalars, fetched, late, near, outs, scratch=(), flops=0):
    copied = [f if isinstance(f, tuple) else (f, None) for f in list(fetched) + list(late)]
    n, m, first = len(copied), len(fetched), len(scalars)
    last = first + n + len(near)
    far = [k for k, (_, _, in_hbm) in enumerate(outs) if in_hbm]

    def view(ref, where):
        return ref if where is None else ref.at[where]

    def kernel(*refs):
        out = list(refs[last : last + len(outs)])
        rest = list(refs[last + len(outs) :])
        buffers, out_buffers, rest = rest[:n], rest[n : n + len(far)], rest[n + len(far) :]
        sems = rest.pop(0) if n else None
        out_sems = rest.pop(0) if far else None
        copies = [
            pltpu.make_async_copy(view(refs[first + i], copied[i][1]), buffers[i], sems.at[i])
            for i in range(n)
        ]
        for copy in copies:
            copy.start()
        for copy in copies[:m]:
            copy.wait()
        written = list(out)
        for k, buffer in zip(far, out_buffers):
            written[k] = buffer
        later = body(*refs[:first], *buffers, *refs[first + n : last], *written, *rest)
        for copy in copies[m:]:
            copy.wait()
        if late:
            later()
        copies = [
            pltpu.make_async_copy(buffer, out[k], out_sems.at[i])
            for i, (k, buffer) in enumerate(zip(far, out_buffers))
        ]
        for copy in copies:
            copy.start()
        for copy in copies:
            copy.wait()

    held = [
        pltpu.VMEM(value.shape if where is None else value.shape[1:], value.dtype)
        for value, where in copied
    ]
    held += [pltpu.VMEM(*outs[k][:2]) for k in far]
    held += [pltpu.SemaphoreType.DMA((n,))] if n else []
    held += [pltpu.SemaphoreType.DMA((len(far),))] if far else []
    result, specs = [], []
    for shape, kind, in_hbm in outs:
        result.append(pltpu.HBM(shape, kind) if in_hbm else jax.ShapeDtypeStruct(shape, kind))
        specs.append(HBM if in_hbm else SMEM if shape == (1,) else VMEM)
    arrays = [pltpu.with_memory_space_constraint(value, pltpu.HBM) for value, _ in copied]
    moved = sum(a.size * a.dtype.itemsize for a in arrays + list(near))
    moved += sum(math.prod(shape) * jnp.dtype(kind).itemsize for shape, kind, _ in outs)
    return pl.pallas_call(
        kernel,
        out_shape=result,
        in_specs=[SMEM] * first + [HBM] * n + [VMEM] * len(near),
        out_specs=specs,
        scratch_shapes=held + [pltpu.VMEM(size, kind) for size, kind in scratch],
        compiler_params=pltpu.CompilerParams(vmem_limit_bytes=20 * 2**20),
        cost_estimate=pl.CostEstimate(flops=flops, bytes_accessed=moved, transcendentals=0),
        name=body.func.__name__ if isinstance(body, functools.partial) else body.__name__,
    )(*scalars, *arrays, *near)


def z_pairs(step):
    pairs = []
    for zh in range(N_Z):
        for core in range(2):
            turn = (1, 3)[step ^ core]
            pairs.append((zh * 2 + core, (zh ^ turn) * 2 + core))
    return pairs


def over_z(value, step):
    return lax.ppermute(value, ("z_hi", "core"), z_pairs(step))


def over_y(value):
    return lax.all_to_all(value, "y", 0, 0, tiled=True)


def swap_core(value):
    return lax.ppermute(value, "core", [(0, 1), (1, 0)])


def to_group(value, hop):
    count = SIZES[0] * SIZES[1]
    return lax.ppermute(value, GROUP, [(i, (i + hop) % count) for i in range(count)])


def to_group_other(value, hop):
    count = SIZES[0] * SIZES[1]
    pairs = [(i * 2 + c, (i + hop) % count * 2 + 1 - c) for i in range(count) for c in range(2)]
    return lax.ppermute(value, GROUP + ("core",), pairs)


OWN = ((BLOCK, COLS), F32, True)


def sum_slab(step, parts, taught):
    whole = ((SLAB, parts.shape[2]), B16, False)
    slab, own = call(functools.partial(sum_over_y, step), [], [parts], [], [taught], [whole, OWN])
    return call(add_slab, [], [], [own], [slab, over_z(slab, 0)], [whole, OWN])


def local(inputs, targets, numerator, momentum, received, push_weight, received_weight, mix_share):
    push, push_got, mix = push_weight, received_weight, mix_share
    state = [(numerator, 0), (received, 0), (momentum, 0)]

    part = [((TOKENS, COLS), B16, False)] * 2
    part_far, part_own = call(first_values, [push], [(inputs, 0), (numerator, 0)], [], [], part)
    part1 = bf16(f32(part_own) + f32(swap_core(part_far)))

    targets, part_far = lax.optimization_barrier((targets, part_far))
    mine, velocity_far = call(
        make_message,
        [],
        [inputs] + state[:2] + [targets, state[2]],
        [],
        [],
        [((MESSAGE, WIDTH), B16, False), ((WIDTH, COLS), F32, True)],
    )
    got = swap_core(mine)
    velocity_got = swap_core(velocity_far)

    part2, taught = call(
        second_values,
        [push, push_got, mix],
        state + [targets, velocity_got],
        [],
        [mine, got],
        [((TOKENS, COLS + HALF), B16, True), ((2, BLOCK, COLS), F32, False)],
    )

    spread = ((N_Y, SLAB, COLS), B16, True)
    parts2 = over_y(part2.reshape(N_Y, SLAB, COLS + HALF))
    slab1, own1 = sum_slab(0, over_y(part1.reshape(N_Y, SLAB, COLS)), taught)
    parts2, _ = lax.optimization_barrier((parts2, slab1))
    sent, own1 = call(add_and_spread, [], [], [own1], [slab1, over_z(slab1, 1)], [spread, OWN])
    all1 = over_y(sent).reshape(TOKENS, COLS)

    slab2, own2 = sum_slab(1, parts2, taught)
    near, far, ready = call(
        first_gradient,
        [push, mix],
        state + [velocity_got],
        [],
        [all1, mine, got],
        [
            ((WIDTH + EXTRA, COLS), B16, True),
            ((WIDTH, COLS), B16, True),
            ((2 * WIDTH, COLS), F32, True),
        ],
    )
    slab2_got, _ = lax.optimization_barrier((over_z(slab2, 1), far))
    arrived, arrived_far = to_group(near, 1), to_group_other(far, 1)
    ahead2, gram, own2 = call(
        add_and_part,
        [],
        [],
        [own2],
        [slab2, slab2_got],
        [((SLAB, COLS), B16, False), ((SLAB, HALF), B16, False), OWN],
    )
    gram_got = swap_core(gram)
    sent, own2 = call(
        second_residual,
        [push, push_got, mix],
        [],
        [own2],
        [all1, gram, gram_got, ahead2],
        [spread, OWN],
        [((SLAB, COLS), F32)],
    )
    all2 = over_y(sent).reshape(TOKENS, COLS)
    all2, arrived, arrived_far = lax.optimization_barrier((all2, arrived, arrived_far))

    far, near, half, message = call(
        second_gradient,
        [push, push_got, mix],
        [ready, own1, own2],
        [],
        [mine, got, all2],
        [
            ((WIDTH, COLS), B16, False),
            ((WIDTH + EXTRA, COLS), B16, False),
            ((WIDTH, COLS), F32, False),
            ((WIDTH + 2 * ROWS, COLS), F32, False),
        ],
    )

    sent_far, sent_own = to_group_other(far, 2), to_group(near, 2)
    whole = ((1, WIDTH, VALUES), B16, False)
    number = ((1,), F32, False)
    final_numerator, value_rows, final_weight = call(
        join_numerator,
        [push, push_got, mix],
        [own1, own2, arrived, arrived_far],
        [],
        [half, swap_core(message)],
        [whole, ((2, ROWS, VALUES), B16, False), number],
    )
    sent_far, final_numerator = lax.optimization_barrier((sent_far, final_numerator))
    final_received, got_weight = call(
        join_received, [], [], [], [sent_own, sent_far], [whole, number]
    )
    return final_numerator, final_weight, final_received, got_weight, value_rows


def solution(mesh):
    fine = Mesh(mesh.devices.reshape(SIZES), GROUP + MP)
    placed = (
        P(None, GROUP, MP),
        P(None, GROUP + MP, None),
        P(GROUP, MP, None),
        P(GROUP, MP, None),
        P(GROUP, MP, None),
        P(GROUP),
        P(GROUP),
        P(GROUP, None),
    )
    return jax.shard_map(
        local,
        mesh=fine,
        in_specs=placed,
        out_specs=(
            P(GROUP, MP, None),
            P(GROUP),
            P(GROUP, MP, None),
            P(GROUP),
            P(None, GROUP + MP, None),
        ),
        check_vma=False,
    )
```

```python
import functools
import math

import jax
import jax.numpy as jnp
from jax import lax
from jax.experimental import pallas as pl
from jax.experimental.pallas import tpu as pltpu
from jax.sharding import Mesh
from jax.sharding import PartitionSpec as P

GROUP = ("x", "z_lo")
MP = ("z_hi", "y", "core")
SIZES = (4, 4, 4, 4, 2)
N_Z, N_Y = SIZES[2], SIZES[3]

momentum_decay = 0.9
step_size = 0.5

ROWS = 24
BLOCK = 2 * ROWS
SLAB = N_Z * BLOCK
TOKENS = N_Y * SLAB
WIDTH = 256
VALUES = 1024
COLS = VALUES // 2
HALF = TOKENS // 2
PADDED = 32
EXTRA = 16
ROW_SCALE = 1.0 / math.sqrt(WIDTH * N_Z * N_Y * 2)
GRAD_SCALE = 1.0 / math.sqrt(TOKENS)

X1_AT = TOKENS
W_AT = 2 * TOKENS
REC_AT = W_AT + 2 * WIDTH
M_AT = REC_AT + 2 * WIDTH
T_AT = M_AT + 4 * WIDTH
P_AT = T_AT + 4 * PADDED
MESSAGE = P_AT + 2 * TOKENS

B16, F32 = jnp.bfloat16, jnp.float32


def f32(value):
    return value.astype(jnp.float32)


def bf16(value):
    return value.astype(jnp.bfloat16)


def dot(a, b, dims=((1,), (0,))):
    return lax.dot_general(a, b, (dims, ((), ())), preferred_element_type=jnp.float32)


def cols_of(core):
    return pl.ds(pl.multiple_of(core * COLS, COLS), COLS)


def half_of(core):
    return pl.ds(pl.multiple_of(core * HALF, 16), HALF)


def own_block():
    return pl.ds(pl.multiple_of(lax.axis_index("z_hi") * BLOCK, 16), BLOCK)


def kept(mix, step):
    return mix[0, step].astype(jnp.float32) * 0.125


def by_y():
    return [((zh * N_Y + y) * BLOCK, (y * N_Z + zh) * BLOCK) for zh in range(N_Z) for y in range(N_Y)]


def prepare(push, x, w, rec, velocity, targets, own, message, tokens):
    core = lax.axis_index("core")
    for side in (1 - core, core):
        scaled = bf16(f32(w[:, cols_of(side)]) / push[0])
        part = bf16(dot(x[0], scaled) * ROW_SCALE)
        for at, to in by_y():
            block = part[at : at + BLOCK]
            if side is core:
                own[to : to + BLOCK] = block
            else:
                message[P_AT + to : P_AT + to + BLOCK] = block[:, :WIDTH]
                message[P_AT + TOKENS + to : P_AT + TOKENS + to + BLOCK] = block[:, WIDTH:]
    far = cols_of(1 - core)
    for step in range(2):
        for at, to in by_y():
            row = (1 - step) * TOKENS + to
            message[row : row + BLOCK] = x[step, at : at + BLOCK]
            tokens[row : row + BLOCK] = x[step, at : at + BLOCK]
    old = velocity[:, far]
    high = bf16(old)
    spare = jnp.zeros((PADDED - ROWS, COLS), jnp.float32)
    halves = [(W_AT, w[:, far]), (REC_AT, rec[:, far]), (M_AT, high)]
    halves += [(M_AT + 2 * WIDTH, bf16(old - f32(high)))]
    for step in range(2):
        padded = jnp.concatenate([f32(targets[step, :, far]), spare], axis=0)
        halves.append((T_AT + 2 * step * PADDED, bf16(padded)))
    for row, half in halves:
        rows = half.shape[0]
        message[row : row + rows] = half[:, :WIDTH]
        message[row + rows : row + 2 * rows] = half[:, WIDTH:]


def add_parts(got, own, out):
    for k in range(2):
        part = slice(k * WIDTH, (k + 1) * WIDTH)
        at = P_AT + k * TOKENS
        out[:, part] = bf16(f32(own[:, part]) + f32(got[at : at + TOKENS]))


def tile(mix, w, rec, velocity, got, first, k):
    keep = kept(mix, 0)
    if k == 0:
        side = cols_of(lax.axis_index("core"))
        start, arrived, old = w[:, side], rec[:, side], velocity[:, side]
    else:
        start, arrived, high, low = (
            jnp.concatenate([got[at : at + WIDTH], got[at + WIDTH : at + 2 * WIDTH]], axis=1)
            for at in (W_AT - first, REC_AT - first, M_AT - first, M_AT + 2 * WIDTH - first)
        )
        old = f32(high) + f32(low)
    ahead = f32(start) - (step_size * momentum_decay) * old
    return ahead, keep * ahead + f32(arrived), old


def second_values(push, push_got, mix, w, rec, velocity, targets, mine, got, out, taught):
    core = lax.axis_index("core")
    weight = kept(mix, 0) * push[0] + push_got[0]
    near, far = mine[:TOKENS], got[:TOKENS]
    scaled = [bf16(tile(mix, w, rec, velocity, got, 0, k)[1] / weight) for k in range(2)]
    out[:, :COLS] = bf16((dot(near, scaled[0]) + dot(far, scaled[1])) * ROW_SCALE)
    rows = pl.ds(pl.multiple_of(X1_AT + core * HALF, 16), HALF)
    across = ((1,), (1,))
    out[:, COLS:] = bf16(dot(near, mine[rows], across) + dot(far, got[rows], across))
    for step in range(2):
        own = f32(targets[step, :, cols_of(core)])
        row = T_AT + 2 * step * PADDED
        other = jnp.concatenate(
            [f32(got[row : row + PADDED]), f32(got[row + PADDED : row + 2 * PADDED])], axis=1
        )[:ROWS]
        taught[step, :ROWS] = jnp.where(core == 0, own, other)
        taught[step, ROWS:] = jnp.where(core == 0, other, own)


def sum_over_y(step, parts, taught, slab, own):
    total = f32(parts[0])
    for y in range(1, N_Y):
        total = total + f32(parts[y])
    slab[...] = bf16(total)
    rows = own_block()
    total = f32(parts[0, rows, :COLS])
    for y in range(1, N_Y):
        total = total + f32(parts[y, rows, :COLS])
    own[...] = total
    slab[rows, :COLS] = bf16(total - taught[step])


def add_slab(own, mine, got, out, own_out):
    out[...] = bf16(f32(mine[...]) + f32(got[...]))
    own_out[...] = own[...] + f32(got[own_block(), :COLS])


def add_and_spread(own, mine, got, out, own_out):
    total = bf16(f32(mine[...]) + f32(got[...]))
    for y in range(N_Y):
        out[y] = total
    own_out[...] = own[...] + f32(got[own_block()])


def add_and_part(own, mine, got, out, gram, own_out):
    out[...] = bf16(f32(mine[:, :COLS]) + f32(got[:, :COLS]))
    gram[...] = bf16(f32(mine[:, COLS:]) + f32(got[:, COLS:]))
    own_out[...] = own[...] + f32(got[own_block(), :COLS])


def second_residual(push, push_got, mix, own, all1, gram, gram_got, base, out, own_out, turned):
    core = lax.axis_index("core")
    keep = kept(mix, 0)
    back = step_size * GRAD_SCALE * ROW_SCALE * keep / (keep * push[0] + push_got[0])
    near, far = all1[half_of(core)], all1[half_of(1 - core)]
    turned[...] = (dot(gram[...], near) + dot(gram_got[...], far)) * back
    residual = bf16(f32(base[...]) - turned[...])
    for y in range(N_Y):
        out[y] = residual
    own_out[...] = own[...] - turned[own_block()]


def first_gradient(push, mix, w, rec, velocity, mine, got, all1, near, far, ready):
    keep = kept(mix, 0)
    down = ((0,), (0,))
    for k, x, out in ((0, mine, near), (1, got, far)):
        ahead, base, old = tile(mix, w, rec, velocity, got, X1_AT, k)
        gradient = dot(x[:TOKENS], all1[...], down) * GRAD_SCALE
        out[:WIDTH] = bf16((1.0 - keep) * (ahead - step_size * gradient))
        current = bf16(base - (step_size * keep) * gradient)
        moved = momentum_decay * old + gradient
        ready[k * WIDTH : (k + 1) * WIDTH] = f32(current) - (step_size * momentum_decay) * moved
    near[WIDTH:] = bf16(jnp.full((EXTRA, COLS), (1.0 - keep) * push[0], jnp.float32))


def second_gradient(push, push_got, mix, ready, mine, got, own1, own2, all2, far, near, half, message):
    core = lax.axis_index("core")
    keep = kept(mix, 1)
    down = ((0,), (0,))
    for k, x, out, held in ((1, got, far, message), (0, mine, near, half)):
        gradient = dot(x[...], all2[...], down) * GRAD_SCALE
        moved = ready[k * WIDTH : (k + 1) * WIDTH] - step_size * gradient
        out[:WIDTH] = bf16((1.0 - keep) * moved)
        held[:WIDTH] = keep * moved
    weight = kept(mix, 0) * push[0] + push_got[0]
    near[WIDTH:] = bf16(jnp.full((EXTRA, COLS), (1.0 - keep) * weight, jnp.float32))
    for step, own in ((0, own1), (1, own2)):
        row = WIDTH + step * ROWS
        message[row : row + ROWS] = jnp.where(core == 0, own[ROWS:], own[:ROWS])


def join_numerator(
    push, push_got, mix, arrived, arrived_far, own1, own2, half, message, out, rows_out, weight
):
    core = lax.axis_index("core")
    out[0, :, cols_of(core)] = bf16(half[...] + f32(arrived[:WIDTH]))
    out[0, :, cols_of(1 - core)] = bf16(message[:WIDTH] + f32(arrived_far[...]))
    for step, own in ((0, own1), (1, own2)):
        row = WIDTH + step * ROWS
        rows_out[step, :, cols_of(core)] = bf16(jnp.where(core == 0, own[:ROWS], own[ROWS:]))
        rows_out[step, :, cols_of(1 - core)] = bf16(message[row : row + ROWS])
    last = kept(mix, 0) * push[0] + push_got[0]
    weight[0] = kept(mix, 1) * last + jnp.max(f32(arrived[WIDTH:]))


def join_received(near, far, out, weight):
    core = lax.axis_index("core")
    out[0, :, cols_of(core)] = near[:WIDTH]
    out[0, :, cols_of(1 - core)] = far[...]
    weight[0] = jnp.max(f32(near[WIDTH:]))


SMEM = pl.BlockSpec(memory_space=pltpu.SMEM)
HBM = pl.BlockSpec(memory_space=pltpu.HBM)
VMEM = pl.BlockSpec(memory_space=pltpu.VMEM)


def call(body, scalars, fetched, late, near, outs, scratch=(), flops=0):
    copied = [f if isinstance(f, tuple) else (f, None) for f in list(fetched) + list(late)]
    n, m, first = len(copied), len(fetched), len(scalars)
    last = first + n + len(near)
    far = [k for k, (_, _, memory) in enumerate(outs) if memory is pltpu.HBM]

    def view(ref, where):
        return ref if where is None else ref.at[where]

    def held_shape(value, where):
        if where is None:
            return value.shape
        return value.shape[1:] if isinstance(where, int) else (where.size,) + value.shape[1:]

    def kernel(*refs):
        out = list(refs[last : last + len(outs)])
        rest = list(refs[last + len(outs) :])
        buffers, out_buffers, rest = rest[:n], rest[n : n + len(far)], rest[n + len(far) :]
        sems = rest.pop(0) if n else None
        out_sems = rest.pop(0) if far else None
        copies = [
            pltpu.make_async_copy(view(refs[first + i], copied[i][1]), buffers[i], sems.at[i])
            for i in range(n)
        ]
        for copy in copies:
            copy.start()
        for copy in copies[:m]:
            copy.wait()
        written = list(out)
        for k, buffer in zip(far, out_buffers):
            written[k] = buffer
        later = body(*refs[:first], *buffers, *refs[first + n : last], *written, *rest)
        for copy in copies[m:]:
            copy.wait()
        if late:
            later()
        copies = [
            pltpu.make_async_copy(buffer, out[k], out_sems.at[i])
            for i, (k, buffer) in enumerate(zip(far, out_buffers))
        ]
        for copy in copies:
            copy.start()
        for copy in copies:
            copy.wait()

    buffered = [pltpu.VMEM(held_shape(value, where), value.dtype) for value, where in copied]
    buffered += [pltpu.VMEM(*outs[k][:2]) for k in far]
    buffered += [pltpu.SemaphoreType.DMA((n,))] if n else []
    buffered += [pltpu.SemaphoreType.DMA((len(far),))] if far else []
    result, specs = [], []
    for shape, kind, memory in outs:
        result.append((memory or jax.ShapeDtypeStruct)(shape, kind))
        specs.append(HBM if memory is pltpu.HBM else SMEM if shape == (1,) else VMEM)
    arrays = [pltpu.with_memory_space_constraint(value, pltpu.HBM) for value, _ in copied]
    moved = sum(a.size * a.dtype.itemsize for a in arrays + list(near))
    moved += sum(math.prod(shape) * jnp.dtype(kind).itemsize for shape, kind, _ in outs)
    return pl.pallas_call(
        kernel,
        out_shape=result,
        in_specs=[SMEM] * first + [HBM] * n + [VMEM] * len(near),
        out_specs=specs,
        scratch_shapes=buffered + [pltpu.VMEM(size, kind) for size, kind in scratch],
        compiler_params=pltpu.CompilerParams(vmem_limit_bytes=20 * 2**20),
        cost_estimate=pl.CostEstimate(flops=flops, bytes_accessed=moved, transcendentals=0),
        name=body.func.__name__ if isinstance(body, functools.partial) else body.__name__,
    )(*scalars, *arrays, *near)


def held(value):
    return pltpu.with_memory_space_constraint(value, pltpu.VMEM)


def z_pairs(step):
    pairs = []
    for zh in range(N_Z):
        for core in range(2):
            turn = (1, 3)[step ^ core]
            pairs.append((zh * 2 + core, (zh ^ turn) * 2 + core))
    return pairs


def over_z(value, step):
    return lax.ppermute(value, ("z_hi", "core"), z_pairs(step))


def over_y(value):
    return lax.all_to_all(value, "y", 0, 0, tiled=True)


def swap_core(value):
    return lax.ppermute(value, "core", [(0, 1), (1, 0)])


def to_group(value, hop):
    count = SIZES[0] * SIZES[1]
    return lax.ppermute(value, GROUP, [(i, (i + hop) % count) for i in range(count)])


def to_group_other(value, hop):
    count = SIZES[0] * SIZES[1]
    pairs = [(i * 2 + c, (i + hop) % count * 2 + 1 - c) for i in range(count) for c in range(2)]
    return lax.ppermute(value, GROUP + ("core",), pairs)


OWN = ((BLOCK, COLS), F32, pltpu.VMEM)


def sum_slab(step, parts, taught):
    whole = ((SLAB, parts.shape[2]), B16, pltpu.VMEM)
    slab, own = call(
        functools.partial(sum_over_y, step), [], [], [], [held(parts), held(taught)], [whole, OWN]
    )
    near = [held(own), held(slab), held(over_z(slab, 0))]
    return call(add_slab, [], [], [], near, [whole, OWN])


def local(inputs, targets, numerator, momentum, received, push_weight, received_weight, mix_share):
    push, push_got, mix = push_weight, received_weight, mix_share
    state = [(numerator, 0), (received, 0), (momentum, 0)]

    part_own, message, mine = call(
        prepare,
        [push],
        [inputs] + state + [targets],
        [],
        [],
        [
            ((TOKENS, COLS), B16, pltpu.VMEM),
            ((MESSAGE, WIDTH), B16, pltpu.VMEM),
            ((2 * TOKENS, WIDTH), B16, pltpu.HBM),
        ],
    )
    got = swap_core(message)
    (part1,) = call(
        add_parts,
        [],
        [],
        [],
        [got, held(part_own)],
        [((TOKENS, COLS), B16, pltpu.HBM)],
    )
    targets, part1 = lax.optimization_barrier((targets, part1))

    part2, taught = call(
        second_values,
        [push, push_got, mix],
        state + [targets, mine, (got, pl.ds(0, P_AT))],
        [],
        [],
        [((TOKENS, COLS + HALF), B16, pltpu.HBM), ((2, BLOCK, COLS), F32, pltpu.VMEM)],
    )

    spread = ((N_Y, SLAB, COLS), B16, pltpu.HBM)
    parts2 = over_y(part2.reshape(N_Y, SLAB, COLS + HALF))
    slab1, own1 = sum_slab(0, over_y(part1.reshape(N_Y, SLAB, COLS)), taught)
    parts2, _ = lax.optimization_barrier((parts2, slab1))
    near = [held(own1), held(slab1), held(over_z(slab1, 1))]
    sent, own1 = call(add_and_spread, [], [], [], near, [spread, OWN])
    all1 = over_y(sent).reshape(TOKENS, COLS)

    slab2, own2 = sum_slab(1, parts2, taught)
    near, far, ready = call(
        first_gradient,
        [push, mix],
        state + [(mine, pl.ds(X1_AT, TOKENS)), (got, pl.ds(X1_AT, T_AT - X1_AT))],
        [],
        [all1],
        [
            ((WIDTH + EXTRA, COLS), B16, pltpu.HBM),
            ((WIDTH, COLS), B16, pltpu.HBM),
            ((2 * WIDTH, COLS), F32, pltpu.HBM),
        ],
    )
    slab2_got, _ = lax.optimization_barrier((over_z(slab2, 1), far))
    arrived, arrived_far = to_group(near, 1), to_group_other(far, 1)
    ahead2, gram, own2 = call(
        add_and_part,
        [],
        [],
        [],
        [held(own2), held(slab2), held(slab2_got)],
        [((SLAB, COLS), B16, pltpu.VMEM), ((SLAB, HALF), B16, pltpu.VMEM), OWN],
    )
    gram_got = held(swap_core(gram))
    gram_got, arrived, arrived_far = lax.optimization_barrier((gram_got, arrived, arrived_far))
    sent, own2 = call(
        second_residual,
        [push, push_got, mix],
        [],
        [],
        [held(own2), all1, held(gram), held(gram_got), held(ahead2)],
        [spread, OWN],
        [((SLAB, COLS), F32)],
    )
    all2 = over_y(sent).reshape(TOKENS, COLS)

    far, near, half, message = call(
        second_gradient,
        [push, push_got, mix],
        [ready, (mine, pl.ds(0, TOKENS)), (got, pl.ds(0, TOKENS))],
        [],
        [held(own1), held(own2), all2],
        [
            ((WIDTH, COLS), B16, None),
            ((WIDTH + EXTRA, COLS), B16, None),
            ((WIDTH, COLS), F32, None),
            ((WIDTH + 2 * ROWS, COLS), F32, None),
        ],
    )

    sent_far, sent_own = to_group_other(far, 2), to_group(near, 2)
    whole = ((1, WIDTH, VALUES), B16, None)
    number = ((1,), F32, None)
    final_numerator, value_rows, final_weight = call(
        join_numerator,
        [push, push_got, mix],
        [],
        [],
        [held(arrived), held(arrived_far), held(own1), held(own2), half, swap_core(message)],
        [whole, ((2, ROWS, VALUES), B16, None), number],
    )
    sent_far, final_numerator = lax.optimization_barrier((sent_far, final_numerator))
    final_received, got_weight = call(
        join_received, [], [], [], [sent_own, sent_far], [whole, number]
    )
    return final_numerator, final_weight, final_received, got_weight, value_rows


def solution(mesh):
    fine = Mesh(mesh.devices.reshape(SIZES), GROUP + MP)
    placed = (
        P(None, GROUP, MP),
        P(None, GROUP + MP, None),
        P(GROUP, MP, None),
        P(GROUP, MP, None),
        P(GROUP, MP, None),
        P(GROUP),
        P(GROUP),
        P(GROUP, None),
    )
    return jax.shard_map(
        local,
        mesh=fine,
        in_specs=placed,
        out_specs=(
            P(GROUP, MP, None),
            P(GROUP),
            P(GROUP, MP, None),
            P(GROUP),
            P(None, GROUP + MP, None),
        ),
        check_vma=False,
    )
```

```python
import functools
import math

import jax
import jax.numpy as jnp
from jax import lax
from jax.experimental import pallas as pl
from jax.experimental.pallas import tpu as pltpu
from jax.sharding import Mesh
from jax.sharding import PartitionSpec as P

GROUP = ("x", "z_lo")
MP = ("z_hi", "y", "core")
SIZES = (4, 4, 4, 4, 2)
N_Z, N_Y = SIZES[2], SIZES[3]

momentum_decay = 0.9
step_size = 0.5

ROWS = 24
BLOCK = 2 * ROWS
SLAB = N_Z * BLOCK
TOKENS = N_Y * SLAB
WIDTH = 256
VALUES = 1024
COLS = VALUES // 2
HALF = TOKENS // 2
PADDED = 32
EXTRA = 16
ROW_SCALE = 1.0 / math.sqrt(WIDTH * N_Z * N_Y * 2)
GRAD_SCALE = 1.0 / math.sqrt(TOKENS)

X1_AT = TOKENS
W_AT = 2 * TOKENS
REC_AT = W_AT + 2 * WIDTH
M_AT = REC_AT + 2 * WIDTH
T_AT = M_AT + 4 * WIDTH
MESSAGE = T_AT + 4 * PADDED

B16, F32 = jnp.bfloat16, jnp.float32


def f32(value):
    return value.astype(jnp.float32)


def bf16(value):
    return value.astype(jnp.bfloat16)


def dot(a, b, dims=((1,), (0,))):
    return lax.dot_general(a, b, (dims, ((), ())), preferred_element_type=jnp.float32)


def cols_of(core):
    return pl.ds(pl.multiple_of(core * COLS, COLS), COLS)


def half_of(core):
    return pl.ds(pl.multiple_of(core * HALF, 16), HALF)


def own_block():
    return pl.ds(pl.multiple_of(lax.axis_index("z_hi") * BLOCK, 16), BLOCK)


def kept(mix, step):
    return mix[0, step].astype(jnp.float32) * 0.125


def by_y():
    return [((zh * N_Y + y) * BLOCK, (y * N_Z + zh) * BLOCK) for zh in range(N_Z) for y in range(N_Y)]


def first_values(push, x, w, far, own):
    core = lax.axis_index("core")
    for out, side in ((far, 1 - core), (own, core)):
        scaled = bf16(f32(w[:, cols_of(side)]) / push[0])
        part = bf16(dot(x[...], scaled) * ROW_SCALE)
        for at, to in by_y():
            out[to : to + BLOCK] = part[at : at + BLOCK]


def make_message(x, w, rec, velocity, targets, message, tokens):
    far = cols_of(1 - lax.axis_index("core"))
    for step in range(2):
        for at, to in by_y():
            row = (1 - step) * TOKENS + to
            message[row : row + BLOCK] = x[step, at : at + BLOCK]
            tokens[row : row + BLOCK] = x[step, at : at + BLOCK]
    old = velocity[:, far]
    high = bf16(old)
    spare = jnp.zeros((PADDED - ROWS, COLS), jnp.float32)
    halves = [(W_AT, w[:, far]), (REC_AT, rec[:, far]), (M_AT, high)]
    halves += [(M_AT + 2 * WIDTH, bf16(old - f32(high)))]
    for step in range(2):
        padded = jnp.concatenate([f32(targets[step, :, far]), spare], axis=0)
        halves.append((T_AT + 2 * step * PADDED, bf16(padded)))
    for row, half in halves:
        rows = half.shape[0]
        message[row : row + rows] = half[:, :WIDTH]
        message[row + rows : row + 2 * rows] = half[:, WIDTH:]


def add_parts(own, got, out):
    out[...] = bf16(f32(own[...]) + f32(got[...]))


def tile(mix, w, rec, velocity, got, first, k):
    keep = kept(mix, 0)
    if k == 0:
        side = cols_of(lax.axis_index("core"))
        start, arrived, old = w[:, side], rec[:, side], velocity[:, side]
    else:
        start, arrived, high, low = (
            jnp.concatenate([got[at : at + WIDTH], got[at + WIDTH : at + 2 * WIDTH]], axis=1)
            for at in (W_AT - first, REC_AT - first, M_AT - first, M_AT + 2 * WIDTH - first)
        )
        old = f32(high) + f32(low)
    ahead = f32(start) - (step_size * momentum_decay) * old
    return ahead, keep * ahead + f32(arrived), old


def second_values(push, push_got, mix, w, rec, velocity, mine, got, out):
    core = lax.axis_index("core")
    weight = kept(mix, 0) * push[0] + push_got[0]
    near, far = mine[:TOKENS], got[:TOKENS]
    scaled = [bf16(tile(mix, w, rec, velocity, got, 0, k)[1] / weight) for k in range(2)]
    out[:, :COLS] = bf16((dot(near, scaled[0]) + dot(far, scaled[1])) * ROW_SCALE)
    rows = pl.ds(pl.multiple_of(X1_AT + core * HALF, 16), HALF)
    across = ((1,), (1,))
    out[:, COLS:] = bf16(dot(near, mine[rows], across) + dot(far, got[rows], across))


def sum_over_y(step, targets, targets_got, parts, slab, own, *gram):
    core = lax.axis_index("core")
    total = f32(parts[0])
    for y in range(1, N_Y):
        total = total + f32(parts[y])
    slab[...] = bf16(total[:, :COLS])
    if gram:
        gram[0][...] = bf16(total[:, COLS:])
    rows = own_block()
    total = f32(parts[0, rows, :COLS])
    for y in range(1, N_Y):
        total = total + f32(parts[y, rows, :COLS])
    own[...] = total
    near = f32(targets[step, :, cols_of(core)])
    row = 2 * step * PADDED
    far = jnp.concatenate(
        [f32(targets_got[row : row + PADDED]), f32(targets_got[row + PADDED : row + 2 * PADDED])],
        axis=1,
    )[:ROWS]
    low, high = jnp.where(core == 0, near, far), jnp.where(core == 0, far, near)
    slab[rows] = bf16(total - jnp.concatenate([low, high], axis=0))


def add_slab(own, mine, got, out, own_out):
    out[...] = bf16(f32(mine[...]) + f32(got[...]))
    own_out[...] = own[...] + f32(got[own_block()])


def add_and_spread(own, mine, got, out, own_out):
    total = bf16(f32(mine[...]) + f32(got[...]))
    for y in range(N_Y):
        out[y] = total
    own_out[...] = own[...] + f32(got[own_block()])


def second_residual(push, push_got, mix, own, all1, gram, gram_got, base, out, own_out, turned):
    core = lax.axis_index("core")
    keep = kept(mix, 0)
    back = step_size * GRAD_SCALE * ROW_SCALE * keep / (keep * push[0] + push_got[0])
    near, far = all1[half_of(core)], all1[half_of(1 - core)]
    turned[...] = (dot(gram[...], near) + dot(gram_got[...], far)) * back
    out[...] = bf16(f32(base[...]) - turned[...])
    own_out[...] = own[...] - turned[own_block()]


def first_gradient(push, mix, w, rec, velocity, mine, got, all1, near, far, ready):
    keep = kept(mix, 0)
    down = ((0,), (0,))
    for k, x, out in ((0, mine, near), (1, got, far)):
        ahead, base, old = tile(mix, w, rec, velocity, got, X1_AT, k)
        gradient = dot(x[:TOKENS], all1[...], down) * GRAD_SCALE
        out[:WIDTH] = bf16((1.0 - keep) * (ahead - step_size * gradient))
        current = bf16(base - (step_size * keep) * gradient)
        moved = momentum_decay * old + gradient
        ready[k * WIDTH : (k + 1) * WIDTH] = f32(current) - (step_size * momentum_decay) * moved
    near[WIDTH:] = bf16(jnp.full((EXTRA, COLS), (1.0 - keep) * push[0], jnp.float32))


def second_gradient(push, push_got, mix, ready, mine, got, own1, own2, all2, far, near, half, message):
    core = lax.axis_index("core")
    keep = kept(mix, 1)
    down = ((0,), (0,))
    for k, x, out, held in ((1, got, far, message), (0, mine, near, half)):
        gradient = dot(x[...], all2[...], down) * GRAD_SCALE
        moved = ready[k * WIDTH : (k + 1) * WIDTH] - step_size * gradient
        out[:WIDTH] = bf16((1.0 - keep) * moved)
        held[:WIDTH] = keep * moved
    weight = kept(mix, 0) * push[0] + push_got[0]
    near[WIDTH:] = bf16(jnp.full((EXTRA, COLS), (1.0 - keep) * weight, jnp.float32))
    for step, own in ((0, own1), (1, own2)):
        row = WIDTH + step * ROWS
        message[row : row + ROWS] = jnp.where(core == 0, own[ROWS:], own[:ROWS])


def join_numerator(
    push, push_got, mix, arrived, arrived_far, own1, own2, half, message, out, rows_out, weight
):
    core = lax.axis_index("core")
    out[0, :, cols_of(core)] = bf16(half[...] + f32(arrived[:WIDTH]))
    out[0, :, cols_of(1 - core)] = bf16(message[:WIDTH] + f32(arrived_far[...]))
    for step, own in ((0, own1), (1, own2)):
        row = WIDTH + step * ROWS
        rows_out[step, :, cols_of(core)] = bf16(jnp.where(core == 0, own[:ROWS], own[ROWS:]))
        rows_out[step, :, cols_of(1 - core)] = bf16(message[row : row + ROWS])
    last = kept(mix, 0) * push[0] + push_got[0]
    weight[0] = kept(mix, 1) * last + jnp.max(f32(arrived[WIDTH:]))


def join_received(near, far, out, weight):
    core = lax.axis_index("core")
    out[0, :, cols_of(core)] = near[:WIDTH]
    out[0, :, cols_of(1 - core)] = far[...]
    weight[0] = jnp.max(f32(near[WIDTH:]))


SMEM = pl.BlockSpec(memory_space=pltpu.SMEM)
HBM = pl.BlockSpec(memory_space=pltpu.HBM)
VMEM = pl.BlockSpec(memory_space=pltpu.VMEM)


def call(body, scalars, fetched, late, near, outs, scratch=(), flops=0):
    copied = [f if isinstance(f, tuple) else (f, None) for f in list(fetched) + list(late)]
    n, m, first = len(copied), len(fetched), len(scalars)
    last = first + n + len(near)
    far = [k for k, (_, _, memory) in enumerate(outs) if memory is pltpu.HBM]

    def view(ref, where):
        return ref if where is None else ref.at[where]

    def held_shape(value, where):
        if where is None:
            return value.shape
        return value.shape[1:] if isinstance(where, int) else (where.size,) + value.shape[1:]

    def kernel(*refs):
        out = list(refs[last : last + len(outs)])
        rest = list(refs[last + len(outs) :])
        buffers, out_buffers, rest = rest[:n], rest[n : n + len(far)], rest[n + len(far) :]
        sems = rest.pop(0) if n else None
        out_sems = rest.pop(0) if far else None
        copies = [
            pltpu.make_async_copy(view(refs[first + i], copied[i][1]), buffers[i], sems.at[i])
            for i in range(n)
        ]
        for copy in copies:
            copy.start()
        for copy in copies[:m]:
            copy.wait()
        written = list(out)
        for k, buffer in zip(far, out_buffers):
            written[k] = buffer
        later = body(*refs[:first], *buffers, *refs[first + n : last], *written, *rest)
        for copy in copies[m:]:
            copy.wait()
        if late:
            later()
        copies = [
            pltpu.make_async_copy(buffer, out[k], out_sems.at[i])
            for i, (k, buffer) in enumerate(zip(far, out_buffers))
        ]
        for copy in copies:
            copy.start()
        for copy in copies:
            copy.wait()

    buffered = [pltpu.VMEM(held_shape(value, where), value.dtype) for value, where in copied]
    buffered += [pltpu.VMEM(*outs[k][:2]) for k in far]
    buffered += [pltpu.SemaphoreType.DMA((n,))] if n else []
    buffered += [pltpu.SemaphoreType.DMA((len(far),))] if far else []
    result, specs = [], []
    for shape, kind, memory in outs:
        result.append((memory or jax.ShapeDtypeStruct)(shape, kind))
        specs.append(HBM if memory is pltpu.HBM else SMEM if shape == (1,) else VMEM)
    arrays = [pltpu.with_memory_space_constraint(value, pltpu.HBM) for value, _ in copied]
    moved = sum(a.size * a.dtype.itemsize for a in arrays + list(near))
    moved += sum(math.prod(shape) * jnp.dtype(kind).itemsize for shape, kind, _ in outs)
    return pl.pallas_call(
        kernel,
        out_shape=result,
        in_specs=[SMEM] * first + [HBM] * n + [VMEM] * len(near),
        out_specs=specs,
        scratch_shapes=buffered + [pltpu.VMEM(size, kind) for size, kind in scratch],
        compiler_params=pltpu.CompilerParams(vmem_limit_bytes=20 * 2**20),
        cost_estimate=pl.CostEstimate(flops=flops, bytes_accessed=moved, transcendentals=0),
        name=body.func.__name__ if isinstance(body, functools.partial) else body.__name__,
    )(*scalars, *arrays, *near)


def held(value):
    return pltpu.with_memory_space_constraint(value, pltpu.VMEM)


def z_pairs(step):
    pairs = []
    for zh in range(N_Z):
        for core in range(2):
            turn = (1, 3)[step ^ core]
            pairs.append((zh * 2 + core, (zh ^ turn) * 2 + core))
    return pairs


def over_z(value, step):
    return lax.ppermute(value, ("z_hi", "core"), z_pairs(step))


def over_y(value):
    return lax.all_to_all(value, "y", 0, 0, tiled=True)


def swap_core(value):
    return lax.ppermute(value, "core", [(0, 1), (1, 0)])


def to_group(value, hop):
    count = SIZES[0] * SIZES[1]
    return lax.ppermute(value, GROUP, [(i, (i + hop) % count) for i in range(count)])


def to_group_other(value, hop):
    count = SIZES[0] * SIZES[1]
    pairs = [(i * 2 + c, (i + hop) % count * 2 + 1 - c) for i in range(count) for c in range(2)]
    return lax.ppermute(value, GROUP + ("core",), pairs)


OWN = ((BLOCK, COLS), F32, pltpu.VMEM)


WHOLE = ((SLAB, COLS), B16, pltpu.VMEM)
SPREAD = ((N_Y, SLAB, COLS), B16, pltpu.HBM)


def add_z(slab, own, step, body, out, before=None):
    got = over_z(slab, step)
    if before is not None:
        got, _ = lax.optimization_barrier((got, before))
    return call(body, [], [], [], [held(own), held(slab), held(got)], [out, OWN])


def local(inputs, targets, numerator, momentum, received, push_weight, received_weight, mix_share):
    push, push_got, mix = push_weight, received_weight, mix_share
    state = [(numerator, 0), (received, 0), (momentum, 0)]

    part = ((TOKENS, COLS), B16, pltpu.VMEM)
    part_far, part_own = call(
        first_values, [push], [(inputs, 0), (numerator, 0)], [], [], [part, part]
    )
    near = [held(part_own), held(swap_core(part_far))]
    (part1,) = call(add_parts, [], [], [], near, [((TOKENS, COLS), B16, pltpu.HBM)])

    later, _ = lax.optimization_barrier((targets, part_own))
    message, mine = call(
        make_message,
        [],
        [inputs] + state + [later],
        [],
        [],
        [((MESSAGE, WIDTH), B16, pltpu.VMEM), ((2 * TOKENS, WIDTH), B16, pltpu.HBM)],
    )
    got = swap_core(message)
    taught = [later, (got, pl.ds(T_AT, 4 * PADDED))]

    parts1 = over_y(part1.reshape(N_Y, SLAB, COLS))
    slab, own1 = call(
        functools.partial(sum_over_y, 0), [], taught, [], [held(parts1)], [WHOLE, OWN]
    )

    mine, _ = lax.optimization_barrier((mine, slab))
    (part2,) = call(
        second_values,
        [push, push_got, mix],
        state + [mine, (got, pl.ds(0, T_AT))],
        [],
        [],
        [((TOKENS, COLS + HALF), B16, pltpu.HBM)],
    )
    slab, own1 = add_z(slab, own1, 0, add_slab, WHOLE, part2)
    part2, _ = lax.optimization_barrier((part2, slab))
    parts2 = over_y(part2.reshape(N_Y, SLAB, COLS + HALF))
    sent, own1 = add_z(slab, own1, 1, add_and_spread, SPREAD)
    all1 = over_y(sent).reshape(TOKENS, COLS)

    parts2, _ = lax.optimization_barrier((parts2, sent))
    base, own2, gram = call(
        functools.partial(sum_over_y, 1),
        [],
        taught,
        [],
        [held(parts2)],
        [WHOLE, OWN, ((SLAB, HALF), B16, pltpu.VMEM)],
    )
    near = [held(own2), all1, held(gram), held(swap_core(gram)), held(base)]
    slab, own2 = call(
        second_residual, [push, push_got, mix], [], [], near, [WHOLE, OWN], [((SLAB, COLS), F32)]
    )
    near, far, ready = call(
        first_gradient,
        [push, mix],
        state + [(mine, pl.ds(X1_AT, TOKENS)), (got, pl.ds(X1_AT, T_AT - X1_AT))],
        [],
        [all1],
        [
            ((WIDTH + EXTRA, COLS), B16, pltpu.VMEM),
            ((WIDTH, COLS), B16, pltpu.VMEM),
            ((2 * WIDTH, COLS), F32, pltpu.HBM),
        ],
    )
    slab, own2 = add_z(slab, own2, 0, add_slab, WHOLE, far)
    sent, own2 = add_z(slab, own2, 1, add_and_spread, SPREAD)
    all2 = over_y(sent).reshape(TOKENS, COLS)
    near, far, _ = lax.optimization_barrier((near, far, sent))
    arrived, arrived_far = to_group(near, 1), to_group_other(far, 1)
    all2, arrived, arrived_far = lax.optimization_barrier((all2, arrived, arrived_far))

    far, near, half, message = call(
        second_gradient,
        [push, push_got, mix],
        [ready, (mine, pl.ds(0, TOKENS)), (got, pl.ds(0, TOKENS))],
        [],
        [held(own1), held(own2), all2],
        [
            ((WIDTH, COLS), B16, None),
            ((WIDTH + EXTRA, COLS), B16, None),
            ((WIDTH, COLS), F32, None),
            ((WIDTH + 2 * ROWS, COLS), F32, None),
        ],
    )

    sent_far, sent_own = to_group_other(far, 2), to_group(near, 2)
    whole = ((1, WIDTH, VALUES), B16, None)
    number = ((1,), F32, None)
    final_numerator, value_rows, final_weight = call(
        join_numerator,
        [push, push_got, mix],
        [],
        [],
        [held(arrived), held(arrived_far), held(own1), held(own2), half, swap_core(message)],
        [whole, ((2, ROWS, VALUES), B16, None), number],
    )
    sent_far, final_numerator = lax.optimization_barrier((sent_far, final_numerator))
    final_received, got_weight = call(
        join_received, [], [], [], [sent_own, sent_far], [whole, number]
    )
    return final_numerator, final_weight, final_received, got_weight, value_rows


def solution(mesh):
    fine = Mesh(mesh.devices.reshape(SIZES), GROUP + MP)
    placed = (
        P(None, GROUP, MP),
        P(None, GROUP + MP, None),
        P(GROUP, MP, None),
        P(GROUP, MP, None),
        P(GROUP, MP, None),
        P(GROUP),
        P(GROUP),
        P(GROUP, None),
    )
    return jax.shard_map(
        local,
        mesh=fine,
        in_specs=placed,
        out_specs=(
            P(GROUP, MP, None),
            P(GROUP),
            P(GROUP, MP, None),
            P(GROUP),
            P(None, GROUP + MP, None),
        ),
        check_vma=False,
    )
```

```python
import functools
import math

import jax
import jax.numpy as jnp
from jax import lax
from jax.experimental import pallas as pl
from jax.experimental.pallas import tpu as pltpu
from jax.sharding import Mesh
from jax.sharding import PartitionSpec as P

GROUP = ("x", "z_lo")
MP = ("z_hi", "y", "core")
SIZES = (4, 4, 4, 4, 2)
N_Z, N_Y = SIZES[2], SIZES[3]

momentum_decay = 0.9
step_size = 0.5

ROWS = 24
BLOCK = 2 * ROWS
SLAB = N_Z * BLOCK
TOKENS = N_Y * SLAB
WIDTH = 256
VALUES = 1024
COLS = VALUES // 2
HALF = TOKENS // 2
PADDED = 32
EXTRA = 16
ROW_SCALE = 1.0 / math.sqrt(WIDTH * N_Z * N_Y * 2)
GRAD_SCALE = 1.0 / math.sqrt(TOKENS)

X1_AT = TOKENS
W_AT = 2 * TOKENS
REC_AT = W_AT + 2 * WIDTH
M_AT = REC_AT + 2 * WIDTH
MESSAGE = M_AT + 4 * WIDTH

B16, F32 = jnp.bfloat16, jnp.float32


def f32(value):
    return value.astype(jnp.float32)


def bf16(value):
    return value.astype(jnp.bfloat16)


def dot(a, b, dims=((1,), (0,))):
    return lax.dot_general(a, b, (dims, ((), ())), preferred_element_type=jnp.float32)


def cols_of(core):
    return pl.ds(pl.multiple_of(core * COLS, COLS), COLS)


def half_of(core):
    return pl.ds(pl.multiple_of(core * HALF, 16), HALF)


def own_block():
    return pl.ds(pl.multiple_of(lax.axis_index("z_hi") * BLOCK, 16), BLOCK)


def kept(mix, step):
    return mix[0, step].astype(jnp.float32) * 0.125


def by_y():
    return [((zh * N_Y + y) * BLOCK, (y * N_Z + zh) * BLOCK) for zh in range(N_Z) for y in range(N_Y)]


def first_values(push, x, w, targets, far, own):
    core = lax.axis_index("core")
    for out, side in ((far, 1 - core), (own, core)):
        scaled = bf16(f32(w[:, cols_of(side)]) / push[0])
        part = bf16(dot(x[...], scaled) * ROW_SCALE)
        for at, to in by_y():
            out[to : to + BLOCK] = part[at : at + BLOCK]
    spare = jnp.zeros((PADDED - ROWS, COLS), jnp.float32)
    for step in range(2):
        row = TOKENS + step * PADDED
        half = jnp.concatenate([f32(targets[step, :, cols_of(1 - core)]), spare], axis=0)
        far[row : row + PADDED] = bf16(half)


def make_message(x, w, rec, velocity, message, tokens):
    far = cols_of(1 - lax.axis_index("core"))
    for step in range(2):
        for at, to in by_y():
            row = (1 - step) * TOKENS + to
            message[row : row + BLOCK] = x[step, at : at + BLOCK]
            tokens[row : row + BLOCK] = x[step, at : at + BLOCK]
    old = velocity[:, far]
    high = bf16(old)
    halves = [(W_AT, w[:, far]), (REC_AT, rec[:, far]), (M_AT, high)]
    halves += [(M_AT + 2 * WIDTH, bf16(old - f32(high)))]
    for row, half in halves:
        message[row : row + WIDTH] = half[:, :WIDTH]
        message[row + WIDTH : row + 2 * WIDTH] = half[:, WIDTH:]


def add_parts(own, got, out):
    out[...] = bf16(f32(own[...]) + f32(got[:TOKENS]))


def tile(mix, w, rec, velocity, got, first, k):
    keep = kept(mix, 0)
    if k == 0:
        side = cols_of(lax.axis_index("core"))
        start, arrived, old = w[:, side], rec[:, side], velocity[:, side]
    else:
        start, arrived, high, low = (
            jnp.concatenate([got[at : at + WIDTH], got[at + WIDTH : at + 2 * WIDTH]], axis=1)
            for at in (W_AT - first, REC_AT - first, M_AT - first, M_AT + 2 * WIDTH - first)
        )
        old = f32(high) + f32(low)
    ahead = f32(start) - (step_size * momentum_decay) * old
    return ahead, keep * ahead + f32(arrived), old


def second_values(push, push_got, mix, w, rec, velocity, mine, got, out):
    core = lax.axis_index("core")
    weight = kept(mix, 0) * push[0] + push_got[0]
    near, far = mine[:TOKENS], got[:TOKENS]
    scaled = [bf16(tile(mix, w, rec, velocity, got, 0, k)[1] / weight) for k in range(2)]
    out[:, :COLS] = bf16((dot(near, scaled[0]) + dot(far, scaled[1])) * ROW_SCALE)
    rows = pl.ds(pl.multiple_of(X1_AT + core * HALF, 16), HALF)
    across = ((1,), (1,))
    out[:, COLS:] = bf16(dot(near, mine[rows], across) + dot(far, got[rows], across))


def sum_over_y(step, targets, targets_got, parts, slab, own, *gram):
    core = lax.axis_index("core")
    total = f32(parts[0])
    for y in range(1, N_Y):
        total = total + f32(parts[y])
    slab[...] = bf16(total[:, :COLS])
    if gram:
        gram[0][...] = bf16(total[:, COLS:])
    rows = own_block()
    total = f32(parts[0, rows, :COLS])
    for y in range(1, N_Y):
        total = total + f32(parts[y, rows, :COLS])
    own[...] = total
    near = f32(targets[step, :, cols_of(core)])
    far = f32(targets_got[step * PADDED : (step + 1) * PADDED])[:ROWS]
    low, high = jnp.where(core == 0, near, far), jnp.where(core == 0, far, near)
    slab[rows] = bf16(total - jnp.concatenate([low, high], axis=0))


def add_slab(own, mine, got, out, own_out):
    out[...] = bf16(f32(mine[...]) + f32(got[...]))
    own_out[...] = own[...] + f32(got[own_block()])


def add_and_spread(own, mine, got, out, own_out):
    total = bf16(f32(mine[...]) + f32(got[...]))
    for y in range(N_Y):
        out[y] = total
    own_out[...] = own[...] + f32(got[own_block()])


def second_residual(push, push_got, mix, own, all1, gram, gram_got, base, out, own_out, turned):
    core = lax.axis_index("core")
    keep = kept(mix, 0)
    back = step_size * GRAD_SCALE * ROW_SCALE * keep / (keep * push[0] + push_got[0])
    near, far = all1[half_of(core)], all1[half_of(1 - core)]
    turned[...] = (dot(gram[...], near) + dot(gram_got[...], far)) * back
    out[...] = bf16(f32(base[...]) - turned[...])
    own_out[...] = own[...] - turned[own_block()]


def first_gradient(push, mix, w, rec, velocity, mine, got, all1, near, far, ready):
    keep = kept(mix, 0)
    down = ((0,), (0,))
    for k, x, out in ((0, mine, near), (1, got, far)):
        ahead, base, old = tile(mix, w, rec, velocity, got, X1_AT, k)
        gradient = dot(x[:TOKENS], all1[...], down) * GRAD_SCALE
        out[:WIDTH] = bf16((1.0 - keep) * (ahead - step_size * gradient))
        current = bf16(base - (step_size * keep) * gradient)
        moved = momentum_decay * old + gradient
        ready[k * WIDTH : (k + 1) * WIDTH] = f32(current) - (step_size * momentum_decay) * moved
    near[WIDTH:] = bf16(jnp.full((EXTRA, COLS), (1.0 - keep) * push[0], jnp.float32))


def second_gradient(push, push_got, mix, ready, mine, got, own1, own2, all2, far, near, half, message):
    core = lax.axis_index("core")
    keep = kept(mix, 1)
    down = ((0,), (0,))
    for k, x, out, held in ((1, got, far, message), (0, mine, near, half)):
        gradient = dot(x[...], all2[...], down) * GRAD_SCALE
        moved = ready[k * WIDTH : (k + 1) * WIDTH] - step_size * gradient
        out[:WIDTH] = bf16((1.0 - keep) * moved)
        held[:WIDTH] = keep * moved
    weight = kept(mix, 0) * push[0] + push_got[0]
    near[WIDTH:] = bf16(jnp.full((EXTRA, COLS), (1.0 - keep) * weight, jnp.float32))
    for step, own in ((0, own1), (1, own2)):
        row = WIDTH + step * ROWS
        message[row : row + ROWS] = jnp.where(core == 0, own[ROWS:], own[:ROWS])


def join_numerator(
    push, push_got, mix, arrived, arrived_far, own1, own2, half, message, out, rows_out, weight
):
    core = lax.axis_index("core")
    out[0, :, cols_of(core)] = bf16(half[...] + f32(arrived[:WIDTH]))
    out[0, :, cols_of(1 - core)] = bf16(message[:WIDTH] + f32(arrived_far[...]))
    for step, own in ((0, own1), (1, own2)):
        row = WIDTH + step * ROWS
        rows_out[step, :, cols_of(core)] = bf16(jnp.where(core == 0, own[:ROWS], own[ROWS:]))
        rows_out[step, :, cols_of(1 - core)] = bf16(message[row : row + ROWS])
    last = kept(mix, 0) * push[0] + push_got[0]
    weight[0] = kept(mix, 1) * last + jnp.max(f32(arrived[WIDTH:]))


def join_received(near, far, out, weight):
    core = lax.axis_index("core")
    out[0, :, cols_of(core)] = near[:WIDTH]
    out[0, :, cols_of(1 - core)] = far[...]
    weight[0] = jnp.max(f32(near[WIDTH:]))


SMEM = pl.BlockSpec(memory_space=pltpu.SMEM)
HBM = pl.BlockSpec(memory_space=pltpu.HBM)
VMEM = pl.BlockSpec(memory_space=pltpu.VMEM)


def call(body, scalars, fetched, late, near, outs, scratch=(), flops=0):
    copied = [f if isinstance(f, tuple) else (f, None) for f in list(fetched) + list(late)]
    n, m, first = len(copied), len(fetched), len(scalars)
    last = first + n + len(near)
    far = [k for k, (_, _, memory) in enumerate(outs) if memory is pltpu.HBM]

    def view(ref, where):
        return ref if where is None else ref.at[where]

    def held_shape(value, where):
        if where is None:
            return value.shape
        return value.shape[1:] if isinstance(where, int) else (where.size,) + value.shape[1:]

    def kernel(*refs):
        out = list(refs[last : last + len(outs)])
        rest = list(refs[last + len(outs) :])
        buffers, out_buffers, rest = rest[:n], rest[n : n + len(far)], rest[n + len(far) :]
        sems = rest.pop(0) if n else None
        out_sems = rest.pop(0) if far else None
        copies = [
            pltpu.make_async_copy(view(refs[first + i], copied[i][1]), buffers[i], sems.at[i])
            for i in range(n)
        ]
        for copy in copies:
            copy.start()
        for copy in copies[:m]:
            copy.wait()
        written = list(out)
        for k, buffer in zip(far, out_buffers):
            written[k] = buffer
        later = body(*refs[:first], *buffers, *refs[first + n : last], *written, *rest)
        for copy in copies[m:]:
            copy.wait()
        if late:
            later()
        copies = [
            pltpu.make_async_copy(buffer, out[k], out_sems.at[i])
            for i, (k, buffer) in enumerate(zip(far, out_buffers))
        ]
        for copy in copies:
            copy.start()
        for copy in copies:
            copy.wait()

    buffered = [pltpu.VMEM(held_shape(value, where), value.dtype) for value, where in copied]
    buffered += [pltpu.VMEM(*outs[k][:2]) for k in far]
    buffered += [pltpu.SemaphoreType.DMA((n,))] if n else []
    buffered += [pltpu.SemaphoreType.DMA((len(far),))] if far else []
    result, specs = [], []
    for shape, kind, memory in outs:
        result.append((memory or jax.ShapeDtypeStruct)(shape, kind))
        specs.append(HBM if memory is pltpu.HBM else SMEM if shape == (1,) else VMEM)
    arrays = [pltpu.with_memory_space_constraint(value, pltpu.HBM) for value, _ in copied]
    moved = sum(a.size * a.dtype.itemsize for a in arrays + list(near))
    moved += sum(math.prod(shape) * jnp.dtype(kind).itemsize for shape, kind, _ in outs)
    return pl.pallas_call(
        kernel,
        out_shape=result,
        in_specs=[SMEM] * first + [HBM] * n + [VMEM] * len(near),
        out_specs=specs,
        scratch_shapes=buffered + [pltpu.VMEM(size, kind) for size, kind in scratch],
        compiler_params=pltpu.CompilerParams(vmem_limit_bytes=20 * 2**20),
        cost_estimate=pl.CostEstimate(flops=flops, bytes_accessed=moved, transcendentals=0),
        name=body.func.__name__ if isinstance(body, functools.partial) else body.__name__,
    )(*scalars, *arrays, *near)


def held(value):
    return pltpu.with_memory_space_constraint(value, pltpu.VMEM)


def z_pairs(step):
    pairs = []
    for zh in range(N_Z):
        for core in range(2):
            turn = (1, 3)[step ^ core]
            pairs.append((zh * 2 + core, (zh ^ turn) * 2 + core))
    return pairs


def over_z(value, step):
    return lax.ppermute(value, ("z_hi", "core"), z_pairs(step))


def over_y(value):
    return lax.all_to_all(value, "y", 0, 0, tiled=True)


def swap_core(value):
    return lax.ppermute(value, "core", [(0, 1), (1, 0)])


def to_group(value, hop):
    count = SIZES[0] * SIZES[1]
    return lax.ppermute(value, GROUP, [(i, (i + hop) % count) for i in range(count)])


def to_group_other(value, hop):
    count = SIZES[0] * SIZES[1]
    pairs = [(i * 2 + c, (i + hop) % count * 2 + 1 - c) for i in range(count) for c in range(2)]
    return lax.ppermute(value, GROUP + ("core",), pairs)


OWN = ((BLOCK, COLS), F32, pltpu.VMEM)


WHOLE = ((SLAB, COLS), B16, pltpu.VMEM)
SPREAD = ((N_Y, SLAB, COLS), B16, pltpu.HBM)


def add_z(slab, own, step, body, out, before=None):
    got = over_z(slab, step)
    if before is not None:
        got, _ = lax.optimization_barrier((got, before))
    return call(body, [], [], [], [held(own), held(slab), held(got)], [out, OWN])


def local(inputs, targets, numerator, momentum, received, push_weight, received_weight, mix_share):
    push, push_got, mix = push_weight, received_weight, mix_share
    state = [(numerator, 0), (received, 0), (momentum, 0)]

    part_far, part_own = call(
        first_values,
        [push],
        [(inputs, 0), (numerator, 0), targets],
        [],
        [],
        [((TOKENS + 2 * PADDED, COLS), B16, pltpu.VMEM), ((TOKENS, COLS), B16, pltpu.VMEM)],
    )
    part_got = swap_core(part_far)
    near = [held(part_own), held(part_got)]
    (part1,) = call(add_parts, [], [], [], near, [((TOKENS, COLS), B16, pltpu.HBM)])
    taught = [targets, part_got[TOKENS:]]

    later, _ = lax.optimization_barrier((numerator, part1))
    message, mine = call(
        make_message,
        [],
        [inputs, (later, 0)] + state[1:],
        [],
        [],
        [((MESSAGE, WIDTH), B16, pltpu.VMEM), ((2 * TOKENS, WIDTH), B16, pltpu.HBM)],
    )
    got = swap_core(message)

    parts1 = over_y(part1.reshape(N_Y, SLAB, COLS))
    slab, own1 = call(
        functools.partial(sum_over_y, 0), [], taught, [], [held(parts1)], [WHOLE, OWN]
    )

    mine, _ = lax.optimization_barrier((mine, slab))
    (part2,) = call(
        second_values,
        [push, push_got, mix],
        state + [mine, got],
        [],
        [],
        [((TOKENS, COLS + HALF), B16, pltpu.HBM)],
    )
    slab, own1 = add_z(slab, own1, 0, add_slab, WHOLE, part2)
    part2, _ = lax.optimization_barrier((part2, slab))
    parts2 = over_y(part2.reshape(N_Y, SLAB, COLS + HALF))
    sent, own1 = add_z(slab, own1, 1, add_and_spread, SPREAD)
    all1 = over_y(sent).reshape(TOKENS, COLS)

    parts2, _ = lax.optimization_barrier((parts2, sent))
    base, own2, gram = call(
        functools.partial(sum_over_y, 1),
        [],
        taught,
        [],
        [held(parts2)],
        [WHOLE, OWN, ((SLAB, HALF), B16, pltpu.VMEM)],
    )
    near = [held(own2), all1, held(gram), held(swap_core(gram)), held(base)]
    slab, own2 = call(
        second_residual, [push, push_got, mix], [], [], near, [WHOLE, OWN], [((SLAB, COLS), F32)]
    )
    near, far, ready = call(
        first_gradient,
        [push, mix],
        state + [(mine, pl.ds(X1_AT, TOKENS)), (got, pl.ds(X1_AT, MESSAGE - X1_AT))],
        [],
        [all1],
        [
            ((WIDTH + EXTRA, COLS), B16, pltpu.VMEM),
            ((WIDTH, COLS), B16, pltpu.VMEM),
            ((2 * WIDTH, COLS), F32, pltpu.HBM),
        ],
    )
    slab, own2 = add_z(slab, own2, 0, add_slab, WHOLE, far)
    sent, own2 = add_z(slab, own2, 1, add_and_spread, SPREAD)
    all2 = over_y(sent).reshape(TOKENS, COLS)
    near, _ = lax.optimization_barrier((near, sent))
    arrived, arrived_far = to_group(near, 1), to_group_other(far, 1)
    all2, arrived = lax.optimization_barrier((all2, arrived))

    far, near, half, message = call(
        second_gradient,
        [push, push_got, mix],
        [ready, (mine, pl.ds(0, TOKENS)), (got, pl.ds(0, TOKENS))],
        [],
        [held(own1), held(own2), all2],
        [
            ((WIDTH, COLS), B16, None),
            ((WIDTH + EXTRA, COLS), B16, None),
            ((WIDTH, COLS), F32, None),
            ((WIDTH + 2 * ROWS, COLS), F32, None),
        ],
    )

    sent_far, sent_own = to_group_other(far, 2), to_group(near, 2)
    whole = ((1, WIDTH, VALUES), B16, None)
    number = ((1,), F32, None)
    final_numerator, value_rows, final_weight = call(
        join_numerator,
        [push, push_got, mix],
        [],
        [],
        [held(arrived), held(arrived_far), held(own1), held(own2), half, swap_core(message)],
        [whole, ((2, ROWS, VALUES), B16, None), number],
    )
    sent_far, final_numerator = lax.optimization_barrier((sent_far, final_numerator))
    final_received, got_weight = call(
        join_received, [], [], [], [sent_own, sent_far], [whole, number]
    )
    return final_numerator, final_weight, final_received, got_weight, value_rows


def solution(mesh):
    fine = Mesh(mesh.devices.reshape(SIZES), GROUP + MP)
    placed = (
        P(None, GROUP, MP),
        P(None, GROUP + MP, None),
        P(GROUP, MP, None),
        P(GROUP, MP, None),
        P(GROUP, MP, None),
        P(GROUP),
        P(GROUP),
        P(GROUP, None),
    )
    return jax.shard_map(
        local,
        mesh=fine,
        in_specs=placed,
        out_specs=(
            P(GROUP, MP, None),
            P(GROUP),
            P(GROUP, MP, None),
            P(GROUP),
            P(None, GROUP + MP, None),
        ),
        check_vma=False,
    )
```

```python
import functools
import math

import jax
import jax.numpy as jnp
from jax import lax
from jax.experimental import pallas as pl
from jax.experimental.pallas import tpu as pltpu
from jax.sharding import Mesh
from jax.sharding import PartitionSpec as P

GROUP = ("x", "z_lo")
MP = ("z_hi", "y", "core")
SIZES = (4, 4, 4, 4, 2)
N_Z, N_Y = SIZES[2], SIZES[3]

momentum_decay = 0.9
step_size = 0.5

ROWS = 24
BLOCK = 2 * ROWS
SLAB = N_Z * BLOCK
TOKENS = N_Y * SLAB
WIDTH = 256
VALUES = 1024
COLS = VALUES // 2
HALF = TOKENS // 2
PADDED = 32
EXTRA = 16
ROW_SCALE = 1.0 / math.sqrt(WIDTH * N_Z * N_Y * 2)
GRAD_SCALE = 1.0 / math.sqrt(TOKENS)

X1_AT = TOKENS
W_AT = 2 * TOKENS
REC_AT = W_AT + 2 * WIDTH
M_AT = REC_AT + 2 * WIDTH
MESSAGE = M_AT + 4 * WIDTH

B16, F32 = jnp.bfloat16, jnp.float32


def f32(value):
    return value.astype(jnp.float32)


def bf16(value):
    return value.astype(jnp.bfloat16)


def dot(a, b, dims=((1,), (0,))):
    return lax.dot_general(a, b, (dims, ((), ())), preferred_element_type=jnp.float32)


def cols_of(core):
    return pl.ds(pl.multiple_of(core * COLS, COLS), COLS)


def half_of(core):
    return pl.ds(pl.multiple_of(core * HALF, 16), HALF)


def own_block():
    return pl.ds(pl.multiple_of(lax.axis_index("z_hi") * BLOCK, 16), BLOCK)


def kept(mix, step):
    return mix[0, step].astype(jnp.float32) * 0.125


def by_y():
    return [((zh * N_Y + y) * BLOCK, (y * N_Z + zh) * BLOCK) for zh in range(N_Z) for y in range(N_Y)]


def prepare(push, x, w, rec, velocity, targets, far, own, message, tokens):
    core = lax.axis_index("core")
    for out, side in ((far, 1 - core), (own, core)):
        scaled = bf16(f32(w[:, cols_of(side)]) / push[0])
        part = bf16(dot(x[0], scaled) * ROW_SCALE)
        for at, to in by_y():
            out[to : to + BLOCK] = part[at : at + BLOCK]
    spare = jnp.zeros((PADDED - ROWS, COLS), jnp.float32)
    side = cols_of(1 - core)
    for step in range(2):
        row = TOKENS + step * PADDED
        far[row : row + PADDED] = bf16(jnp.concatenate([f32(targets[step, :, side]), spare], axis=0))
        for at, to in by_y():
            row = (1 - step) * TOKENS + to
            message[row : row + BLOCK] = x[step, at : at + BLOCK]
            tokens[row : row + BLOCK] = x[step, at : at + BLOCK]
    old = velocity[:, side]
    high = bf16(old)
    halves = [(W_AT, w[:, side]), (REC_AT, rec[:, side]), (M_AT, high)]
    halves += [(M_AT + 2 * WIDTH, bf16(old - f32(high)))]
    for row, half in halves:
        message[row : row + WIDTH] = half[:, :WIDTH]
        message[row + WIDTH : row + 2 * WIDTH] = half[:, WIDTH:]


def add_parts(own, got, out):
    out[...] = bf16(f32(own[...]) + f32(got[:TOKENS]))


def tile(mix, w, rec, velocity, got, first, k):
    keep = kept(mix, 0)
    if k == 0:
        side = cols_of(lax.axis_index("core"))
        start, arrived, old = w[:, side], rec[:, side], velocity[:, side]
    else:
        start, arrived, high, low = (
            jnp.concatenate([got[at : at + WIDTH], got[at + WIDTH : at + 2 * WIDTH]], axis=1)
            for at in (W_AT - first, REC_AT - first, M_AT - first, M_AT + 2 * WIDTH - first)
        )
        old = f32(high) + f32(low)
    ahead = f32(start) - (step_size * momentum_decay) * old
    return ahead, keep * ahead + f32(arrived), old


def second_values(push, push_got, mix, w, rec, velocity, mine, got, out):
    core = lax.axis_index("core")
    weight = kept(mix, 0) * push[0] + push_got[0]
    near, far = mine[:TOKENS], got[:TOKENS]
    scaled = [bf16(tile(mix, w, rec, velocity, got, 0, k)[1] / weight) for k in range(2)]
    out[:, :COLS] = bf16((dot(near, scaled[0]) + dot(far, scaled[1])) * ROW_SCALE)
    rows = pl.ds(pl.multiple_of(X1_AT + core * HALF, 16), HALF)
    across = ((1,), (1,))
    out[:, COLS:] = bf16(dot(near, mine[rows], across) + dot(far, got[rows], across))


def sum_over_y(step, targets, targets_got, parts, slab, own, *gram):
    core = lax.axis_index("core")
    total = f32(parts[0])
    for y in range(1, N_Y):
        total = total + f32(parts[y])
    slab[...] = bf16(total[:, :COLS])
    if gram:
        gram[0][...] = bf16(total[:, COLS:])
    rows = own_block()
    total = f32(parts[0, rows, :COLS])
    for y in range(1, N_Y):
        total = total + f32(parts[y, rows, :COLS])
    own[...] = total
    near = f32(targets[step, :, cols_of(core)])
    far = f32(targets_got[step * PADDED : (step + 1) * PADDED])[:ROWS]
    low, high = jnp.where(core == 0, near, far), jnp.where(core == 0, far, near)
    slab[rows] = bf16(total - jnp.concatenate([low, high], axis=0))


def add_slab(own, mine, got, out, own_out):
    out[...] = bf16(f32(mine[...]) + f32(got[...]))
    own_out[...] = own[...] + f32(got[own_block()])


def add_and_spread(own, mine, got, out, own_out):
    total = bf16(f32(mine[...]) + f32(got[...]))
    for y in range(N_Y):
        out[y] = total
    own_out[...] = own[...] + f32(got[own_block()])


def second_residual(push, push_got, mix, own, all1, gram, gram_got, base, out, own_out, turned):
    core = lax.axis_index("core")
    keep = kept(mix, 0)
    back = step_size * GRAD_SCALE * ROW_SCALE * keep / (keep * push[0] + push_got[0])
    near, far = all1[half_of(core)], all1[half_of(1 - core)]
    turned[...] = (dot(gram[...], near) + dot(gram_got[...], far)) * back
    out[...] = bf16(f32(base[...]) - turned[...])
    own_out[...] = own[...] - turned[own_block()]


def first_gradient(push, mix, w, rec, velocity, mine, got, all1, near, far, ready):
    keep = kept(mix, 0)
    down = ((0,), (0,))
    for k, x, out in ((0, mine, near), (1, got, far)):
        ahead, base, old = tile(mix, w, rec, velocity, got, X1_AT, k)
        gradient = dot(x[:TOKENS], all1[...], down) * GRAD_SCALE
        out[:WIDTH] = bf16((1.0 - keep) * (ahead - step_size * gradient))
        current = bf16(base - (step_size * keep) * gradient)
        moved = momentum_decay * old + gradient
        ready[k * WIDTH : (k + 1) * WIDTH] = f32(current) - (step_size * momentum_decay) * moved
    near[WIDTH:] = bf16(jnp.full((EXTRA, COLS), (1.0 - keep) * push[0], jnp.float32))


def second_gradient(
    push, push_got, mix, ready, mine, got, own1, own2, all2, far, near, half, message, message_low
):
    core = lax.axis_index("core")
    keep = kept(mix, 1)
    down = ((0,), (0,))
    gradient = dot(got[...], all2[...], down) * GRAD_SCALE
    moved = ready[WIDTH:] - step_size * gradient
    far[...] = bf16((1.0 - keep) * moved)
    message[: WIDTH // 2] = bf16(keep * moved[: WIDTH // 2])
    message_low[...] = bf16(keep * moved[WIDTH // 2 :])
    gradient = dot(mine[...], all2[...], down) * GRAD_SCALE
    moved = ready[:WIDTH] - step_size * gradient
    near[:WIDTH] = bf16((1.0 - keep) * moved)
    half[...] = keep * moved
    weight = kept(mix, 0) * push[0] + push_got[0]
    near[WIDTH:] = bf16(jnp.full((EXTRA, COLS), (1.0 - keep) * weight, jnp.float32))
    spare = jnp.zeros((PADDED - ROWS, COLS), jnp.float32)
    for step, own in ((0, own1), (1, own2)):
        row = WIDTH // 2 + step * PADDED
        block = jnp.where(core == 0, own[ROWS:], own[:ROWS])
        message[row : row + PADDED] = bf16(jnp.concatenate([block, spare], axis=0))


def join_numerator(
    push, push_got, mix, arrived, arrived_far, own1, own2, half, message, message_low, out, rows_out, weight
):
    core = lax.axis_index("core")
    cut = WIDTH // 2
    out[0, :, cols_of(core)] = bf16(half[...] + f32(arrived[:WIDTH]))
    out[0, :cut, cols_of(1 - core)] = bf16(f32(message[:cut]) + f32(arrived_far[:cut]))
    out[0, cut:, cols_of(1 - core)] = bf16(f32(message_low[...]) + f32(arrived_far[cut:]))
    for step, own in ((0, own1), (1, own2)):
        row = cut + step * PADDED
        rows_out[step, :, cols_of(core)] = bf16(jnp.where(core == 0, own[:ROWS], own[ROWS:]))
        rows_out[step, :, cols_of(1 - core)] = bf16(f32(message[row : row + PADDED])[:ROWS])
    last = kept(mix, 0) * push[0] + push_got[0]
    weight[0] = kept(mix, 1) * last + jnp.max(f32(arrived[WIDTH:]))


def join_received(near, far, out, weight):
    core = lax.axis_index("core")
    out[0, :, cols_of(core)] = near[:WIDTH]
    out[0, :, cols_of(1 - core)] = far[...]
    weight[0] = jnp.max(f32(near[WIDTH:]))


SMEM = pl.BlockSpec(memory_space=pltpu.SMEM)
HBM = pl.BlockSpec(memory_space=pltpu.HBM)
VMEM = pl.BlockSpec(memory_space=pltpu.VMEM)


def call(body, scalars, fetched, late, near, outs, scratch=(), flops=0):
    copied = [f if isinstance(f, tuple) else (f, None) for f in list(fetched) + list(late)]
    n, m, first = len(copied), len(fetched), len(scalars)
    last = first + n + len(near)
    far = [k for k, (_, _, memory) in enumerate(outs) if memory is pltpu.HBM]

    def view(ref, where):
        return ref if where is None else ref.at[where]

    def held_shape(value, where):
        if where is None:
            return value.shape
        return value.shape[1:] if isinstance(where, int) else (where.size,) + value.shape[1:]

    def kernel(*refs):
        out = list(refs[last : last + len(outs)])
        rest = list(refs[last + len(outs) :])
        buffers, out_buffers, rest = rest[:n], rest[n : n + len(far)], rest[n + len(far) :]
        sems = rest.pop(0) if n else None
        out_sems = rest.pop(0) if far else None
        copies = [
            pltpu.make_async_copy(view(refs[first + i], copied[i][1]), buffers[i], sems.at[i])
            for i in range(n)
        ]
        for copy in copies:
            copy.start()
        for copy in copies[:m]:
            copy.wait()
        written = list(out)
        for k, buffer in zip(far, out_buffers):
            written[k] = buffer
        later = body(*refs[:first], *buffers, *refs[first + n : last], *written, *rest)
        for copy in copies[m:]:
            copy.wait()
        if late:
            later()
        copies = [
            pltpu.make_async_copy(buffer, out[k], out_sems.at[i])
            for i, (k, buffer) in enumerate(zip(far, out_buffers))
        ]
        for copy in copies:
            copy.start()
        for copy in copies:
            copy.wait()

    buffered = [pltpu.VMEM(held_shape(value, where), value.dtype) for value, where in copied]
    buffered += [pltpu.VMEM(*outs[k][:2]) for k in far]
    buffered += [pltpu.SemaphoreType.DMA((n,))] if n else []
    buffered += [pltpu.SemaphoreType.DMA((len(far),))] if far else []
    result, specs = [], []
    for shape, kind, memory in outs:
        result.append((memory or jax.ShapeDtypeStruct)(shape, kind))
        specs.append(HBM if memory is pltpu.HBM else SMEM if shape == (1,) else VMEM)
    arrays = [pltpu.with_memory_space_constraint(value, pltpu.HBM) for value, _ in copied]
    moved = sum(a.size * a.dtype.itemsize for a in arrays + list(near))
    moved += sum(math.prod(shape) * jnp.dtype(kind).itemsize for shape, kind, _ in outs)
    return pl.pallas_call(
        kernel,
        out_shape=result,
        in_specs=[SMEM] * first + [HBM] * n + [VMEM] * len(near),
        out_specs=specs,
        scratch_shapes=buffered + [pltpu.VMEM(size, kind) for size, kind in scratch],
        compiler_params=pltpu.CompilerParams(vmem_limit_bytes=20 * 2**20),
        cost_estimate=pl.CostEstimate(flops=flops, bytes_accessed=moved, transcendentals=0),
        name=body.func.__name__ if isinstance(body, functools.partial) else body.__name__,
    )(*scalars, *arrays, *near)


def held(value):
    return pltpu.with_memory_space_constraint(value, pltpu.VMEM)


def z_pairs(step):
    pairs = []
    for zh in range(N_Z):
        for core in range(2):
            turn = (1, 3)[step ^ core]
            pairs.append((zh * 2 + core, (zh ^ turn) * 2 + core))
    return pairs


def over_z(value, step):
    return lax.ppermute(value, ("z_hi", "core"), z_pairs(step))


def over_y(value):
    return lax.all_to_all(value, "y", 0, 0, tiled=True)


def swap_core(value):
    return lax.ppermute(value, "core", [(0, 1), (1, 0)])


def to_group(value, hop):
    count = SIZES[0] * SIZES[1]
    return lax.ppermute(value, GROUP, [(i, (i + hop) % count) for i in range(count)])


def to_group_other(value, hop):
    count = SIZES[0] * SIZES[1]
    pairs = [(i * 2 + c, (i + hop) % count * 2 + 1 - c) for i in range(count) for c in range(2)]
    return lax.ppermute(value, GROUP + ("core",), pairs)


OWN = ((BLOCK, COLS), F32, pltpu.VMEM)


WHOLE = ((SLAB, COLS), B16, pltpu.VMEM)
SPREAD = ((N_Y, SLAB, COLS), B16, pltpu.HBM)


def add_z(slab, own, step, body, out, before=None):
    got = over_z(slab, step)
    if before is not None:
        got, _ = lax.optimization_barrier((got, before))
    return call(body, [], [], [], [held(own), held(slab), held(got)], [out, OWN])


def local(inputs, targets, numerator, momentum, received, push_weight, received_weight, mix_share):
    push, push_got, mix = push_weight, received_weight, mix_share
    state = [(numerator, 0), (received, 0), (momentum, 0)]

    part_far, part_own, message, mine = call(
        prepare,
        [push],
        [inputs] + state + [targets],
        [],
        [],
        [
            ((TOKENS + 2 * PADDED, COLS), B16, pltpu.VMEM),
            ((TOKENS, COLS), B16, pltpu.VMEM),
            ((MESSAGE, WIDTH), B16, pltpu.VMEM),
            ((2 * TOKENS, WIDTH), B16, pltpu.HBM),
        ],
    )
    part_got = swap_core(part_far)
    near = [held(part_own), held(part_got)]
    (part1,) = call(add_parts, [], [], [], near, [((TOKENS, COLS), B16, pltpu.HBM)])
    taught = [targets, part_got[TOKENS:]]

    message, _ = lax.optimization_barrier((message, part1))
    got = swap_core(message)

    parts1 = over_y(part1.reshape(N_Y, SLAB, COLS))
    slab, own1 = call(
        functools.partial(sum_over_y, 0), [], taught, [], [held(parts1)], [WHOLE, OWN]
    )

    mine, _ = lax.optimization_barrier((mine, slab))
    (part2,) = call(
        second_values,
        [push, push_got, mix],
        state + [mine, got],
        [],
        [],
        [((TOKENS, COLS + HALF), B16, pltpu.HBM)],
    )
    slab, own1 = add_z(slab, own1, 0, add_slab, WHOLE, part2)
    part2, _ = lax.optimization_barrier((part2, slab))
    parts2 = over_y(part2.reshape(N_Y, SLAB, COLS + HALF))
    sent, own1 = add_z(slab, own1, 1, add_and_spread, SPREAD)
    all1 = over_y(sent).reshape(TOKENS, COLS)

    parts2, _ = lax.optimization_barrier((parts2, sent))
    base, own2, gram = call(
        functools.partial(sum_over_y, 1),
        [],
        taught,
        [],
        [held(parts2)],
        [WHOLE, OWN, ((SLAB, HALF), B16, pltpu.VMEM)],
    )
    near = [held(own2), all1, held(gram), held(swap_core(gram)), held(base)]
    slab, own2 = call(
        second_residual, [push, push_got, mix], [], [], near, [WHOLE, OWN], [((SLAB, COLS), F32)]
    )
    near, far, ready = call(
        first_gradient,
        [push, mix],
        state + [(mine, pl.ds(X1_AT, TOKENS)), (got, pl.ds(X1_AT, MESSAGE - X1_AT))],
        [],
        [all1],
        [
            ((WIDTH + EXTRA, COLS), B16, pltpu.VMEM),
            ((WIDTH, COLS), B16, pltpu.VMEM),
            ((2 * WIDTH, COLS), F32, pltpu.HBM),
        ],
    )
    slab, own2 = add_z(slab, own2, 0, add_slab, WHOLE, far)
    sent, own2 = add_z(slab, own2, 1, add_and_spread, SPREAD)
    all2 = over_y(sent).reshape(TOKENS, COLS)
    near, _ = lax.optimization_barrier((near, sent))
    arrived, arrived_far = to_group(near, 1), to_group_other(far, 1)
    all2, arrived = lax.optimization_barrier((all2, arrived))

    far, near, half, message, message_low = call(
        second_gradient,
        [push, push_got, mix],
        [ready, (mine, pl.ds(0, TOKENS)), (got, pl.ds(0, TOKENS))],
        [],
        [held(own1), held(own2), all2],
        [
            ((WIDTH, COLS), B16, None),
            ((WIDTH + EXTRA, COLS), B16, None),
            ((WIDTH, COLS), F32, None),
            ((WIDTH // 2 + 2 * PADDED, COLS), B16, None),
            ((WIDTH // 2, COLS), B16, None),
        ],
    )

    sent_far, sent_own = to_group_other(far, 2), to_group(near, 2)
    whole = ((1, WIDTH, VALUES), B16, None)
    number = ((1,), F32, None)
    final_numerator, value_rows, final_weight = call(
        join_numerator,
        [push, push_got, mix],
        [],
        [],
        [
            held(arrived),
            held(arrived_far),
            held(own1),
            held(own2),
            half,
            swap_core(message),
            swap_core(message_low),
        ],
        [whole, ((2, ROWS, VALUES), B16, None), number],
    )
    sent_far, final_numerator = lax.optimization_barrier((sent_far, final_numerator))
    final_received, got_weight = call(
        join_received, [], [], [], [sent_own, sent_far], [whole, number]
    )
    return final_numerator, final_weight, final_received, got_weight, value_rows


def solution(mesh):
    fine = Mesh(mesh.devices.reshape(SIZES), GROUP + MP)
    placed = (
        P(None, GROUP, MP),
        P(None, GROUP + MP, None),
        P(GROUP, MP, None),
        P(GROUP, MP, None),
        P(GROUP, MP, None),
        P(GROUP),
        P(GROUP),
        P(GROUP, None),
    )
    return jax.shard_map(
        local,
        mesh=fine,
        in_specs=placed,
        out_specs=(
            P(GROUP, MP, None),
            P(GROUP),
            P(GROUP, MP, None),
            P(GROUP),
            P(None, GROUP + MP, None),
        ),
        check_vma=False,
    )
```

```python
import functools
import math

import jax
import jax.numpy as jnp
from jax import lax
from jax.experimental import pallas as pl
from jax.experimental.pallas import tpu as pltpu
from jax.sharding import Mesh
from jax.sharding import PartitionSpec as P

GROUP = ("x", "z_lo")
MP = ("z_hi", "y", "core")
SIZES = (4, 4, 4, 4, 2)
N_Z, N_Y = SIZES[2], SIZES[3]

momentum_decay = 0.9
step_size = 0.5

ROWS = 24
BLOCK = 2 * ROWS
SLAB = N_Z * BLOCK
TOKENS = N_Y * SLAB
WIDTH = 256
VALUES = 1024
COLS = VALUES // 2
HALF = TOKENS // 2
PADDED = 32
EXTRA = 16
ROW_SCALE = 1.0 / math.sqrt(WIDTH * N_Z * N_Y * 2)
GRAD_SCALE = 1.0 / math.sqrt(TOKENS)

X1_AT = TOKENS
W_AT = 2 * TOKENS
REC_AT = W_AT + 2 * WIDTH
M_AT = REC_AT + 2 * WIDTH
MESSAGE = M_AT + 4 * WIDTH

B16, F32 = jnp.bfloat16, jnp.float32


def f32(value):
    return value.astype(jnp.float32)


def bf16(value):
    return value.astype(jnp.bfloat16)


def dot(a, b, dims=((1,), (0,))):
    return lax.dot_general(a, b, (dims, ((), ())), preferred_element_type=jnp.float32)


def cols_of(core):
    return pl.ds(pl.multiple_of(core * COLS, COLS), COLS)


def half_of(core):
    return pl.ds(pl.multiple_of(core * HALF, 16), HALF)


def own_block():
    return pl.ds(pl.multiple_of(lax.axis_index("z_hi") * BLOCK, 16), BLOCK)


def kept(mix, step):
    return mix[0, step].astype(jnp.float32) * 0.125


def by_y():
    return [((zh * N_Y + y) * BLOCK, (y * N_Z + zh) * BLOCK) for zh in range(N_Z) for y in range(N_Y)]


def first_values(push, x, w, targets, far, own):
    core = lax.axis_index("core")
    for out, side in ((far, 1 - core), (own, core)):
        scaled = bf16(f32(w[:, cols_of(side)]) / push[0])
        part = bf16(dot(x[...], scaled) * ROW_SCALE)
        for at, to in by_y():
            out[to : to + BLOCK] = part[at : at + BLOCK]
    spare = jnp.zeros((PADDED - ROWS, COLS), jnp.float32)
    for step in range(2):
        row = TOKENS + step * PADDED
        half = jnp.concatenate([f32(targets[step, :, cols_of(1 - core)]), spare], axis=0)
        far[row : row + PADDED] = bf16(half)


def make_message(x, w, rec, velocity, message, tokens):
    side = cols_of(1 - lax.axis_index("core"))
    for step in range(2):
        for at, to in by_y():
            row = (1 - step) * TOKENS + to
            message[row : row + BLOCK] = x[step, at : at + BLOCK]
            tokens[row : row + BLOCK] = x[step, at : at + BLOCK]
    old = velocity[:, side]
    high = bf16(old)
    halves = [(W_AT, w[:, side]), (REC_AT, rec[:, side]), (M_AT, high)]
    halves += [(M_AT + 2 * WIDTH, bf16(old - f32(high)))]
    for row, half in halves:
        message[row : row + WIDTH] = half[:, :WIDTH]
        message[row + WIDTH : row + 2 * WIDTH] = half[:, WIDTH:]


def add_parts(own, got, out):
    out[...] = bf16(f32(own[...]) + f32(got[:TOKENS]))


def tile(mix, w, rec, velocity, got, first, k):
    keep = kept(mix, 0)
    if k == 0:
        side = cols_of(lax.axis_index("core"))
        start, arrived, old = w[:, side], rec[:, side], velocity[:, side]
    else:
        start, arrived, high, low = (
            jnp.concatenate([got[at : at + WIDTH], got[at + WIDTH : at + 2 * WIDTH]], axis=1)
            for at in (W_AT - first, REC_AT - first, M_AT - first, M_AT + 2 * WIDTH - first)
        )
        old = f32(high) + f32(low)
    ahead = f32(start) - (step_size * momentum_decay) * old
    return ahead, keep * ahead + f32(arrived), old


def second_values(push, push_got, mix, w, rec, velocity, mine, got, out):
    core = lax.axis_index("core")
    weight = kept(mix, 0) * push[0] + push_got[0]
    near, far = mine[:TOKENS], got[:TOKENS]
    scaled = [bf16(tile(mix, w, rec, velocity, got, 0, k)[1] / weight) for k in range(2)]
    out[:, :COLS] = bf16((dot(near, scaled[0]) + dot(far, scaled[1])) * ROW_SCALE)
    rows = pl.ds(pl.multiple_of(X1_AT + core * HALF, 16), HALF)
    across = ((1,), (1,))
    out[:, COLS:] = bf16(dot(near, mine[rows], across) + dot(far, got[rows], across))


def sum_over_y(step, targets, targets_got, parts, slab, own, *gram):
    core = lax.axis_index("core")
    total = f32(parts[0])
    for y in range(1, N_Y):
        total = total + f32(parts[y])
    slab[...] = bf16(total[:, :COLS])
    if gram:
        gram[0][...] = bf16(total[:, COLS:])
    rows = own_block()
    total = f32(parts[0, rows, :COLS])
    for y in range(1, N_Y):
        total = total + f32(parts[y, rows, :COLS])
    own[...] = total
    near = f32(targets[step, :, cols_of(core)])
    far = f32(targets_got[step * PADDED : (step + 1) * PADDED])[:ROWS]
    low, high = jnp.where(core == 0, near, far), jnp.where(core == 0, far, near)
    slab[rows] = bf16(total - jnp.concatenate([low, high], axis=0))


def add_slab(own, mine, got, out, own_out):
    out[...] = bf16(f32(mine[...]) + f32(got[...]))
    own_out[...] = own[...] + f32(got[own_block()])


def add_and_spread(own, mine, got, out, own_out):
    total = bf16(f32(mine[...]) + f32(got[...]))
    for y in range(N_Y):
        out[y] = total
    own_out[...] = own[...] + f32(got[own_block()])


def second_residual(push, push_got, mix, own, all1, gram, gram_got, base, out, own_out, turned):
    core = lax.axis_index("core")
    keep = kept(mix, 0)
    back = step_size * GRAD_SCALE * ROW_SCALE * keep / (keep * push[0] + push_got[0])
    near, far = all1[half_of(core)], all1[half_of(1 - core)]
    turned[...] = (dot(gram[...], near) + dot(gram_got[...], far)) * back
    out[...] = bf16(f32(base[...]) - turned[...])
    own_out[...] = own[...] - turned[own_block()]


def first_gradient(push, mix, w, rec, velocity, mine, got, all1, near, far, ready):
    keep = kept(mix, 0)
    down = ((0,), (0,))
    for k, x, out in ((0, mine, near), (1, got, far)):
        ahead, base, old = tile(mix, w, rec, velocity, got, X1_AT, k)
        gradient = dot(x[:TOKENS], all1[...], down) * GRAD_SCALE
        out[:WIDTH] = bf16((1.0 - keep) * (ahead - step_size * gradient))
        current = bf16(base - (step_size * keep) * gradient)
        moved = momentum_decay * old + gradient
        ready[k * WIDTH : (k + 1) * WIDTH] = f32(current) - (step_size * momentum_decay) * moved
    near[WIDTH:] = bf16(jnp.full((EXTRA, COLS), (1.0 - keep) * push[0], jnp.float32))


def second_gradient(
    push, push_got, mix, ready, mine, got, own1, own2, all2, far, near, half, message, message_low
):
    core = lax.axis_index("core")
    keep = kept(mix, 1)
    down = ((0,), (0,))
    gradient = dot(got[...], all2[...], down) * GRAD_SCALE
    moved = ready[WIDTH:] - step_size * gradient
    far[...] = bf16((1.0 - keep) * moved)
    message[: WIDTH // 2] = bf16(keep * moved[: WIDTH // 2])
    message_low[...] = bf16(keep * moved[WIDTH // 2 :])
    gradient = dot(mine[...], all2[...], down) * GRAD_SCALE
    moved = ready[:WIDTH] - step_size * gradient
    near[:WIDTH] = bf16((1.0 - keep) * moved)
    half[...] = keep * moved
    weight = kept(mix, 0) * push[0] + push_got[0]
    near[WIDTH:] = bf16(jnp.full((EXTRA, COLS), (1.0 - keep) * weight, jnp.float32))
    spare = jnp.zeros((PADDED - ROWS, COLS), jnp.float32)
    for step, own in ((0, own1), (1, own2)):
        row = WIDTH // 2 + step * PADDED
        block = jnp.where(core == 0, own[ROWS:], own[:ROWS])
        message[row : row + PADDED] = bf16(jnp.concatenate([block, spare], axis=0))


def join_numerator(
    push, push_got, mix, arrived, arrived_far, own1, own2, half, message, message_low, out, rows_out, weight
):
    core = lax.axis_index("core")
    cut = WIDTH // 2
    out[0, :, cols_of(core)] = bf16(half[...] + f32(arrived[:WIDTH]))
    out[0, :cut, cols_of(1 - core)] = bf16(f32(message[:cut]) + f32(arrived_far[:cut]))
    out[0, cut:, cols_of(1 - core)] = bf16(f32(message_low[...]) + f32(arrived_far[cut:]))
    for step, own in ((0, own1), (1, own2)):
        row = cut + step * PADDED
        rows_out[step, :, cols_of(core)] = bf16(jnp.where(core == 0, own[:ROWS], own[ROWS:]))
        rows_out[step, :, cols_of(1 - core)] = bf16(f32(message[row : row + PADDED])[:ROWS])
    last = kept(mix, 0) * push[0] + push_got[0]
    weight[0] = kept(mix, 1) * last + jnp.max(f32(arrived[WIDTH:]))


def join_received(near, far, out, weight):
    core = lax.axis_index("core")
    out[0, :, cols_of(core)] = near[:WIDTH]
    out[0, :, cols_of(1 - core)] = far[...]
    weight[0] = jnp.max(f32(near[WIDTH:]))


SMEM = pl.BlockSpec(memory_space=pltpu.SMEM)
HBM = pl.BlockSpec(memory_space=pltpu.HBM)
VMEM = pl.BlockSpec(memory_space=pltpu.VMEM)


def call(body, scalars, fetched, late, near, outs, scratch=(), flops=0):
    copied = [f if isinstance(f, tuple) else (f, None) for f in list(fetched) + list(late)]
    n, m, first = len(copied), len(fetched), len(scalars)
    last = first + n + len(near)
    far = [k for k, (_, _, memory) in enumerate(outs) if memory is pltpu.HBM]

    def view(ref, where):
        return ref if where is None else ref.at[where]

    def held_shape(value, where):
        if where is None:
            return value.shape
        return value.shape[1:] if isinstance(where, int) else (where.size,) + value.shape[1:]

    def kernel(*refs):
        out = list(refs[last : last + len(outs)])
        rest = list(refs[last + len(outs) :])
        buffers, out_buffers, rest = rest[:n], rest[n : n + len(far)], rest[n + len(far) :]
        sems = rest.pop(0) if n else None
        out_sems = rest.pop(0) if far else None
        copies = [
            pltpu.make_async_copy(view(refs[first + i], copied[i][1]), buffers[i], sems.at[i])
            for i in range(n)
        ]
        for copy in copies:
            copy.start()
        for copy in copies[:m]:
            copy.wait()
        written = list(out)
        for k, buffer in zip(far, out_buffers):
            written[k] = buffer
        later = body(*refs[:first], *buffers, *refs[first + n : last], *written, *rest)
        for copy in copies[m:]:
            copy.wait()
        if late:
            later()
        copies = [
            pltpu.make_async_copy(buffer, out[k], out_sems.at[i])
            for i, (k, buffer) in enumerate(zip(far, out_buffers))
        ]
        for copy in copies:
            copy.start()
        for copy in copies:
            copy.wait()

    buffered = [pltpu.VMEM(held_shape(value, where), value.dtype) for value, where in copied]
    buffered += [pltpu.VMEM(*outs[k][:2]) for k in far]
    buffered += [pltpu.SemaphoreType.DMA((n,))] if n else []
    buffered += [pltpu.SemaphoreType.DMA((len(far),))] if far else []
    result, specs = [], []
    for shape, kind, memory in outs:
        result.append((memory or jax.ShapeDtypeStruct)(shape, kind))
        specs.append(HBM if memory is pltpu.HBM else SMEM if shape == (1,) else VMEM)
    arrays = [pltpu.with_memory_space_constraint(value, pltpu.HBM) for value, _ in copied]
    moved = sum(a.size * a.dtype.itemsize for a in arrays + list(near))
    moved += sum(math.prod(shape) * jnp.dtype(kind).itemsize for shape, kind, _ in outs)
    return pl.pallas_call(
        kernel,
        out_shape=result,
        in_specs=[SMEM] * first + [HBM] * n + [VMEM] * len(near),
        out_specs=specs,
        scratch_shapes=buffered + [pltpu.VMEM(size, kind) for size, kind in scratch],
        compiler_params=pltpu.CompilerParams(vmem_limit_bytes=20 * 2**20),
        cost_estimate=pl.CostEstimate(flops=flops, bytes_accessed=moved, transcendentals=0),
        name=body.func.__name__ if isinstance(body, functools.partial) else body.__name__,
    )(*scalars, *arrays, *near)


def held(value):
    return pltpu.with_memory_space_constraint(value, pltpu.VMEM)


def z_pairs(step):
    pairs = []
    for zh in range(N_Z):
        for core in range(2):
            turn = (1, 3)[step ^ core]
            pairs.append((zh * 2 + core, (zh ^ turn) * 2 + core))
    return pairs


def over_z(value, step):
    return lax.ppermute(value, ("z_hi", "core"), z_pairs(step))


def over_y(value):
    return lax.all_to_all(value, "y", 0, 0, tiled=True)


def swap_core(value):
    return lax.ppermute(value, "core", [(0, 1), (1, 0)])


def to_group(value, hop):
    count = SIZES[0] * SIZES[1]
    return lax.ppermute(value, GROUP, [(i, (i + hop) % count) for i in range(count)])


def to_group_other(value, hop):
    count = SIZES[0] * SIZES[1]
    pairs = [(i * 2 + c, (i + hop) % count * 2 + 1 - c) for i in range(count) for c in range(2)]
    return lax.ppermute(value, GROUP + ("core",), pairs)


OWN = ((BLOCK, COLS), F32, pltpu.VMEM)


WHOLE = ((SLAB, COLS), B16, pltpu.VMEM)
SPREAD = ((N_Y, SLAB, COLS), B16, pltpu.HBM)


def add_z(slab, own, step, body, out, before=None):
    got = over_z(slab, step)
    if before is not None:
        got, _ = lax.optimization_barrier((got, before))
    return call(body, [], [], [], [held(own), held(slab), held(got)], [out, OWN])


def local(inputs, targets, numerator, momentum, received, push_weight, received_weight, mix_share):
    push, push_got, mix = push_weight, received_weight, mix_share
    state = [(numerator, 0), (received, 0), (momentum, 0)]

    part_far, part_own = call(
        first_values,
        [push],
        [(inputs, 0), (numerator, 0), targets],
        [],
        [],
        [((TOKENS + 2 * PADDED, COLS), B16, pltpu.VMEM), ((TOKENS, COLS), B16, pltpu.VMEM)],
    )
    later, _ = lax.optimization_barrier((numerator, part_own))
    message, mine = call(
        make_message,
        [],
        [inputs, (later, 0)] + state[1:],
        [],
        [],
        [((MESSAGE, WIDTH), B16, pltpu.VMEM), ((2 * TOKENS, WIDTH), B16, pltpu.HBM)],
    )
    part_got, _ = lax.optimization_barrier((swap_core(part_far), mine))
    near = [held(part_own), held(part_got)]
    (part1,) = call(add_parts, [], [], [], near, [((TOKENS, COLS), B16, pltpu.HBM)])
    taught = [targets, part_got[TOKENS:]]

    message, _ = lax.optimization_barrier((message, part1))
    got = swap_core(message)

    parts1 = over_y(part1.reshape(N_Y, SLAB, COLS))
    slab, own1 = call(
        functools.partial(sum_over_y, 0), [], taught, [], [held(parts1)], [WHOLE, OWN]
    )

    mine, _ = lax.optimization_barrier((mine, slab))
    (part2,) = call(
        second_values,
        [push, push_got, mix],
        state + [mine, got],
        [],
        [],
        [((TOKENS, COLS + HALF), B16, pltpu.HBM)],
    )
    slab, own1 = add_z(slab, own1, 0, add_slab, WHOLE, part2)
    part2, _ = lax.optimization_barrier((part2, slab))
    parts2 = over_y(part2.reshape(N_Y, SLAB, COLS + HALF))
    sent, own1 = add_z(slab, own1, 1, add_and_spread, SPREAD)
    all1 = over_y(sent).reshape(TOKENS, COLS)

    parts2, _ = lax.optimization_barrier((parts2, sent))
    base, own2, gram = call(
        functools.partial(sum_over_y, 1),
        [],
        taught,
        [],
        [held(parts2)],
        [WHOLE, OWN, ((SLAB, HALF), B16, pltpu.VMEM)],
    )
    near = [held(own2), all1, held(gram), held(swap_core(gram)), held(base)]
    slab, own2 = call(
        second_residual, [push, push_got, mix], [], [], near, [WHOLE, OWN], [((SLAB, COLS), F32)]
    )
    near, far, ready = call(
        first_gradient,
        [push, mix],
        state + [(mine, pl.ds(X1_AT, TOKENS)), (got, pl.ds(X1_AT, MESSAGE - X1_AT))],
        [],
        [all1],
        [
            ((WIDTH + EXTRA, COLS), B16, pltpu.VMEM),
            ((WIDTH, COLS), B16, pltpu.VMEM),
            ((2 * WIDTH, COLS), F32, pltpu.HBM),
        ],
    )
    slab, own2 = add_z(slab, own2, 0, add_slab, WHOLE)
    sent, own2 = add_z(slab, own2, 1, add_and_spread, SPREAD, far)
    all2 = over_y(sent).reshape(TOKENS, COLS)
    near, _ = lax.optimization_barrier((near, sent))
    arrived, arrived_far = to_group(near, 1), to_group_other(far, 1)
    all2, arrived = lax.optimization_barrier((all2, arrived))

    far, near, half, message, message_low = call(
        second_gradient,
        [push, push_got, mix],
        [ready, (mine, pl.ds(0, TOKENS)), (got, pl.ds(0, TOKENS))],
        [],
        [held(own1), held(own2), all2],
        [
            ((WIDTH, COLS), B16, None),
            ((WIDTH + EXTRA, COLS), B16, None),
            ((WIDTH, COLS), F32, None),
            ((WIDTH // 2 + 2 * PADDED, COLS), B16, None),
            ((WIDTH // 2, COLS), B16, None),
        ],
    )

    sent_far, sent_own = to_group_other(far, 2), to_group(near, 2)
    whole = ((1, WIDTH, VALUES), B16, None)
    number = ((1,), F32, None)
    final_numerator, value_rows, final_weight = call(
        join_numerator,
        [push, push_got, mix],
        [],
        [],
        [
            held(arrived),
            held(arrived_far),
            held(own1),
            held(own2),
            half,
            swap_core(message),
            swap_core(message_low),
        ],
        [whole, ((2, ROWS, VALUES), B16, None), number],
    )
    sent_far, final_numerator = lax.optimization_barrier((sent_far, final_numerator))
    final_received, got_weight = call(
        join_received, [], [], [], [sent_own, sent_far], [whole, number]
    )
    return final_numerator, final_weight, final_received, got_weight, value_rows


def solution(mesh):
    fine = Mesh(mesh.devices.reshape(SIZES), GROUP + MP)
    placed = (
        P(None, GROUP, MP),
        P(None, GROUP + MP, None),
        P(GROUP, MP, None),
        P(GROUP, MP, None),
        P(GROUP, MP, None),
        P(GROUP),
        P(GROUP),
        P(GROUP, None),
    )
    return jax.shard_map(
        local,
        mesh=fine,
        in_specs=placed,
        out_specs=(
            P(GROUP, MP, None),
            P(GROUP),
            P(GROUP, MP, None),
            P(GROUP),
            P(None, GROUP + MP, None),
        ),
        check_vma=False,
    )
```

```python
import functools
import math

import jax
import jax.numpy as jnp
from jax import lax
from jax.experimental import pallas as pl
from jax.experimental.pallas import tpu as pltpu
from jax.sharding import Mesh
from jax.sharding import PartitionSpec as P

GROUP = ("x", "z_lo")
MP = ("z_hi", "y", "core")
SIZES = (4, 4, 4, 4, 2)
N_Z, N_Y = SIZES[2], SIZES[3]

momentum_decay = 0.9
step_size = 0.5

ROWS = 24
BLOCK = 2 * ROWS
SLAB = N_Z * BLOCK
TOKENS = N_Y * SLAB
WIDTH = 256
VALUES = 1024
COLS = VALUES // 2
HALF = TOKENS // 2
PADDED = 32
EXTRA = 16
ROW_SCALE = 1.0 / math.sqrt(WIDTH * N_Z * N_Y * 2)
GRAD_SCALE = 1.0 / math.sqrt(TOKENS)

X1_AT = TOKENS

B16, F32 = jnp.bfloat16, jnp.float32


def f32(value):
    return value.astype(jnp.float32)


def bf16(value):
    return value.astype(jnp.bfloat16)


def dot(a, b, dims=((1,), (0,))):
    return lax.dot_general(a, b, (dims, ((), ())), preferred_element_type=jnp.float32)


def cols_of(core):
    return pl.ds(pl.multiple_of(core * COLS, COLS), COLS)


def half_of(core):
    return pl.ds(pl.multiple_of(core * HALF, 16), HALF)


def own_block():
    return pl.ds(pl.multiple_of(lax.axis_index("z_hi") * BLOCK, 16), BLOCK)


def kept(mix, step):
    return mix[0, step].astype(jnp.float32) * 0.125


def by_y():
    return [((zh * N_Y + y) * BLOCK, (y * N_Z + zh) * BLOCK) for zh in range(N_Z) for y in range(N_Y)]


def first_values(push, x, w, targets, far, own):
    core = lax.axis_index("core")
    for out, side in ((far, 1 - core), (own, core)):
        scaled = bf16(f32(w[:, cols_of(side)]) / push[0])
        part = bf16(dot(x[...], scaled) * ROW_SCALE)
        for at, to in by_y():
            out[to : to + BLOCK] = part[at : at + BLOCK]
    spare = jnp.zeros((PADDED - ROWS, COLS), jnp.float32)
    for step in range(2):
        row = TOKENS + step * PADDED
        half = jnp.concatenate([f32(targets[step, :, cols_of(1 - core)]), spare], axis=0)
        far[row : row + PADDED] = bf16(half)


def make_message(x, w, rec, velocity, second, first, state, moving, tokens):
    side = cols_of(1 - lax.axis_index("core"))
    for step, out in ((0, first), (1, second)):
        for at, to in by_y():
            row = (1 - step) * TOKENS + to
            out[to : to + BLOCK] = x[step, at : at + BLOCK]
            tokens[row : row + BLOCK] = x[step, at : at + BLOCK]
    old = velocity[:, side]
    high = bf16(old)
    halves = [(state, 0, w[:, side]), (state, 2 * WIDTH, rec[:, side])]
    halves += [(moving, 0, high), (moving, 2 * WIDTH, bf16(old - f32(high)))]
    for out, row, half in halves:
        out[row : row + WIDTH] = half[:, :WIDTH]
        out[row + WIDTH : row + 2 * WIDTH] = half[:, WIDTH:]


def add_parts(own, got, out):
    out[...] = bf16(f32(own[...]) + f32(got[:TOKENS]))


def tile(mix, w, rec, velocity, state, moving, k):
    keep = kept(mix, 0)
    if k == 0:
        side = cols_of(lax.axis_index("core"))
        start, arrived, old = w[:, side], rec[:, side], velocity[:, side]
    else:
        start, arrived, high, low = (
            jnp.concatenate([got[at : at + WIDTH], got[at + WIDTH : at + 2 * WIDTH]], axis=1)
            for got in (state, moving)
            for at in (0, 2 * WIDTH)
        )
        old = f32(high) + f32(low)
    ahead = f32(start) - (step_size * momentum_decay) * old
    return ahead, keep * ahead + f32(arrived), old


def second_values(push, push_got, mix, w, rec, velocity, mine, got2, got1, state, moving, out):
    core = lax.axis_index("core")
    weight = kept(mix, 0) * push[0] + push_got[0]
    near, far = mine[:TOKENS], got2[...]
    scaled = [bf16(tile(mix, w, rec, velocity, state, moving, k)[1] / weight) for k in range(2)]
    out[:, :COLS] = bf16((dot(near, scaled[0]) + dot(far, scaled[1])) * ROW_SCALE)
    rows = pl.ds(pl.multiple_of(X1_AT + core * HALF, 16), HALF)
    rows_got = half_of(core)
    across = ((1,), (1,))
    out[:, COLS:] = bf16(dot(near, mine[rows], across) + dot(far, got1[rows_got], across))


def sum_over_y(step, targets, targets_got, parts, slab, own, *gram):
    core = lax.axis_index("core")
    total = f32(parts[0])
    for y in range(1, N_Y):
        total = total + f32(parts[y])
    slab[...] = bf16(total[:, :COLS])
    if gram:
        gram[0][...] = bf16(total[:, COLS:])
    rows = own_block()
    total = f32(parts[0, rows, :COLS])
    for y in range(1, N_Y):
        total = total + f32(parts[y, rows, :COLS])
    own[...] = total
    near = f32(targets[step, :, cols_of(core)])
    far = f32(targets_got[step * PADDED : (step + 1) * PADDED])[:ROWS]
    low, high = jnp.where(core == 0, near, far), jnp.where(core == 0, far, near)
    slab[rows] = bf16(total - jnp.concatenate([low, high], axis=0))


def add_slab(own, mine, got, out, own_out):
    out[...] = bf16(f32(mine[...]) + f32(got[...]))
    own_out[...] = own[...] + f32(got[own_block()])


def add_and_spread(own, mine, got, out, own_out):
    total = bf16(f32(mine[...]) + f32(got[...]))
    for y in range(N_Y):
        out[y] = total
    own_out[...] = own[...] + f32(got[own_block()])


def second_residual(push, push_got, mix, own, all1, gram, gram_got, base, out, own_out, turned):
    core = lax.axis_index("core")
    keep = kept(mix, 0)
    back = step_size * GRAD_SCALE * ROW_SCALE * keep / (keep * push[0] + push_got[0])
    near, far = all1[half_of(core)], all1[half_of(1 - core)]
    turned[...] = (dot(gram[...], near) + dot(gram_got[...], far)) * back
    out[...] = bf16(f32(base[...]) - turned[...])
    own_out[...] = own[...] - turned[own_block()]


def first_gradient(push, mix, w, rec, velocity, mine, got, state, moving, all1, near, far, ready):
    keep = kept(mix, 0)
    down = ((0,), (0,))
    for k, x, out in ((0, mine, near), (1, got, far)):
        ahead, base, old = tile(mix, w, rec, velocity, state, moving, k)
        gradient = dot(x[:TOKENS], all1[...], down) * GRAD_SCALE
        out[:WIDTH] = bf16((1.0 - keep) * (ahead - step_size * gradient))
        current = bf16(base - (step_size * keep) * gradient)
        moved = momentum_decay * old + gradient
        ready[k * WIDTH : (k + 1) * WIDTH] = f32(current) - (step_size * momentum_decay) * moved
    near[WIDTH:] = bf16(jnp.full((EXTRA, COLS), (1.0 - keep) * push[0], jnp.float32))


def second_gradient(
    push, push_got, mix, ready, mine, got, own1, own2, all2, far, near, half, message, message_low
):
    core = lax.axis_index("core")
    keep = kept(mix, 1)
    down = ((0,), (0,))
    gradient = dot(got[...], all2[...], down) * GRAD_SCALE
    moved = ready[WIDTH:] - step_size * gradient
    far[...] = bf16((1.0 - keep) * moved)
    message[: WIDTH // 2] = bf16(keep * moved[: WIDTH // 2])
    message_low[...] = bf16(keep * moved[WIDTH // 2 :])
    gradient = dot(mine[...], all2[...], down) * GRAD_SCALE
    moved = ready[:WIDTH] - step_size * gradient
    near[:WIDTH] = bf16((1.0 - keep) * moved)
    half[...] = keep * moved
    weight = kept(mix, 0) * push[0] + push_got[0]
    near[WIDTH:] = bf16(jnp.full((EXTRA, COLS), (1.0 - keep) * weight, jnp.float32))
    spare = jnp.zeros((PADDED - ROWS, COLS), jnp.float32)
    for step, own in ((0, own1), (1, own2)):
        row = WIDTH // 2 + step * PADDED
        block = jnp.where(core == 0, own[ROWS:], own[:ROWS])
        message[row : row + PADDED] = bf16(jnp.concatenate([block, spare], axis=0))


def join_numerator(
    push, push_got, mix, arrived, arrived_far, own1, own2, half, message, message_low, out, rows_out, weight
):
    core = lax.axis_index("core")
    cut = WIDTH // 2
    out[0, :, cols_of(core)] = bf16(half[...] + f32(arrived[:WIDTH]))
    out[0, :cut, cols_of(1 - core)] = bf16(f32(message[:cut]) + f32(arrived_far[:cut]))
    out[0, cut:, cols_of(1 - core)] = bf16(f32(message_low[...]) + f32(arrived_far[cut:]))
    for step, own in ((0, own1), (1, own2)):
        row = cut + step * PADDED
        rows_out[step, :, cols_of(core)] = bf16(jnp.where(core == 0, own[:ROWS], own[ROWS:]))
        rows_out[step, :, cols_of(1 - core)] = bf16(f32(message[row : row + PADDED])[:ROWS])
    last = kept(mix, 0) * push[0] + push_got[0]
    weight[0] = kept(mix, 1) * last + jnp.max(f32(arrived[WIDTH:]))


def join_received(near, far, out, weight):
    core = lax.axis_index("core")
    out[0, :, cols_of(core)] = near[:WIDTH]
    out[0, :, cols_of(1 - core)] = far[...]
    weight[0] = jnp.max(f32(near[WIDTH:]))


SMEM = pl.BlockSpec(memory_space=pltpu.SMEM)
HBM = pl.BlockSpec(memory_space=pltpu.HBM)
VMEM = pl.BlockSpec(memory_space=pltpu.VMEM)


def call(body, scalars, fetched, late, near, outs, scratch=(), flops=0):
    copied = [f if isinstance(f, tuple) else (f, None) for f in list(fetched) + list(late)]
    n, m, first = len(copied), len(fetched), len(scalars)
    last = first + n + len(near)
    far = [k for k, (_, _, memory) in enumerate(outs) if memory is pltpu.HBM]

    def view(ref, where):
        return ref if where is None else ref.at[where]

    def held_shape(value, where):
        if where is None:
            return value.shape
        return value.shape[1:] if isinstance(where, int) else (where.size,) + value.shape[1:]

    def kernel(*refs):
        out = list(refs[last : last + len(outs)])
        rest = list(refs[last + len(outs) :])
        buffers, out_buffers, rest = rest[:n], rest[n : n + len(far)], rest[n + len(far) :]
        sems = rest.pop(0) if n else None
        out_sems = rest.pop(0) if far else None
        copies = [
            pltpu.make_async_copy(view(refs[first + i], copied[i][1]), buffers[i], sems.at[i])
            for i in range(n)
        ]
        for copy in copies:
            copy.start()
        for copy in copies[:m]:
            copy.wait()
        written = list(out)
        for k, buffer in zip(far, out_buffers):
            written[k] = buffer
        later = body(*refs[:first], *buffers, *refs[first + n : last], *written, *rest)
        for copy in copies[m:]:
            copy.wait()
        if late:
            later()
        copies = [
            pltpu.make_async_copy(buffer, out[k], out_sems.at[i])
            for i, (k, buffer) in enumerate(zip(far, out_buffers))
        ]
        for copy in copies:
            copy.start()
        for copy in copies:
            copy.wait()

    buffered = [pltpu.VMEM(held_shape(value, where), value.dtype) for value, where in copied]
    buffered += [pltpu.VMEM(*outs[k][:2]) for k in far]
    buffered += [pltpu.SemaphoreType.DMA((n,))] if n else []
    buffered += [pltpu.SemaphoreType.DMA((len(far),))] if far else []
    result, specs = [], []
    for shape, kind, memory in outs:
        result.append((memory or jax.ShapeDtypeStruct)(shape, kind))
        specs.append(HBM if memory is pltpu.HBM else SMEM if shape == (1,) else VMEM)
    arrays = [pltpu.with_memory_space_constraint(value, pltpu.HBM) for value, _ in copied]
    moved = sum(a.size * a.dtype.itemsize for a in arrays + list(near))
    moved += sum(math.prod(shape) * jnp.dtype(kind).itemsize for shape, kind, _ in outs)
    return pl.pallas_call(
        kernel,
        out_shape=result,
        in_specs=[SMEM] * first + [HBM] * n + [VMEM] * len(near),
        out_specs=specs,
        scratch_shapes=buffered + [pltpu.VMEM(size, kind) for size, kind in scratch],
        compiler_params=pltpu.CompilerParams(vmem_limit_bytes=20 * 2**20),
        cost_estimate=pl.CostEstimate(flops=flops, bytes_accessed=moved, transcendentals=0),
        name=body.func.__name__ if isinstance(body, functools.partial) else body.__name__,
    )(*scalars, *arrays, *near)


def held(value):
    return pltpu.with_memory_space_constraint(value, pltpu.VMEM)


def z_pairs(step):
    pairs = []
    for zh in range(N_Z):
        for core in range(2):
            turn = (1, 3)[step ^ core]
            pairs.append((zh * 2 + core, (zh ^ turn) * 2 + core))
    return pairs


def over_z(value, step):
    return lax.ppermute(value, ("z_hi", "core"), z_pairs(step))


def over_y(value):
    return lax.all_to_all(value, "y", 0, 0, tiled=True)


def swap_core(value):
    return lax.ppermute(value, "core", [(0, 1), (1, 0)])


def to_group(value, hop):
    count = SIZES[0] * SIZES[1]
    return lax.ppermute(value, GROUP, [(i, (i + hop) % count) for i in range(count)])


def to_group_other(value, hop):
    count = SIZES[0] * SIZES[1]
    pairs = [(i * 2 + c, (i + hop) % count * 2 + 1 - c) for i in range(count) for c in range(2)]
    return lax.ppermute(value, GROUP + ("core",), pairs)


OWN = ((BLOCK, COLS), F32, pltpu.VMEM)


WHOLE = ((SLAB, COLS), B16, pltpu.VMEM)
SPREAD = ((N_Y, SLAB, COLS), B16, pltpu.HBM)


def add_z(slab, own, step, body, out, before=None):
    got = over_z(slab, step)
    if before is not None:
        got, _ = lax.optimization_barrier((got, before))
    return call(body, [], [], [], [held(own), held(slab), held(got)], [out, OWN])


def local(inputs, targets, numerator, momentum, received, push_weight, received_weight, mix_share):
    push, push_got, mix = push_weight, received_weight, mix_share
    state = [(numerator, 0), (received, 0), (momentum, 0)]

    part_far, part_own = call(
        first_values,
        [push],
        [(inputs, 0), (numerator, 0), targets],
        [],
        [],
        [((TOKENS + 2 * PADDED, COLS), B16, pltpu.VMEM), ((TOKENS, COLS), B16, pltpu.VMEM)],
    )
    later, _ = lax.optimization_barrier((numerator, part_own))
    *message, mine = call(
        make_message,
        [],
        [inputs, (later, 0)] + state[1:],
        [],
        [],
        [((TOKENS, WIDTH), B16, pltpu.VMEM)] * 2
        + [((4 * WIDTH, WIDTH), B16, pltpu.VMEM)] * 2
        + [((2 * TOKENS, WIDTH), B16, pltpu.HBM)],
    )
    part_got, _ = lax.optimization_barrier((swap_core(part_far), mine))
    near = [held(part_own), held(part_got)]
    (part1,) = call(add_parts, [], [], [], near, [((TOKENS, COLS), B16, pltpu.HBM)])
    taught = [targets, part_got[TOKENS:]]

    message, _ = lax.optimization_barrier((message, part1))
    got2, got1, state_got, moving_got = [swap_core(value) for value in message]

    parts1 = over_y(part1.reshape(N_Y, SLAB, COLS))
    slab, own1 = call(
        functools.partial(sum_over_y, 0), [], taught, [], [held(parts1)], [WHOLE, OWN]
    )

    mine, _ = lax.optimization_barrier((mine, slab))
    (part2,) = call(
        second_values,
        [push, push_got, mix],
        state + [mine, got2, got1, state_got, moving_got],
        [],
        [],
        [((TOKENS, COLS + HALF), B16, pltpu.HBM)],
    )
    slab, own1 = add_z(slab, own1, 0, add_slab, WHOLE, part2)
    part2, _ = lax.optimization_barrier((part2, slab))
    parts2 = over_y(part2.reshape(N_Y, SLAB, COLS + HALF))
    sent, own1 = add_z(slab, own1, 1, add_and_spread, SPREAD)
    all1 = over_y(sent).reshape(TOKENS, COLS)

    parts2, _ = lax.optimization_barrier((parts2, sent))
    base, own2, gram = call(
        functools.partial(sum_over_y, 1),
        [],
        taught,
        [],
        [held(parts2)],
        [WHOLE, OWN, ((SLAB, HALF), B16, pltpu.VMEM)],
    )
    near = [held(own2), all1, held(gram), held(swap_core(gram)), held(base)]
    slab, own2 = call(
        second_residual, [push, push_got, mix], [], [], near, [WHOLE, OWN], [((SLAB, COLS), F32)]
    )
    near, far, ready = call(
        first_gradient,
        [push, mix],
        state + [(mine, pl.ds(X1_AT, TOKENS)), got1, state_got, moving_got],
        [],
        [all1],
        [
            ((WIDTH + EXTRA, COLS), B16, pltpu.VMEM),
            ((WIDTH, COLS), B16, pltpu.VMEM),
            ((2 * WIDTH, COLS), F32, pltpu.HBM),
        ],
    )
    slab, own2 = add_z(slab, own2, 0, add_slab, WHOLE)
    sent, own2 = add_z(slab, own2, 1, add_and_spread, SPREAD, far)
    all2 = over_y(sent).reshape(TOKENS, COLS)
    near, _ = lax.optimization_barrier((near, sent))
    arrived, arrived_far = to_group(near, 1), to_group_other(far, 1)
    all2, arrived = lax.optimization_barrier((all2, arrived))

    far, near, half, message, message_low = call(
        second_gradient,
        [push, push_got, mix],
        [ready, (mine, pl.ds(0, TOKENS)), got2],
        [],
        [held(own1), held(own2), all2],
        [
            ((WIDTH, COLS), B16, None),
            ((WIDTH + EXTRA, COLS), B16, None),
            ((WIDTH, COLS), F32, None),
            ((WIDTH // 2 + 2 * PADDED, COLS), B16, None),
            ((WIDTH // 2, COLS), B16, None),
        ],
    )

    sent_far, sent_own = to_group_other(far, 2), to_group(near, 2)
    whole = ((1, WIDTH, VALUES), B16, None)
    number = ((1,), F32, None)
    final_numerator, value_rows, final_weight = call(
        join_numerator,
        [push, push_got, mix],
        [],
        [],
        [
            held(arrived),
            held(arrived_far),
            held(own1),
            held(own2),
            half,
            swap_core(message),
            swap_core(message_low),
        ],
        [whole, ((2, ROWS, VALUES), B16, None), number],
    )
    sent_far, final_numerator = lax.optimization_barrier((sent_far, final_numerator))
    final_received, got_weight = call(
        join_received, [], [], [], [sent_own, sent_far], [whole, number]
    )
    return final_numerator, final_weight, final_received, got_weight, value_rows


def solution(mesh):
    fine = Mesh(mesh.devices.reshape(SIZES), GROUP + MP)
    placed = (
        P(None, GROUP, MP),
        P(None, GROUP + MP, None),
        P(GROUP, MP, None),
        P(GROUP, MP, None),
        P(GROUP, MP, None),
        P(GROUP),
        P(GROUP),
        P(GROUP, None),
    )
    return jax.shard_map(
        local,
        mesh=fine,
        in_specs=placed,
        out_specs=(
            P(GROUP, MP, None),
            P(GROUP),
            P(GROUP, MP, None),
            P(GROUP),
            P(None, GROUP + MP, None),
        ),
        check_vma=False,
    )
```
